32 devices in a mesh: dp: 8 (over z, x), tensor: 4 (over y, core).
Axes of the slice: x: 2, y: 2, z: 4, core: 2. Of those that a mesh axis runs over, the one named last changes fastest.
Arguments:
- tokens: bfloat16 [16384, 2048], P(('dp', 'tensor')), may hold values from -8 to 8
- attention_norm_gain: float32 [2048], replicated, may hold values from 0.5 to 1.5
- w_query: bfloat16 [2048, 2048], P(None, 'tensor'), may hold values from -0.125 to 0.125
- w_key: bfloat16 [2048, 2048], P(None, 'tensor'), may hold values from -0.125 to 0.125
- w_value: bfloat16 [2048, 2048], P(None, 'tensor'), may hold values from -0.125 to 0.125
- w_out: bfloat16 [2048, 2048], P('tensor'), may hold values from -0.125 to 0.125
- gate_bias: float32 [16], P('tensor'), may hold values from -2 to 2
- feedforward_norm_gain: float32 [2048], replicated, may hold values from 0.5 to 1.5
- w_gate: bfloat16 [2048, 8192], P(None, 'tensor'), may hold values from -0.125 to 0.125
- w_up: bfloat16 [2048, 8192], P(None, 'tensor'), may hold values from -0.125 to 0.125
- w_down: bfloat16 [8192, 2048], P('tensor'), may hold values from -0.0625 to 0.0625
- seg_starts: int32 [8], P('dp'), may hold values from 0 to 1, as said below
- seg_valid: int32 [8], P('dp'), may hold values from 1024 to 2048, as said below
- cotangent: bfloat16 [16384, 2048], P(('dp', 'tensor')), may hold values from -6 to 6
Outputs:
- out: bfloat16 [16384, 2048], P(('dp', 'tensor'))
- grad_tokens: float32 [16384, 2048], P(('dp', 'tensor'))
- grad_gain1: float32 [2048], replicated
- grad_w_query: float32 [2048, 2048], P('dp', 'tensor')
- grad_w_key: float32 [2048, 2048], P('dp', 'tensor')
- grad_w_value: float32 [2048, 2048], P('dp', 'tensor')
- grad_w_out: float32 [2048, 2048], P('tensor', 'dp')
- grad_gate_bias: float32 [16], replicated
- grad_gain2: float32 [2048], replicated
- grad_w_gate: float32 [2048, 8192], P('dp', 'tensor')
- grad_w_up: float32 [2048, 8192], P('dp', 'tensor')
- grad_w_down: float32 [8192, 2048], P('tensor', 'dp')
The draws below stay inside these ranges and needn't reach their ends.
Inputs may be any that keep to these rules, and one draw needn't show every extreme that they name: `seg_starts`: 1 where the segment begins a sequence and 0 where it continues the sequence of the segment before it; the first segment begins one; segments 1, 4 and 7 continue the segment before them. `seg_valid`: the number of leading live rows of a segment; it is 2048 in every segment but the last one of a sequence.
All inputs are finite; a program needn't handle non-finite values.
Results may differ from the reference program's by a relative error of at most 0.015.
Values may be sent and summed in bfloat16 or wider, within the bound.
No kernel may reach another device: no remote copies, remote signals or barrier semaphores. Data moves between devices by JAX's collectives and lax.ppermute only.
A program may use at most 320 MiB of HBM per device.

```python
import jax
import jax.numpy as jnp
from jax import lax

D = 2048
HEADS = 16
HEAD = 128
FF = 8192
SEG = 2048
SEGS = 8
TOKENS = 16384


def segment_plan(key):
    key_base, key_tail = jax.random.split(key, 2)
    index_row = jnp.arange(SEGS)
    base_flags = (jax.random.randint(key_base, (SEGS,), 0, 5) < 2).astype(jnp.int32)
    continuing = (index_row == 1) | (index_row == SEGS // 2) | (index_row == SEGS - 1)
    begin_flags = jnp.where(continuing, 0, base_flags)
    begin_flags = jnp.where(index_row == 0, 1, begin_flags).astype(jnp.int32)
    following = jnp.concatenate([begin_flags[1:], jnp.ones((1,), jnp.int32)])
    tail_rows = jax.random.randint(key_tail, (SEGS,), SEG // 2, SEG + 1)
    valid_rows = jnp.where(following == 1, tail_rows, SEG).astype(jnp.int32)
    return (begin_flags, valid_rows)


def draw_seg_starts(key, part):
    begin_flags, valid_rows = segment_plan(key)
    return begin_flags


def draw_seg_valid(key, part):
    begin_flags, valid_rows = segment_plan(key)
    return valid_rows


def draw_tokens(key, part):
    key = jax.random.fold_in(key, 3)
    key_common, key_noise = jax.random.split(key)
    common = jax.random.normal(key_common, (D,), jnp.float32)
    noise = jax.random.normal(key_noise, (TOKENS, D), jnp.float32)
    mixed_rows = noise + 0.8 * common[None, :]
    return jnp.clip(mixed_rows, -8.0, 8.0).astype(jnp.bfloat16)


def shard_levels(own_key, extent, cuts, least, largest):
    level, own = 1.0, jax.random.fold_in(own_key, 6)
    for dim, shards_of in cuts:
        draws = jnp.exp(jax.random.uniform(jax.random.fold_in(own, dim), (shards_of,), jnp.float32, least / len(cuts), largest / len(cuts)))
        level = level * jnp.repeat(draws, extent[dim] // shards_of).reshape([-1 if axis == dim else 1 for axis in range(len(extent))])
    return level


def gaussian(rng, shape, spread, bound, cuts=(), held_as=jnp.bfloat16):
    array = spread * jax.random.normal(rng, shape, jnp.float32)
    if cuts:
        array = array * shard_levels(rng, shape, cuts, -0.22, 0.18)
    return jnp.clip(array, -bound, bound).astype(held_as)


def setup_inputs(seed: int = 0) -> dict:
    splits = jax.random.split(jax.random.key(seed), 15)
    return {
        "tokens": draw_tokens(jax.random.fold_in(splits[14], 71), 0),
        "attention_norm_gain": jnp.clip(1.0 + 0.1 * jax.random.normal(splits[1], (D,), jnp.float32), 0.5, 1.5),
        "w_query": gaussian(splits[2], (D, HEADS * HEAD), D ** -0.5, 0.125, ((1, 4),)),
        "w_key": gaussian(splits[3], (D, HEADS * HEAD), D ** -0.5, 0.125, ((1, 4),)),
        "w_value": gaussian(splits[4], (D, HEADS * HEAD), D ** -0.5, 0.125, ((1, 4),)),
        "w_out": gaussian(splits[5], (HEADS * HEAD, D), (HEADS * HEAD) ** -0.5, 0.125, ((0, 4),)),
        "gate_bias": jnp.clip(jax.random.uniform(splits[6], (HEADS,), jnp.float32, -2.0, 2.0) * shard_levels(splits[6], (HEADS,), ((0, 4),), -0.4, 0.0), -2.0, 2.0),
        "feedforward_norm_gain": jnp.clip(1.0 + 0.1 * jax.random.normal(splits[7], (D,), jnp.float32), 0.5, 1.5),
        "w_gate": gaussian(splits[8], (D, FF), D ** -0.5, 0.125, ((1, 4),)),
        "w_up": gaussian(splits[9], (D, FF), D ** -0.5, 0.125, ((1, 4),)),
        "w_down": gaussian(splits[10], (FF, D), FF ** -0.5, 0.0625, ((0, 4),)),
        "seg_starts": draw_seg_starts(jax.random.fold_in(splits[14], 71), 0),
        "seg_valid": draw_seg_valid(jax.random.fold_in(splits[14], 71), 0),
        "cotangent": gaussian(splits[13], (TOKENS, D), 1.0, 6.0, ((0, 32),)),
    }


EPSILON = 1e-06

@jax.custom_vjp
def low(v):
    return lax.optimization_barrier(v.astype(jnp.bfloat16)).astype(jnp.float32)

@jax.custom_vjp
def low_back(v):
    return v

def low_keep(v):
    return (low(v), None)

def low_pass(kept, grad):
    return (grad,)

def back_keep(v):
    return (v, None)

def back_low(kept, grad):
    return (low(grad),)
low.defvjp(low_keep, low_pass)
low_back.defvjp(back_keep, back_low)

def elu_plus(values):
    return jnp.where(values > 0, values + 1.0, jnp.exp(jnp.minimum(values, 0.0)))

def normalize(values, gain):
    return values * lax.rsqrt(lax.optimization_barrier(jnp.mean(values * values, axis=-1, keepdims=True)) + EPSILON) * gain

def memory_terms(memory_in, norm_in, phi_q, phi_k, values):
    den_q = jnp.maximum(jnp.einsum('thd,hd->th', phi_q, norm_in, precision=lax.Precision.HIGHEST), 1.0)
    memory_read = jnp.einsum('thd,hde->the', phi_q, memory_in, precision=lax.Precision.HIGHEST) / den_q[..., None]
    den_k = jnp.maximum(jnp.einsum('thd,hd->th', phi_k, norm_in, precision=lax.Precision.HIGHEST), 1.0)
    recalled = jnp.einsum('thd,hde->the', phi_k, memory_in, precision=lax.Precision.HIGHEST) / den_k[..., None]
    memory_out = memory_in + jnp.einsum('thd,the->hde', phi_k, values - recalled, precision=lax.Precision.HIGHEST)
    norm_out = norm_in + lax.optimization_barrier(jnp.sum(phi_k, axis=0))
    return (memory_read, memory_out, norm_out)

def segment_step(params, state_in, inputs):
    attention_norm_gain, w_query, w_key, w_value, w_out, gate_bias, feedforward_norm_gain, w_gate, w_up, w_down = params
    memory_prev, norm_prev = state_in
    seg_rows, begins, valid_rows = inputs
    keep_flag = (1 - begins).astype(jnp.float32)
    position = jnp.arange(SEG)
    live_rows = (position < valid_rows).astype(jnp.float32)
    attention_normed_rows = low(normalize(seg_rows, attention_norm_gain))
    queries = low(low_back(jnp.dot(attention_normed_rows, w_query, precision=lax.Precision.HIGHEST))).reshape(SEG, HEADS, HEAD)
    key_rows = low(low_back(jnp.dot(attention_normed_rows, w_key, precision=lax.Precision.HIGHEST))).reshape(SEG, HEADS, HEAD)
    values = low(low_back(jnp.dot(attention_normed_rows, w_value, precision=lax.Precision.HIGHEST))).reshape(SEG, HEADS, HEAD)
    raw_scores = jnp.einsum('thd,shd->hts', queries, key_rows, precision=lax.Precision.HIGHEST)
    scores = low_back(raw_scores) * HEAD ** (-0.5)
    allowed = (position[None, :] <= position[:, None]) & (position[None, :] < valid_rows)
    scores = jnp.where(allowed[None], scores, -1e+30)
    softmax_w = jax.nn.softmax(scores, axis=-1)
    local_read = low_back(jnp.einsum('hts,shd->thd', low(softmax_w), values, precision=lax.Precision.HIGHEST))
    phi_q = elu_plus(queries)
    phi_k = elu_plus(key_rows) * live_rows[:, None, None]
    memory_read, memory_out, norm_out = memory_terms(keep_flag * memory_prev, keep_flag * norm_prev, phi_q, phi_k, values)
    mix_w = jax.nn.sigmoid(gate_bias)[None, :, None]
    mixed_out = low((mix_w * memory_read + (1.0 - mix_w) * local_read).reshape(SEG, HEADS * HEAD))
    hidden_rows_state = seg_rows + low_back(jnp.dot(mixed_out, w_out, precision=lax.Precision.HIGHEST))
    feedforward_normed_rows = low(normalize(hidden_rows_state, feedforward_norm_gain))
    gate_pre = low_back(jnp.dot(feedforward_normed_rows, w_gate, precision=lax.Precision.HIGHEST))
    up_proj = low_back(jnp.dot(feedforward_normed_rows, w_up, precision=lax.Precision.HIGHEST))
    inner_act = low(jax.nn.silu(gate_pre) * up_proj)
    seg_out = hidden_rows_state + low_back(jnp.dot(inner_act, w_down, precision=lax.Precision.HIGHEST))
    return ((memory_out, norm_out), seg_out)

def forward(tokens_as_float, attention_norm_gain, w_query, w_key, w_value, w_out, gate_bias, feedforward_norm_gain, w_gate, w_up, w_down, seg_starts, seg_valid):
    params = (attention_norm_gain, w_query, w_key, w_value, w_out, gate_bias, feedforward_norm_gain, w_gate, w_up, w_down)
    checked = jax.checkpoint(segment_step)
    initial = (jnp.zeros((HEADS, HEAD, HEAD), jnp.float32), jnp.zeros((HEADS, HEAD), jnp.float32))
    _, results = lax.scan(lambda state_in, inputs: checked(params, state_in, inputs), initial, (tokens_as_float.reshape(SEGS, SEG, D), seg_starts, seg_valid))
    return results.reshape(TOKENS, D)

def reference(tokens, attention_norm_gain, w_query, w_key, w_value, w_out, gate_bias, feedforward_norm_gain, w_gate, w_up, w_down, seg_starts, seg_valid, cotangent):
    floats = (tokens.astype(jnp.float32), attention_norm_gain.astype(jnp.float32), w_query.astype(jnp.float32), w_key.astype(jnp.float32), w_value.astype(jnp.float32), w_out.astype(jnp.float32), gate_bias.astype(jnp.float32), feedforward_norm_gain.astype(jnp.float32), w_gate.astype(jnp.float32), w_up.astype(jnp.float32), w_down.astype(jnp.float32))
    result, pullback = jax.vjp(lambda *weights: forward(*weights, seg_starts, seg_valid), *floats)
    gradients = pullback(cotangent.astype(jnp.float32))
    return (result.astype(jnp.bfloat16), gradients[0], gradients[1], gradients[2], gradients[3], gradients[4], gradients[5], gradients[6], gradients[7], gradients[8], gradients[9], gradients[10])
```

```python
import jax
import jax.numpy as jnp
from jax import lax
from jax.experimental import pallas as pl
from jax.experimental.pallas import tpu as pltpu
from jax.sharding import PartitionSpec as P

HEADS = 16
HEAD = 128
EPSILON = 1e-06
BF = jnp.bfloat16
F32 = jnp.float32
LOG2E = 1.4426950408889634
NEG = -1e30
VMEM_BYTES = 56 << 20


def dot(a, b):
    return jnp.dot(a, b, preferred_element_type=F32)


def dot_nt(a, b):
    return lax.dot_general(a, b, (((1,), (1,)), ((), ())), preferred_element_type=F32)


def dot_tn(a, b):
    return lax.dot_general(a, b, (((0,), (0,)), ((), ())), preferred_element_type=F32)


def shape(dims, dtype):
    return jax.ShapeDtypeStruct(dims, dtype)


def call(kernel, out_shape, grid, in_specs, out_specs, cost, scratch=(), alias=None):
    return pl.pallas_call(
        kernel,
        out_shape=out_shape,
        grid_spec=pltpu.PrefetchScalarGridSpec(
            num_scalar_prefetch=1,
            grid=grid,
            in_specs=in_specs,
            out_specs=out_specs,
            scratch_shapes=list(scratch),
        ),
        input_output_aliases=alias or {},
        compiler_params=pltpu.CompilerParams(
            dimension_semantics=("arbitrary",) * len(grid), vmem_limit_bytes=VMEM_BYTES
        ),
        cost_estimate=pl.CostEstimate(
            flops=int(cost[0]), bytes_accessed=int(cost[1]), transcendentals=0
        ),
    )


def whole(dims):
    return pl.BlockSpec(dims, lambda *_: (0,) * len(dims), pipeline_mode=pl.Buffered(1))


def exp_low(values):
    return jnp.exp(jnp.minimum(values, 0.0))


def phi_of(values, low):
    return jnp.where(values > 0, values + 1.0, low)


def row_ids(count, begin):
    return begin + lax.broadcasted_iota(jnp.int32, (count, 1), 0)


CHIP, CORE, PLACE, VALID, ORDER = 0, 1, 2, 3, 4


def chip_block(s, j, chips):
    return lax.rem(s[CHIP] + j, chips)


def qkv_call(sc, j, chips, xa, xb, wq, wk, wv, prev):
    R, D = xa.shape
    E = wq.shape[1]
    T = 2 * R * chips
    n = min(256, E)

    def kernel(s, xa_ref, xb_ref, wq_ref, wk_ref, wv_ref, *rest):
        q_ref, k_ref, v_ref, c_ref = rest[-4:]
        base = chip_block(s, j, chips) * 2 * R
        sums = jnp.zeros((1, n), F32)
        for i, x_ref in enumerate((xa_ref, xb_ref)):
            off = pl.multiple_of((s[CORE] if i == 0 else 1 - s[CORE]) * R, R)
            rows = pl.ds(off, R)
            x = x_ref[...]
            q_ref[rows] = dot(x, wq_ref[...]).astype(BF)
            v_ref[rows] = dot(x, wv_ref[...]).astype(BF)
            k = dot(x, wk_ref[...]).astype(BF)
            k_ref[rows] = k
            k = k.astype(F32)
            phi = jnp.where(row_ids(R, base + off) < s[VALID], phi_of(k, exp_low(k)), 0.0)
            sums = sums + jnp.sum(phi, axis=0, keepdims=True)
        c_ref[...] = sums

    rows = pl.BlockSpec((R, D), lambda c, s: (0, 0))
    cols = pl.BlockSpec((D, n), lambda c, s: (0, c))
    out = pl.BlockSpec((2 * R, n), lambda c, s: (chip_block(s, j, chips), c))
    o = shape((T, E), BF)
    extra = [pl.BlockSpec(memory_space=pl.ANY)] * 3 if prev else []
    return call(
        kernel,
        (o, o, o, shape((1, E), F32)),
        (E // n,),
        [rows, rows, cols, cols, cols] + extra,
        [out, out, out, pl.BlockSpec((1, n), lambda c, s: (0, c))],
        (12 * R * D * E, 4 * R * D + 6 * D * E + 12 * R * E),
        alias={6: 0, 7: 1, 8: 2} if prev else None,
    )(sc, xa, xb, wq, wk, wv, *(prev or ()))


def grad_inner_call(sc, ca, cb, wd):
    R, D = ca.shape
    F = wd.shape[0]
    n = min(512, F)

    def kernel(s, ca_ref, cb_ref, w_ref, o_ref):
        o_ref[:R] = dot_nt(ca_ref[...], w_ref[...]).astype(BF)
        o_ref[R:] = dot_nt(cb_ref[...], w_ref[...]).astype(BF)

    rows = pl.BlockSpec((R, D), lambda c, s: (0, 0))
    return call(
        kernel,
        shape((2 * R, F), BF),
        (F // n,),
        [rows, rows, pl.BlockSpec((n, D), lambda c, s: (c, 0))],
        pl.BlockSpec((2 * R, n), lambda c, s: (0, c)),
        (4 * R * D * F, 4 * R * D + 2 * D * F + 4 * R * F),
    )(sc, ca, cb, wd)


def ffn_a_call(sc, xa, xb, wg, wu, gi):
    R, D = xa.shape
    F = wg.shape[1]
    n = min(512, F)

    def kernel(s, xa_ref, xb_ref, wg_ref, wu_ref, gi_ref, inner_ref, gg_ref, gu_ref):
        for i, x_ref in enumerate((xa_ref, xb_ref)):
            rows = slice(i * R, (i + 1) * R)
            g = dot(x_ref[...], wg_ref[...])
            u = dot(x_ref[...], wu_ref[...])
            sig = 0.5 * jnp.tanh(0.5 * g) + 0.5
            silu = g * sig
            inner_ref[rows] = (silu * u).astype(BF)
            gi_rows = gi_ref[rows].astype(F32)
            gu_ref[rows] = (gi_rows * silu).astype(BF)
            gg_ref[rows] = (gi_rows * u * (sig + silu * (1.0 - sig))).astype(BF)

    o = shape((2 * R, F), BF)
    rows = pl.BlockSpec((R, D), lambda c, s: (0, 0))
    cols = pl.BlockSpec((D, n), lambda c, s: (0, c))
    out = pl.BlockSpec((2 * R, n), lambda c, s: (0, c))
    return call(
        kernel,
        (o, o, o),
        (F // n,),
        [rows, rows, cols, cols, out],
        [out, out, out],
        (8 * R * D * F, 4 * R * D + 4 * D * F + 16 * R * F),
    )(sc, xa, xb, wg, wu, gi)


def ffn_b_call(sc, gg, gu, wg, wu):
    R2, F = gg.shape
    R = R2 // 2
    D = wg.shape[0]
    n = min(512, D)

    def kernel(s, gg_ref, gu_ref, wg_ref, wu_ref, oa_ref, ob_ref):
        for i, o_ref in enumerate((oa_ref, ob_ref)):
            rows = slice(i * R, (i + 1) * R)
            o_ref[...] = (
                dot_nt(gg_ref[rows], wg_ref[...]) + dot_nt(gu_ref[rows], wu_ref[...])
            ).astype(BF)

    o = shape((R, D), BF)
    rows = pl.BlockSpec((R2, F), lambda c, s: (0, 0))
    cols = pl.BlockSpec((n, F), lambda c, s: (c, 0))
    out = pl.BlockSpec((R, n), lambda c, s: (0, c))
    return call(
        kernel,
        (o, o),
        (D // n,),
        [rows, rows, cols, cols],
        [out, out],
        (8 * R * D * F, 8 * R * F + 4 * D * F + 4 * R * D),
    )(sc, gg, gu, wg, wu)


def down_call(sc, inner, wd):
    R2, F = inner.shape
    R = R2 // 2
    D = wd.shape[1]
    n = min(512, D)

    def kernel(s, x_ref, w_ref, oa_ref, ob_ref):
        oa_ref[...] = dot(x_ref[:R], w_ref[...]).astype(BF)
        ob_ref[...] = dot(x_ref[R:], w_ref[...]).astype(BF)

    o = shape((R, D), BF)
    out = pl.BlockSpec((R, n), lambda c, s: (0, c))
    return call(
        kernel,
        (o, o),
        (D // n,),
        [pl.BlockSpec((R2, F), lambda c, s: (0, 0)), pl.BlockSpec((F, n), lambda c, s: (0, c))],
        [out, out],
        (4 * R * D * F, 4 * R * F + 2 * D * F + 4 * R * D),
    )(sc, inner, wd)


def wgrad_call(sc, xs, gs, ndp):
    R, D = xs[0].shape
    nx = len(xs)
    C = D // ndp
    nb = len(gs[0])
    widths = [blocks[0].shape[1] for blocks in gs]
    T = R * nx
    rb = T // nb
    N = sum(widths)

    def kernel(s, *refs):
        x_refs, g_refs, (o_ref, xt) = refs[:nx], refs[nx:-2], refs[-2:]
        for p in range(nx):
            xt[:, p * R : (p + 1) * R] = x_refs[p][...].T
        at = 0
        for w, width in enumerate(widths):
            acc = None
            for b in range(nb):
                term = dot(xt[:, b * rb : (b + 1) * rb], g_refs[w * nb + b][...])
                acc = term if acc is None else acc + term
            o_ref[0, :, at : at + width] = acc.astype(BF)
            at += width

    flat = [g for blocks in gs for g in blocks]
    return call(
        kernel,
        shape((ndp, C, N), BF),
        (ndp,),
        [pl.BlockSpec((R, C), lambda j, s: (0, s[ORDER + j]))] * nx + [whole(g.shape) for g in flat],
        pl.BlockSpec((1, C, N), lambda j, s: (j, 0, 0)),
        (2 * T * D * N, 2 * T * (D + N) + 2 * D * N),
        scratch=[pltpu.VMEM((C, T), BF)],
    )(sc, *xs, *flat)


def attn_fwd_call(sc, q, k, v):
    T, E = q.shape
    hh = E // HEAD
    B = min(512, T)
    nb = T // B
    c = HEAD**-0.5 * LOG2E

    def kernel(s, q_ref, k_ref, v_ref, o_ref, lse_ref):
        valid = s[VALID]
        for i in range(nb):
            qb = q_ref[i * B : (i + 1) * B]
            parts = []
            for j in range(i + 1):
                x = dot_nt(k_ref[j * B : (j + 1) * B], qb)
                if j == i:
                    u = lax.broadcasted_iota(jnp.int32, (B, B), 0)
                    t = lax.broadcasted_iota(jnp.int32, (B, B), 1)
                    x = jnp.where(u <= t, x, NEG)
                if (j + 1) * B > T // 2:
                    x = jnp.where(row_ids(B, j * B) < valid, x, NEG)
                parts.append(x)
            top = jnp.max(parts[0], axis=0, keepdims=True)
            for x in parts[1:]:
                top = jnp.maximum(top, jnp.max(x, axis=0, keepdims=True))
            top = top * c
            total = jnp.zeros((1, B), F32)
            acc = jnp.zeros((HEAD, B), F32)
            for j, x in enumerate(parts):
                p = jnp.exp2(x * c - top)
                total = total + jnp.sum(p, axis=0, keepdims=True)
                acc = acc + dot_tn(v_ref[j * B : (j + 1) * B], p.astype(BF))
            o_ref[i * B : (i + 1) * B] = (acc * (1.0 / total)).T
            lse_ref[0, :, i * B : (i + 1) * B] = top + jnp.log2(total)

    head = pl.BlockSpec((T, HEAD), lambda h, s: (0, h))
    return call(
        kernel,
        (shape((T, E), F32), shape((hh, 1, T), F32)),
        (hh,),
        [head, head, head],
        [head, pl.BlockSpec((1, 1, T), lambda h, s: (h, 0, 0))],
        (6 * T * T * E, 10 * T * E),
    )(sc, q, k, v)


def attn_bwd_call(sc, q, k, v, do, lo, lse, h0, nh):
    T = q.shape[0]
    B = min(512, T)
    nb = T // B
    scale = HEAD**-0.5
    c = scale * LOG2E

    def kernel(s, q_ref, k_ref, v_ref, do_ref, lo_ref, lse_ref, dq_ref, dk_ref, dv_ref, delta):
        valid = s[VALID]
        ones = jnp.ones((8, HEAD), F32)
        for i in range(nb):
            rows = slice(i * B, (i + 1) * B)
            prod = do_ref[rows].astype(F32) * lo_ref[rows]
            delta[:, rows] = lax.dot_general(
                ones,
                prod,
                (((1,), (1,)), ((), ())),
                precision=lax.Precision.HIGHEST,
                preferred_element_type=F32,
            )
        dq_ref[...] = jnp.zeros_like(dq_ref)
        for j in range(nb):
            kb = k_ref[j * B : (j + 1) * B]
            vb = v_ref[j * B : (j + 1) * B]
            dk = jnp.zeros((B, HEAD), F32)
            dv = jnp.zeros((B, HEAD), F32)
            for i in range(j, nb):
                rows = slice(i * B, (i + 1) * B)
                qb = q_ref[rows]
                dob = do_ref[rows]
                p = jnp.exp2(dot_nt(kb, qb) * c - lse_ref[0, :, rows])
                if i == j:
                    u = lax.broadcasted_iota(jnp.int32, (B, B), 0)
                    t = lax.broadcasted_iota(jnp.int32, (B, B), 1)
                    p = jnp.where(u <= t, p, 0.0)
                if (j + 1) * B > T // 2:
                    p = jnp.where(row_ids(B, j * B) < valid, p, 0.0)
                ds = (p * (dot_nt(vb, dob) - delta[0:1, rows])).astype(BF)
                dv = dv + dot(p.astype(BF), dob)
                dk = dk + dot(ds, qb)
                dq_ref[rows] += dot_tn(ds, kb)
            dk_ref[j * B : (j + 1) * B] = dk * scale
            dv_ref[j * B : (j + 1) * B] = dv
        dq_ref[...] *= scale

    o = shape((T, nh * HEAD), F32)
    head = pl.BlockSpec((T, HEAD), lambda h, s: (0, h0 + h))
    out = pl.BlockSpec((T, HEAD), lambda h, s: (0, h))
    return call(
        kernel,
        (o, o, o),
        (nh,),
        [head] * 5 + [pl.BlockSpec((1, 1, T), lambda h, s: (h0 + h, 0, 0))],
        [out, out, out],
        (12 * T * T * HEAD * nh, 26 * T * HEAD * nh),
        scratch=[pltpu.VMEM((8, T), F32)],
    )(sc, q, k, v, do, lo, lse)


def maps_call(sc, k, v, gathered):
    T, E = k.shape
    hh = E // HEAD
    ndp = gathered.shape[0]

    def kernel(s, k_ref, v_ref, g_ref, maps_ref, norm_ref):
        h = pl.program_id(0)
        norm = jnp.zeros((1, HEAD), F32)
        for a in range(ndp - 1):
            after = (norm + g_ref[a, pl.ds(h, 1)]) * g_ref[a + 1, hh : hh + 1]
            norm = jnp.where(a < s[PLACE], after, norm)
        norm_ref[0] = norm
        k = k_ref[...].astype(F32)
        phi = jnp.where(row_ids(T, 0) < s[VALID], phi_of(k, exp_low(k)), 0.0)
        den = jnp.maximum(jnp.sum(phi * norm, axis=1, keepdims=True), 1.0)
        low = phi.astype(BF)
        maps_ref[0, 0] = dot_tn((phi * (1.0 / den)).astype(BF), low).astype(BF)
        maps_ref[1, 0] = dot_tn(low, v_ref[...]).astype(BF)

    head = pl.BlockSpec((T, HEAD), lambda h, s: (0, h))
    return call(
        kernel,
        (shape((2, hh, HEAD, HEAD), BF), shape((hh, 1, HEAD), F32)),
        (hh,),
        [head, head, whole(gathered.shape)],
        [
            pl.BlockSpec((2, 1, HEAD, HEAD), lambda h, s: (0, h, 0, 0)),
            pl.BlockSpec((1, 1, HEAD), lambda h, s: (h, 0, 0)),
        ],
        (4 * T * E * HEAD, 4 * T * E),
    )(sc, k, v, gathered)


def times_state(g, state):
    high = state.astype(BF)
    return dot(g, high) + dot(g, (state - high.astype(F32)).astype(BF))


def chain_call(sc, gathered, maps):
    ndp, _, hh = maps.shape[:3]

    def kernel(s, g_ref, maps_ref, m_ref):
        state = [jnp.zeros((HEAD, HEAD), F32) for _ in range(hh)]
        for a in range(ndp - 1):
            keep = g_ref[a + 1, hh : hh + 1]
            before = a < s[PLACE]
            for h in range(hh):
                after = state[h] - times_state(maps_ref[a, 0, h], state[h])
                after = (after + maps_ref[a, 1, h].astype(F32)) * keep
                state[h] = jnp.where(before, after, state[h])
        for h in range(hh):
            m_ref[h] = state[h]

    return call(
        kernel,
        shape((hh, HEAD, HEAD), F32),
        (1,),
        [whole(gathered.shape), whole(maps.shape)],
        whole((hh, HEAD, HEAD)),
        (4e8, 2 * maps.size),
    )(sc, gathered, maps)


def mixout_call(sc, j, chips, q, local, memory, norm, mix, wo):
    T, E = q.shape
    hh = E // HEAD
    D = wo.shape[1]
    R = T // chips // 2
    n = min(512, D)

    def kernel(s, q_ref, l_ref, m_ref, n_ref, mix_ref, w_ref, oa_ref, ob_ref, mixed_ref, diff_ref):
        @pl.when(pl.program_id(0) == 0)
        def _():
            for i in range(2):
                off = pl.multiple_of((s[CORE] if i == 0 else 1 - s[CORE]) * R, R)
                for h in range(hh):
                    cols = slice(h * HEAD, (h + 1) * HEAD)
                    qv = q_ref[pl.ds(off, R), cols].astype(F32)
                    phi = phi_of(qv, exp_low(qv))
                    den = jnp.maximum(jnp.sum(phi * n_ref[h], axis=1, keepdims=True), 1.0)
                    read = dot(phi.astype(BF), m_ref[h].astype(BF)) * (1.0 / den)
                    diff = read - l_ref[pl.ds(off, R), cols]
                    mixed = l_ref[pl.ds(off, R), cols] + mix_ref[h] * diff
                    diff_ref[i * R : (i + 1) * R, cols] = diff.astype(BF)
                    mixed_ref[i * R : (i + 1) * R, cols] = mixed.astype(BF)

        oa_ref[...] = dot(mixed_ref[:R], w_ref[...]).astype(BF)
        ob_ref[...] = dot(mixed_ref[R:], w_ref[...]).astype(BF)

    rows = pl.BlockSpec((2 * R, E), lambda c, s: (chip_block(s, j, chips), 0))
    out = pl.BlockSpec((R, n), lambda c, s: (0, c))
    rel = pl.BlockSpec((2 * R, E), lambda c, s: (0, 0))
    return call(
        kernel,
        (shape((R, D), BF), shape((R, D), BF), shape((2 * R, E), BF), shape((2 * R, E), BF)),
        (D // n,),
        [rows, rows, whole(memory.shape), whole(norm.shape), whole(mix.shape), pl.BlockSpec((E, n), lambda c, s: (0, c))],
        [out, out, rel, rel],
        (4 * R * E * D + 8 * R * E * HEAD, 20 * R * E + 2 * E * D + 4 * R * D),
    )(sc, q, local, memory, norm, mix, wo)


def gradmix_call(sc, j, chips, ya, yb, wo, diff, q, norm, mix, prev):
    R, D = ya.shape
    E = wo.shape[0]
    hh = E // HEAD
    T = 2 * R * chips
    n = min(256, E)
    per = n // HEAD

    def kernel(s, ya_ref, yb_ref, w_ref, diff_ref, q_ref, n_ref, mix_ref, *rest):
        do_ref, gm_ref, cot_ref, b_ref = rest[-4:]
        sums = jnp.zeros((1, n), F32)
        cots = [jnp.zeros((HEAD, HEAD), F32) for _ in range(per)]
        for i, y_ref in enumerate((ya_ref, yb_ref)):
            off = pl.multiple_of((s[CORE] if i == 0 else 1 - s[CORE]) * R, R)
            grad = dot_nt(y_ref[...], w_ref[...])
            sums = sums + jnp.sum(grad * diff_ref[i * R : (i + 1) * R].astype(F32), axis=0, keepdims=True)
            for h in range(per):
                cols = slice(h * HEAD, (h + 1) * HEAD)
                part = grad[:, cols]
                grad_read = part * mix_ref[h]
                do_ref[pl.ds(off, R), cols] = (part - grad_read).astype(BF)
                gm_ref[pl.ds(off, R), cols] = grad_read.astype(BF)
                qv = q_ref[pl.ds(off, R), cols].astype(F32)
                phi = phi_of(qv, exp_low(qv))
                den = jnp.maximum(jnp.sum(phi * n_ref[h], axis=1, keepdims=True), 1.0)
                cots[h] = cots[h] + dot_tn(phi.astype(BF), (grad_read * (1.0 / den)).astype(BF))
        for h in range(per):
            cot_ref[h] = cots[h]
        b_ref[...] = sums

    rows = pl.BlockSpec((R, D), lambda c, s: (0, 0))
    place = pl.BlockSpec((2 * R, n), lambda c, s: (chip_block(s, j, chips), c))
    per_head = pl.BlockSpec((per, 1, HEAD), lambda c, s: (c, 0, 0))
    o = shape((T, E), BF)
    extra = [pl.BlockSpec(memory_space=pl.ANY)] * 2 if prev else []
    return call(
        kernel,
        (o, o, shape((hh, HEAD, HEAD), F32), shape((1, E), F32)),
        (E // n,),
        [rows, rows, pl.BlockSpec((n, D), lambda c, s: (c, 0)), pl.BlockSpec((2 * R, n), lambda c, s: (0, c)), place, per_head, per_head] + extra,
        [place, place, pl.BlockSpec((per, HEAD, HEAD), lambda c, s: (c, 0, 0)), pl.BlockSpec((1, n), lambda c, s: (0, c))],
        (4 * R * E * D + 4 * R * E * HEAD, 4 * R * D + 2 * E * D + 16 * R * E),
        alias={8: 0, 9: 1} if prev else None,
    )(sc, ya, yb, wo, diff, q, norm, mix, *(prev or ()))


def memory_rows(q, k, grad_read, live, memory, norm, cot):
    low_q = exp_low(q)
    low_k = exp_low(k)
    phi_q = phi_of(q, low_q)
    phi_k = jnp.where(live, phi_of(k, low_k), 0.0)
    raw_q = jnp.sum(phi_q * norm, axis=1, keepdims=True)
    raw_k = jnp.sum(phi_k * norm, axis=1, keepdims=True)
    inv_q = 1.0 / jnp.maximum(raw_q, 1.0)
    inv_k = 1.0 / jnp.maximum(raw_k, 1.0)
    read = dot(phi_q.astype(BF), memory)
    recalled = dot(phi_k.astype(BF), memory) * inv_k
    pushed = dot(phi_k.astype(BF), cot)
    scaled = grad_read * inv_q
    w_q = jnp.where(raw_q > 1.0, -jnp.sum(scaled * read, axis=1, keepdims=True) * inv_q, 0.0)
    w_k = jnp.where(raw_k > 1.0, jnp.sum(pushed * recalled, axis=1, keepdims=True) * inv_k, 0.0)
    return low_q, low_k, phi_q, phi_k, inv_k, recalled, pushed, scaled, w_q, w_k


def memory_cot_call(sc, gathered, maps, cots, q, k, grad_read, memory, norm):
    T, E = q.shape
    hh = E // HEAD
    ndp = maps.shape[0]
    B = min(512, T)

    def kernel(s, g_ref, maps_ref, cots_ref, q_ref, k_ref, gm_ref, m_ref, n_ref, x_ref, nb_ref):
        cot = jnp.zeros((HEAD, HEAD), F32)
        for a in range(ndp - 1, 0, -1):
            before = cot - times_state(maps_ref[a, 0, 0], cot) + cots_ref[a, 0].astype(F32)
            cot = jnp.where(a > s[PLACE], before * g_ref[a, hh : hh + 1], cot)
        x_ref[0] = cot
        cot = cot.astype(BF)
        memory = m_ref[0].astype(BF)
        sums = jnp.zeros((1, HEAD), F32)
        for i in range(T // B):
            rows = slice(i * B, (i + 1) * B)
            live = row_ids(B, i * B) < s[VALID]
            terms = memory_rows(
                q_ref[rows].astype(F32), k_ref[rows].astype(F32), gm_ref[rows].astype(F32), live, memory, n_ref[0], cot
            )
            sums = sums + jnp.sum(terms[2] * terms[8] + terms[3] * terms[9], axis=0, keepdims=True)
        nb_ref[0] = sums

    head = pl.BlockSpec((T, HEAD), lambda h, s: (0, h))
    square = pl.BlockSpec((1, HEAD, HEAD), lambda h, s: (h, 0, 0))
    row = pl.BlockSpec((1, 1, HEAD), lambda h, s: (h, 0, 0))
    return call(
        kernel,
        (shape((hh, HEAD, HEAD), F32), shape((hh, 1, HEAD), F32)),
        (hh,),
        [
            whole(gathered.shape),
            pl.BlockSpec((ndp, 1, 1, HEAD, HEAD), lambda h, s: (0, 0, h, 0, 0)),
            pl.BlockSpec((ndp, 1, HEAD, HEAD), lambda h, s: (0, h, 0, 0)),
            head,
            head,
            head,
            square,
            row,
        ],
        [square, row],
        (8 * T * E * HEAD, 6 * T * E),
    )(sc, gathered, maps, cots, q, k, grad_read, memory, norm)


def combine_call(sc, chips, q, k, v, grad_read, local_grads, memory, norm, cot, gathered, norm_parts):
    T, E = q.shape
    hh = E // HEAD
    R = T // chips // 2
    ndp = gathered.shape[0]
    per = local_grads[0][0].shape[1] // HEAD
    groups = len(local_grads)

    def kernel(s, q_ref, k_ref, v_ref, gm_ref, *rest):
        local_refs = rest[: 3 * groups]
        m_ref, n_ref, x_ref, g_ref, nb_ref, gq_ref, gk_ref, gv_ref = rest[3 * groups :]
        begin = piece(pl.program_id(0), s) * R
        live = row_ids(R, begin) < s[VALID]
        for h in range(hh):
            cols = slice(h * HEAD, (h + 1) * HEAD)
            part = slice(h % per * HEAD, (h % per + 1) * HEAD)
            dq, dk, dv = (ref[:, part] for ref in local_refs[3 * (h // per) : 3 * (h // per) + 3])
            norm_cot = jnp.zeros((1, HEAD), F32)
            for a in range(ndp - 1, 0, -1):
                before = (norm_cot + nb_ref[a, h : h + 1]) * g_ref[a, hh : hh + 1]
                norm_cot = jnp.where(a > s[PLACE], before, norm_cot)
            memory = m_ref[h].astype(BF)
            cot = x_ref[h].astype(BF)
            norm = n_ref[h]
            low_q, low_k, _, _, inv_k, recalled, pushed, scaled, w_q, w_k = memory_rows(
                q_ref[:, cols].astype(F32), k_ref[:, cols].astype(F32), gm_ref[:, cols].astype(F32), live, memory, norm, cot
            )
            grad_phi_q = dot_nt(scaled.astype(BF), memory) + w_q * norm
            grad_phi_k = (
                dot_nt((v_ref[:, cols].astype(F32) - recalled).astype(BF), cot)
                - dot_nt((pushed * inv_k).astype(BF), memory)
                + w_k * norm
                + norm_cot
            )
            gq_ref[:, cols] = (dq + grad_phi_q * low_q).astype(BF)
            gk_ref[:, cols] = (dk + jnp.where(live, grad_phi_k * low_k, 0.0)).astype(BF)
            gv_ref[:, cols] = (dv + pushed).astype(BF)

    def piece(p, s):
        core = lax.rem(s[CORE] + p, 2)
        return chip_block(s, p // 2, chips) * 2 + core

    rows = pl.BlockSpec((R, E), lambda p, s: (piece(p, s), 0))
    part_rows = pl.BlockSpec((R, per * HEAD), lambda p, s: (piece(p, s), 0))
    out = pl.BlockSpec((R, E), lambda p, s: (p, 0))
    o = shape((T, E), BF)
    return call(
        kernel,
        (o, o, o),
        (2 * chips,),
        [rows] * 4 + [part_rows] * (3 * groups) + [whole(x.shape) for x in (memory, norm, cot, gathered, norm_parts)],
        [out, out, out],
        (14 * T * E * HEAD, 26 * T * E),
    )(sc, q, k, v, grad_read, *[x for group in local_grads for x in group], memory, norm, cot, gathered, norm_parts)


def grad_normed_call(sc, j, gq, gk, gv, wq, wk, wv, chips):
    T, E = gq.shape
    R = T // chips // 2
    D = wq.shape[0]
    n = min(512, D)

    def kernel(s, gq_ref, gk_ref, gv_ref, wq_ref, wk_ref, wv_ref, oa_ref, ob_ref):
        for i, o_ref in enumerate((oa_ref, ob_ref)):
            rows = slice(i * R, (i + 1) * R)
            o_ref[...] = (
                dot_nt(gq_ref[rows], wq_ref[...]) + dot_nt(gk_ref[rows], wk_ref[...]) + dot_nt(gv_ref[rows], wv_ref[...])
            ).astype(BF)

    o = shape((R, D), BF)
    rows = pl.BlockSpec((2 * R, E), lambda c, s: (j, 0))
    cols = pl.BlockSpec((n, E), lambda c, s: (c, 0))
    out = pl.BlockSpec((R, n), lambda c, s: (0, c))
    return call(
        kernel,
        (o, o),
        (D // n,),
        [rows, rows, rows, cols, cols, cols],
        [out, out],
        (12 * R * D * E, 12 * R * E + 6 * D * E + 4 * R * D),
    )(sc, gq, gk, gv, wq, wk, wv)


def swap_core(x):
    return lax.ppermute(x, "tensor", [(i, i ^ 1) for i in range(lax.axis_size("tensor"))])


def shift_chip(x, j):
    count = lax.axis_size("tensor")
    return lax.ppermute(x, "tensor", [(i, (i + 2 * j) % count) for i in range(count)])


def after(x, *others):
    return lax.optimization_barrier((x, *others))[0]


def gather_rows(x, chips, wait=None):
    blocks = [(x, swap_core(x))]
    far = x if wait is None else after(x, wait)
    for j in range(1, chips):
        moved = shift_chip(far, -j)
        blocks.append((moved, swap_core(moved)))
    return blocks


def scatter_rows(blocks, wait=None):
    sums = [mine.astype(F32) + swap_core(other).astype(F32) for mine, other in blocks]
    total = sums[0]
    for j in range(1, len(blocks)):
        low = sums[j].astype(BF)
        if wait is not None:
            low = after(low, wait)
        total = total + shift_chip(low, j).astype(F32)
    return total


def chunk_order(me, ndp):
    parity = me % 2
    order = [2 * i + (1 - parity) for i in range(ndp // 2)] + [2 * i + parity for i in range(ndp // 2)]
    return jnp.stack(order)


def sum_over_dp(grads):
    ndp = grads.shape[0]
    half = ndp // 2
    got = lax.ppermute(grads[:half], "dp", [(i, i ^ 1) for i in range(ndp)])
    pair = (got.astype(F32) + grads[half:].astype(F32)).astype(BF)
    groups = [list(range(0, ndp, 2)), list(range(1, ndp, 2))]
    out = lax.psum_scatter(pair.reshape((-1, grads.shape[2])), "dp", scatter_dimension=0, axis_index_groups=groups, tiled=True)
    return out.astype(F32)


def sum_everywhere(x):
    for axis in ("tensor", "dp"):
        count, step = lax.axis_size(axis), 1
        while step < count:
            x = x + lax.ppermute(x, axis, [(i, i ^ step) for i in range(count)])
            step *= 2
    return x


def body(
    tokens,
    gain1,
    w_query,
    w_key,
    w_value,
    w_out,
    gate_bias,
    gain2,
    w_gate,
    w_up,
    w_down,
    seg_starts,
    seg_valid,
    cotangent,
):
    count = lax.axis_size("tensor")
    ndp = lax.axis_size("dp")
    chips = count // 2
    hh = gate_bias.shape[0]
    E = hh * HEAD
    here = lax.axis_index("tensor")
    place = lax.axis_index("dp")
    sc = jnp.concatenate(
        [
            jnp.stack([here // 2, here % 2, place]).astype(jnp.int32),
            seg_valid.astype(jnp.int32),
            chunk_order(place, ndp).astype(jnp.int32),
        ]
    )
    keep = (1 - seg_starts[0]).astype(F32)
    sig_bias = jax.nn.sigmoid(gate_bias)
    mix = jnp.broadcast_to(sig_bias[:, None, None], (hh, 1, HEAD))

    x = tokens.astype(F32)
    inv1 = lax.rsqrt(jnp.mean(x * x, axis=-1, keepdims=True) + EPSILON)
    normed1 = (x * inv1 * gain1).astype(BF)
    rows1 = gather_rows(normed1, chips)
    qkv = None
    sums = 0.0
    for j, (a, b) in enumerate(rows1):
        *qkv, column_sums = qkv_call(sc, j, chips, a, b, w_query, w_key, w_value, qkv)
        sums = sums + column_sums
    q, k, v = qkv
    cot_rows = gather_rows(cotangent, chips, wait=rows1[-1][0])

    own = jnp.concatenate([sums.reshape(hh, HEAD), jnp.full((8 - hh, HEAD), keep, F32)])
    gathered = lax.all_gather(own, "dp")
    maps, norm = maps_call(sc, k, v, gathered)
    all_maps = lax.all_gather(maps, "dp")
    local, lse = attn_fwd_call(sc, q, k, v)
    memory = chain_call(sc, gathered, all_maps)

    grad_inner = [grad_inner_call(sc, a, b, w_down) for a, b in cot_rows]
    partial, mixed, diff = [None] * chips, [None] * chips, [None] * chips
    for j in reversed(range(chips)):
        a, b, mixed[j], diff[j] = mixout_call(sc, j, chips, q, local, memory, norm, mix, w_out)
        partial[j] = (a, b)
    hidden = x + scatter_rows(partial)
    inv2 = lax.rsqrt(jnp.mean(hidden * hidden, axis=-1, keepdims=True) + EPSILON)
    unit2 = hidden * inv2
    normed2 = (unit2 * gain2).astype(BF)
    rows2 = gather_rows(normed2, chips)

    inner, grad_gate, grad_up = [], [], []
    for (a, b), gi in zip(rows2, grad_inner):
        one, two, three = ffn_a_call(sc, a, b, w_gate, w_up, gi)
        inner.append(one)
        grad_gate.append(two)
        grad_up.append(three)
    back = [None] * chips
    for j in reversed(range(chips)):
        back[j] = ffn_b_call(sc, grad_gate[j], grad_up[j], w_gate, w_up)
    grad_normed2 = scatter_rows(back)
    flat_rows2 = [piece for block in rows2 for piece in block]
    flat_cot = [piece for block in cot_rows for piece in block]
    grad_down = sum_over_dp(wgrad_call(sc, flat_cot, [inner], ndp))
    grad_gate_up = sum_over_dp(wgrad_call(sc, flat_rows2, [grad_gate, grad_up], ndp))

    gain2_part = jnp.sum(grad_normed2 * unit2, axis=0)
    scaled2 = grad_normed2 * gain2
    grad_hidden = cotangent.astype(F32) + inv2 * (
        scaled2 - unit2 * jnp.mean(scaled2 * unit2, axis=-1, keepdims=True)
    )
    grad_rows = gather_rows(grad_hidden.astype(BF), chips)
    grads = None
    cot_part, bias_part = 0.0, 0.0
    for j, (a, b) in enumerate(grad_rows):
        *grads, cot_j, bias_j = gradmix_call(sc, j, chips, a, b, w_out, diff[j], q, norm, mix, grads)
        cot_part = cot_part + cot_j
        bias_part = bias_part + bias_j
    grad_local, grad_read = grads
    all_cots = lax.all_gather(cot_part.astype(BF), "dp")

    down = [down_call(sc, block, w_down) for block in inner]
    output = (hidden + scatter_rows(down, wait=grad_rows[-1][0])).astype(BF)
    flat_grad = [piece for block in grad_rows for piece in block]
    grad_out = sum_over_dp(wgrad_call(sc, flat_grad, [mixed], ndp))

    per = max(1, hh // 2)
    local_grads = [
        attn_bwd_call(sc, q, k, v, grad_local, local, lse, h, per) for h in range(0, hh, per)
    ]
    memory_cot, norm_part = memory_cot_call(sc, gathered, all_maps, all_cots, q, k, grad_read, memory, norm)
    norm_pad = jnp.concatenate([norm_part.reshape(hh, HEAD), jnp.zeros((8 - hh, HEAD), F32)])
    norm_parts = lax.all_gather(norm_pad, "dp")
    gq, gk, gv = combine_call(
        sc, chips, q, k, v, grad_read, local_grads, memory, norm, memory_cot, gathered, norm_parts
    )
    flat_rows1 = [piece for block in rows1 for piece in block]
    grad_qkv = sum_over_dp(wgrad_call(sc, flat_rows1, [[gq], [gk], [gv]], ndp))
    back1 = [None] * chips
    for j in reversed(range(chips)):
        back1[j] = grad_normed_call(sc, j, gq, gk, gv, w_query, w_key, w_value, chips)
    grad_normed1 = scatter_rows(back1)
    unit1 = x * inv1
    gain1_part = jnp.sum(grad_normed1 * unit1, axis=0)
    scaled1 = grad_normed1 * gain1
    grad_tokens = grad_hidden + inv1 * (
        scaled1 - unit1 * jnp.mean(scaled1 * unit1, axis=-1, keepdims=True)
    )

    bias_here = jnp.sum(bias_part.reshape(hh, HEAD), axis=1) * sig_bias * (1.0 - sig_bias)
    bias_full = lax.dynamic_update_slice(jnp.zeros((HEADS,), F32), bias_here, (here * hh,))
    small = sum_everywhere(jnp.concatenate([gain1_part, gain2_part, bias_full]))
    D = gain1.shape[0]
    F = w_gate.shape[1]
    return (
        output,
        grad_tokens,
        small[:D],
        grad_qkv[:, :E],
        grad_qkv[:, E : 2 * E],
        grad_qkv[:, 2 * E :],
        grad_out.T,
        small[2 * D :],
        small[D : 2 * D],
        grad_gate_up[:, :F],
        grad_gate_up[:, F:],
        grad_down.T,
    )


def solution(mesh):
    rows = P(("dp", "tensor"), None)
    return jax.shard_map(
        body,
        mesh=mesh,
        in_specs=(
            rows,
            P(),
            P(None, "tensor"),
            P(None, "tensor"),
            P(None, "tensor"),
            P("tensor", None),
            P("tensor"),
            P(),
            P(None, "tensor"),
            P(None, "tensor"),
            P("tensor", None),
            P("dp"),
            P("dp"),
            rows,
        ),
        out_specs=(
            rows,
            rows,
            P(),
            P("dp", "tensor"),
            P("dp", "tensor"),
            P("dp", "tensor"),
            P("tensor", "dp"),
            P(),
            P(),
            P("dp", "tensor"),
            P("dp", "tensor"),
            P("tensor", "dp"),
        ),
        check_vma=False,
    )
```

```python
import jax
import jax.numpy as jnp
from jax import lax
from jax.experimental import pallas as pl
from jax.experimental.pallas import tpu as pltpu
from jax.sharding import PartitionSpec as P

HEADS = 16
HEAD = 128
EPSILON = 1e-06
BF = jnp.bfloat16
F32 = jnp.float32
LOG2E = 1.4426950408889634
NEG = -1e30
VMEM_BYTES = 56 << 20


def dot(a, b):
    return jnp.dot(a, b, preferred_element_type=F32)


def dot_nt(a, b):
    return lax.dot_general(a, b, (((1,), (1,)), ((), ())), preferred_element_type=F32)


def dot_tn(a, b):
    return lax.dot_general(a, b, (((0,), (0,)), ((), ())), preferred_element_type=F32)


def shape(dims, dtype):
    return jax.ShapeDtypeStruct(dims, dtype)


COST = 20.0
ORDERED = []


def call(kernel, out_shape, grid, in_specs, out_specs, cost, scratch=(), alias=None):
    many = isinstance(out_shape, tuple)
    plain = len(in_specs) + 1
    token = [pl.BlockSpec(memory_space=pl.ANY)] * len(ORDERED)

    def ordered_kernel(*refs):
        kernel(*refs[:plain], *refs[plain + len(token) :])

    made = pl.pallas_call(
        ordered_kernel,
        out_shape=out_shape,
        grid_spec=pltpu.PrefetchScalarGridSpec(
            num_scalar_prefetch=1,
            grid=grid,
            in_specs=list(in_specs) + token,
            out_specs=out_specs,
            scratch_shapes=list(scratch),
        ),
        input_output_aliases=alias or {},
        compiler_params=pltpu.CompilerParams(
            dimension_semantics=("arbitrary",) * len(grid), vmem_limit_bytes=VMEM_BYTES
        ),
        cost_estimate=pl.CostEstimate(
            flops=int(COST * cost[0]), bytes_accessed=int(COST * cost[1]), transcendentals=0
        ),
    )

    def run(*operands):
        out = made(*operands, *ORDERED)
        ORDERED[:] = [out[-1] if many else out]
        return out

    return run


def require(*arrays):
    ORDERED.extend(arrays)


def hold(sc, *arrays):
    n = len(arrays)

    def kernel(*refs):
        del refs

    one = pl.BlockSpec(memory_space=pl.ANY)
    found = call(
        kernel,
        tuple(shape(x.shape, x.dtype) for x in arrays),
        (1,),
        [one] * n,
        [one] * n,
        (1e6, 1e4),
        alias={1 + i: i for i in range(n)},
    )(sc, *arrays)
    ORDERED.clear()
    ORDERED.append(found[0])
    return found


def hold_pairs(sc, pairs):
    found = hold(sc, *[x for pair in pairs for x in pair])
    return [tuple(found[2 * i : 2 * i + 2]) for i in range(len(pairs))]


class Halves:
    def __init__(self, low, high, first):
        self.low, self.high, self.first = low, high, first

    def __getitem__(self, at):
        return jnp.where(self.first, self.low[at], self.high[at])

    def __setitem__(self, at, value):
        @pl.when(self.first)
        def _():
            self.low[at] = value

        @pl.when(jnp.logical_not(self.first))
        def _():
            self.high[at] = value


def rows_call(kernel, outs, sc, rows, shared, sums=0):
    first = rows[0]
    R, D = (2 * first[0].shape[0], first[0].shape[1]) if isinstance(first, tuple) else first.shape
    n = min(128, R // 2)
    half = R // 2 // n
    block = pl.BlockSpec((n, D), lambda i, s: (i, 0))
    low = pl.BlockSpec((n, D), lambda i, s: (jnp.minimum(i, half - 1), 0))
    high = pl.BlockSpec((n, D), lambda i, s: (jnp.maximum(i - half, 0), 0))
    one = pl.BlockSpec((1, D), lambda i, s: (0, 0))
    in_specs, operands, kinds = [], [], []
    for x in rows:
        pair = isinstance(x, tuple)
        kinds.append(pair)
        in_specs += [low, high] if pair else [block]
        operands += list(x) if pair else [x]
    kinds += [False] * len(shared)
    out_specs, out_shapes = [], []
    for x in outs:
        pair = isinstance(x, list)
        kinds.append(pair)
        out_specs += [low, high] if pair else [block]
        out_shapes += [shape((R // 2, D), x[0])] * 2 if pair else [shape((R, D), x)]
    kinds += [False] * sums

    def body_kernel(s, *refs):
        i = pl.program_id(0)

        @pl.when(i == 0)
        def _():
            for ref in refs[len(refs) - sums :] if sums else ():
                ref[...] = jnp.zeros_like(ref)

        views, at = [], 0
        for pair in kinds:
            views.append(Halves(refs[at], refs[at + 1], i < half) if pair else refs[at])
            at += 2 if pair else 1
        kernel(*views)

    found = call(
        body_kernel,
        tuple(out_shapes + [shape((1, D), F32)] * sums),
        (R // n,),
        in_specs + [one] * len(shared),
        out_specs + [one] * sums,
        (10 * R * D, 20 * R * D),
    )(sc, *operands, *shared)
    result, at = [], 0
    for x in outs:
        pair = isinstance(x, list)
        result.append(tuple(found[at : at + 2]) if pair else found[at])
        at += 2 if pair else 1
    return result + list(found[at:])


def add_rows(sc, terms, split):
    def kernel(*refs):
        refs[-1][...] = sum(ref[...].astype(F32) for ref in refs[:-1]).astype(BF)

    return rows_call(kernel, [[BF] if split else BF], sc, terms, [])[0]


def unit_rows(values):
    inverse = lax.rsqrt(jnp.mean(values * values, axis=-1, keepdims=True) + EPSILON)
    return values * inverse, inverse


def norm_call(sc, terms, gain):
    def kernel(*refs):
        gain_ref, sum_ref, out_ref = refs[-3:]
        total = sum(ref[...].astype(F32) for ref in refs[:-3])
        sum_ref[...] = total
        out_ref[...] = (unit_rows(total)[0] * gain_ref[...]).astype(BF)

    return rows_call(kernel, [F32, [BF]], sc, terms, [gain])


def norm_back_call(sc, base, values, terms, gain, low):
    def kernel(base_ref, values_ref, *refs):
        term_refs, gain_ref, outs = refs[: len(terms)], refs[len(terms)], refs[len(terms) + 1 :]
        grad = sum(ref[...].astype(F32) for ref in term_refs)
        unit, inverse = unit_rows(values_ref[...].astype(F32))
        if low:
            outs[-1][...] += jnp.sum(grad * unit, axis=0, keepdims=True)
        scaled = grad * gain_ref[...]
        out = base_ref[...].astype(F32) + inverse * (
            scaled - unit * jnp.mean(scaled * unit, axis=-1, keepdims=True)
        )
        outs[0][...] = out
        if low:
            outs[1][...] = out.astype(BF)

    return rows_call(kernel, [F32, [BF]] if low else [F32], sc, [base, values, *terms], [gain], sums=1 if low else 0)


def pair_call(sc, parts):
    half, C, _ = parts[0][0].shape
    widths = [near.shape[2] for _, near in parts]
    N = sum(widths)

    def kernel(s, *refs):
        at = 0
        for p, width in enumerate(widths):
            total = refs[2 * p][0].astype(F32) + refs[2 * p + 1][0].astype(F32)
            refs[-1][:, at : at + width] = total.astype(BF)
            at += width

    return call(
        kernel,
        shape((half * C, N), BF),
        (half,),
        [pl.BlockSpec((1, C, width), lambda i, s: (i, 0, 0)) for width in widths for _ in range(2)],
        pl.BlockSpec((C, N), lambda i, s: (i, 0)),
        (half * C * N, 6 * half * C * N),
    )(sc, *[x for part in parts for x in part])


def stage(refs, x_ref):
    @pl.when(pl.program_id(0) == 0)
    def _():
        at = 0
        for ref in refs:
            x_ref[at : at + ref.shape[0]] = ref[...]
            at += ref.shape[0]


def staged(block):
    H, D = block[0].shape
    return [pl.BlockSpec((H, D), lambda c, s: (0, 0), pipeline_mode=pl.Buffered(1))] * 4, pltpu.VMEM((4 * H, D), BF)


def put_rows(refs, value):
    at = 0
    for ref in refs:
        ref[...] = value[at : at + ref.shape[0]].astype(BF)
        at += ref.shape[0]


def whole(dims):
    return pl.BlockSpec(dims, lambda *_: (0,) * len(dims), pipeline_mode=pl.Buffered(1))


def exp_low(values):
    return jnp.exp(jnp.minimum(values, 0.0))


def phi_of(values, low):
    return jnp.where(values > 0, values + 1.0, low)


def row_ids(count, begin):
    return begin + lax.broadcasted_iota(jnp.int32, (count, 1), 0)


CHIP, CORE, PLACE, VALID, ORDER = 0, 1, 2, 3, 4


def chip_block(s, j, chips):
    return lax.rem(s[CHIP] + j, chips)


def qkv_call(sc, j, chips, block, wq, wk, wv, prev):
    R, D = 2 * block[0].shape[0], block[0].shape[1]
    E = wq.shape[1]
    T = 2 * R * chips
    n = min(256, E)

    def kernel(s, *refs):
        wq_ref, wk_ref, wv_ref = refs[4:7]
        q_ref, k_ref, v_ref, c_ref, x_ref = refs[-5:]
        stage(refs[:4], x_ref)
        base = chip_block(s, j, chips) * 2 * R
        sums = jnp.zeros((1, n), F32)
        x = x_ref[...]
        q, k, v = (dot(x, ref[...]).astype(BF) for ref in (wq_ref, wk_ref, wv_ref))
        for i in range(2):
            off = pl.multiple_of((s[CORE] if i == 0 else 1 - s[CORE]) * R, R)
            rows, part = pl.ds(off, R), slice(i * R, (i + 1) * R)
            q_ref[rows] = q[part]
            k_ref[rows] = k[part]
            v_ref[rows] = v[part]
            keys = k[part].astype(F32)
            phi = jnp.where(row_ids(R, base + off) < s[VALID], phi_of(keys, exp_low(keys)), 0.0)
            sums = sums + jnp.sum(phi, axis=0, keepdims=True)
        c_ref[...] = sums

    rows, scratch = staged(block)
    cols = pl.BlockSpec((D, n), lambda c, s: (0, c))
    out = pl.BlockSpec((2 * R, n), lambda c, s: (chip_block(s, j, chips), c))
    o = shape((T, E), BF)
    extra = [pl.BlockSpec(memory_space=pl.ANY)] * 3 if prev else []
    return call(
        kernel,
        (o, o, o, shape((1, E), F32)),
        (E // n,),
        rows + [cols, cols, cols] + extra,
        [out, out, out, pl.BlockSpec((1, n), lambda c, s: (0, c))],
        (12 * R * D * E, 4 * R * D + 6 * D * E + 12 * R * E),
        scratch=[scratch],
        alias={8: 0, 9: 1, 10: 2} if prev else None,
    )(sc, *block, wq, wk, wv, *(prev or ()))


def grad_inner_call(sc, block, wd):
    R, D = 2 * block[0].shape[0], block[0].shape[1]
    F = wd.shape[0]
    n = min(512, F)

    def kernel(s, *refs):
        w_ref, o_ref, x_ref = refs[4:]
        stage(refs[:4], x_ref)
        o_ref[...] = dot_nt(x_ref[...], w_ref[...]).astype(BF)

    rows, scratch = staged(block)
    return call(
        kernel,
        shape((2 * R, F), BF),
        (F // n,),
        rows + [pl.BlockSpec((n, D), lambda c, s: (c, 0))],
        pl.BlockSpec((2 * R, n), lambda c, s: (0, c)),
        (4 * R * D * F, 4 * R * D + 2 * D * F + 4 * R * F),
        scratch=[scratch],
    )(sc, *block, wd)


def ffn_a_call(sc, block, wg, wu, gi):
    R, D = 2 * block[0].shape[0], block[0].shape[1]
    F = wg.shape[1]
    n = min(512, F)

    def kernel(s, *refs):
        wg_ref, wu_ref, gi_ref, inner_ref, gg_ref, gu_ref, x_ref = refs[4:]
        stage(refs[:4], x_ref)
        for i in range(2):
            rows = slice(i * R, (i + 1) * R)
            g = dot(x_ref[rows], wg_ref[...])
            u = dot(x_ref[rows], wu_ref[...])
            sig = 0.5 * jnp.tanh(0.5 * g) + 0.5
            silu = g * sig
            inner_ref[rows] = (silu * u).astype(BF)
            gi_rows = gi_ref[rows].astype(F32)
            gu_ref[rows] = (gi_rows * silu).astype(BF)
            gg_ref[rows] = (gi_rows * u * (sig + silu * (1.0 - sig))).astype(BF)

    o = shape((2 * R, F), BF)
    rows, scratch = staged(block)
    cols = pl.BlockSpec((D, n), lambda c, s: (0, c))
    out = pl.BlockSpec((2 * R, n), lambda c, s: (0, c))
    return call(
        kernel,
        (o, o, o),
        (F // n,),
        rows + [cols, cols, out],
        [out, out, out],
        (8 * R * D * F, 4 * R * D + 4 * D * F + 16 * R * F),
        scratch=[scratch],
    )(sc, *block, wg, wu, gi)


def halves_out(R, D, n):
    H = R // 2
    return (shape((H, D), BF),) * 4, [pl.BlockSpec((H, n), lambda c, s: (0, c))] * 4


def ffn_b_call(sc, gg, gu, wg, wu):
    R2, F = gg.shape
    R = R2 // 2
    D = wg.shape[0]
    n = min(512, D)

    def kernel(s, gg_ref, gu_ref, wg_ref, wu_ref, *outs):
        put_rows(outs, dot_nt(gg_ref[...], wg_ref[...]) + dot_nt(gu_ref[...], wu_ref[...]))

    rows = pl.BlockSpec((R2, F), lambda c, s: (0, 0))
    cols = pl.BlockSpec((n, F), lambda c, s: (c, 0))
    shapes, specs = halves_out(R, D, n)
    return call(
        kernel,
        shapes,
        (D // n,),
        [rows, rows, cols, cols],
        specs,
        (8 * R * D * F, 8 * R * F + 4 * D * F + 4 * R * D),
    )(sc, gg, gu, wg, wu)


def down_call(sc, inner, wd):
    R2, F = inner.shape
    R = R2 // 2
    D = wd.shape[1]
    n = min(512, D)

    def kernel(s, x_ref, w_ref, *outs):
        put_rows(outs, dot(x_ref[...], w_ref[...]))

    shapes, specs = halves_out(R, D, n)
    return call(
        kernel,
        shapes,
        (D // n,),
        [pl.BlockSpec((R2, F), lambda c, s: (0, 0)), pl.BlockSpec((F, n), lambda c, s: (0, c))],
        specs,
        (4 * R * D * F, 4 * R * F + 2 * D * F + 4 * R * D),
    )(sc, inner, wd)


def wgrad_call(sc, blocks, gs, ndp, pieces):
    xs = [x for block in blocks for x in block]
    H, D = xs[0].shape
    nx = len(xs)
    C = D // ndp
    nb = len(gs[0])
    widths = [parts[0].shape[1] for parts in gs]
    T = H * nx
    rb = T // nb
    N = sum(widths)
    flat = [g for parts in gs for g in parts]
    far = ndp // 2 if pieces else 0
    sizes = [far // max(pieces, 1)] * pieces + [ndp - far]
    begins = [p * sizes[0] for p in range(len(sizes))]

    def kernel(s, *refs):
        x_refs, g_refs, o_refs, xt = refs[:nx], refs[nx : nx + len(flat)], refs[nx + len(flat) : -1], refs[-1]
        j = pl.program_id(0)
        for p in range(nx):
            xt[:, p * H : (p + 1) * H] = x_refs[p][...].T
        at = 0
        for w, width in enumerate(widths):
            acc = None
            for b in range(nb):
                term = dot(xt[:, b * rb : (b + 1) * rb], g_refs[w * nb + b][...])
                acc = term if acc is None else acc + term
            cols = slice(at, at + width)
            at += width
            low = acc.astype(BF)
            for o_ref, begin, size in zip(o_refs, begins, sizes):

                @pl.when((j >= begin) & (j < begin + size))
                def _():
                    o_ref[0, :, cols] = low

    def spec(begin, size):
        return pl.BlockSpec((1, C, N), lambda j, s: (jnp.clip(j - begin, 0, size - 1), 0, 0))

    order = (lambda j, s: (0, s[ORDER + j])) if pieces else (lambda j, s: (0, j))
    return call(
        kernel,
        tuple(shape((size, C, N), BF) for size in sizes),
        (ndp,),
        [pl.BlockSpec((H, C), order)] * nx + [whole(g.shape) for g in flat],
        [spec(begin, size) for begin, size in zip(begins, sizes)],
        (2 * T * D * N, 2 * T * (D + N) + 2 * D * N),
        scratch=[pltpu.VMEM((C, T), BF)],
    )(sc, *xs, *flat)


def attn_fwd_call(sc, q, k, v, h0, hh):
    T = q.shape[0]
    E = hh * HEAD
    B = min(512, T)
    nb = T // B
    c = HEAD**-0.5 * LOG2E

    def kernel(s, q_ref, k_ref, v_ref, o_ref, lse_ref):
        valid = s[VALID]
        for i in range(nb):
            qb = q_ref[i * B : (i + 1) * B]
            parts = []
            for j in range(i + 1):
                x = dot_nt(k_ref[j * B : (j + 1) * B], qb)
                if j == i:
                    u = lax.broadcasted_iota(jnp.int32, (B, B), 0)
                    t = lax.broadcasted_iota(jnp.int32, (B, B), 1)
                    x = jnp.where(u <= t, x, NEG)
                if (j + 1) * B > T // 2:
                    x = jnp.where(row_ids(B, j * B) < valid, x, NEG)
                parts.append(x)
            top = jnp.max(parts[0], axis=0, keepdims=True)
            for x in parts[1:]:
                top = jnp.maximum(top, jnp.max(x, axis=0, keepdims=True))
            top = top * c
            total = jnp.zeros((1, B), F32)
            acc = jnp.zeros((HEAD, B), F32)
            for j, x in enumerate(parts):
                p = jnp.exp2(x * c - top)
                total = total + jnp.sum(p, axis=0, keepdims=True)
                acc = acc + dot_tn(v_ref[j * B : (j + 1) * B], p.astype(BF))
            o_ref[i * B : (i + 1) * B] = (acc * (1.0 / total)).T
            lse_ref[0, :, i * B : (i + 1) * B] = top + jnp.log2(total)

    head = pl.BlockSpec((T, HEAD), lambda h, s: (0, h0 + h))
    out = pl.BlockSpec((T, HEAD), lambda h, s: (0, h))
    return call(
        kernel,
        (shape((T, E), F32), shape((hh, 1, T), F32)),
        (hh,),
        [head, head, head],
        [out, pl.BlockSpec((1, 1, T), lambda h, s: (h, 0, 0))],
        (6 * T * T * E, 10 * T * E),
    )(sc, q, k, v)


def attn_bwd_call(sc, q, k, v, do, attended, h0, part):
    lo, lse = attended
    nh = 1
    T = q.shape[0]
    B = min(512, T)
    nb = T // B
    scale = HEAD**-0.5
    c = scale * LOG2E

    def kernel(s, q_ref, k_ref, v_ref, do_ref, lo_ref, lse_ref, dq_ref, dk_ref, dv_ref, delta):
        valid = s[VALID]
        ones = jnp.ones((8, HEAD), F32)
        for i in range(nb):
            rows = slice(i * B, (i + 1) * B)
            prod = do_ref[rows].astype(F32) * lo_ref[rows]
            delta[:, rows] = lax.dot_general(
                ones,
                prod,
                (((1,), (1,)), ((), ())),
                precision=lax.Precision.HIGHEST,
                preferred_element_type=F32,
            )
        dq_ref[...] = jnp.zeros_like(dq_ref)
        for j in range(nb):
            kb = k_ref[j * B : (j + 1) * B]
            vb = v_ref[j * B : (j + 1) * B]
            dk = jnp.zeros((B, HEAD), F32)
            dv = jnp.zeros((B, HEAD), F32)
            for i in range(j, nb):
                rows = slice(i * B, (i + 1) * B)
                qb = q_ref[rows]
                dob = do_ref[rows]
                p = jnp.exp2(dot_nt(kb, qb) * c - lse_ref[0, :, rows])
                if i == j:
                    u = lax.broadcasted_iota(jnp.int32, (B, B), 0)
                    t = lax.broadcasted_iota(jnp.int32, (B, B), 1)
                    p = jnp.where(u <= t, p, 0.0)
                if (j + 1) * B > T // 2:
                    p = jnp.where(row_ids(B, j * B) < valid, p, 0.0)
                ds = (p * (dot_nt(vb, dob) - delta[0:1, rows])).astype(BF)
                dv = dv + dot(p.astype(BF), dob)
                dk = dk + dot(ds, qb)
                dq_ref[rows] += dot_tn(ds, kb)
            dk_ref[j * B : (j + 1) * B] = dk * scale
            dv_ref[j * B : (j + 1) * B] = dv
        dq_ref[...] *= scale

    o = shape((T, nh * HEAD), F32)
    head = pl.BlockSpec((T, HEAD), lambda h, s: (0, h0 + h))
    out = pl.BlockSpec((T, HEAD), lambda h, s: (0, h))
    return call(
        kernel,
        (o, o, o),
        (nh,),
        [head] * 4
        + [pl.BlockSpec((T, HEAD), lambda h, s: (0, part)), pl.BlockSpec((1, 1, T), lambda h, s: (part, 0, 0))],
        [out, out, out],
        (12 * T * T * HEAD * nh, 26 * T * HEAD * nh),
        scratch=[pltpu.VMEM((8, T), F32)],
    )(sc, q, k, v, do, lo, lse)


def maps_call(sc, k, v, gathered):
    T, E = k.shape
    hh = E // HEAD
    ndp = gathered.shape[0]

    def kernel(s, k_ref, v_ref, g_ref, maps_ref, norm_ref):
        h = pl.program_id(0)
        norm = jnp.zeros((1, HEAD), F32)
        for a in range(ndp - 1):
            after = (norm + g_ref[shared_at(s, a, ndp), pl.ds(h, 1)]) * g_ref[shared_at(s, a + 1, ndp), hh : hh + 1]
            norm = jnp.where(a < s[PLACE], after, norm)
        norm_ref[0] = norm
        k = k_ref[...].astype(F32)
        phi = jnp.where(row_ids(T, 0) < s[VALID], phi_of(k, exp_low(k)), 0.0)
        den = jnp.maximum(jnp.sum(phi * norm, axis=1, keepdims=True), 1.0)
        low = phi.astype(BF)
        maps_ref[0, 0] = dot_tn((phi * (1.0 / den)).astype(BF), low).astype(BF)
        maps_ref[1, 0] = dot_tn(low, v_ref[...]).astype(BF)

    head = pl.BlockSpec((T, HEAD), lambda h, s: (0, h))
    return call(
        kernel,
        (shape((2, hh, HEAD, HEAD), BF), shape((hh, 1, HEAD), F32)),
        (hh,),
        [head, head, whole(gathered.shape)],
        [
            pl.BlockSpec((2, 1, HEAD, HEAD), lambda h, s: (0, h, 0, 0)),
            pl.BlockSpec((1, 1, HEAD), lambda h, s: (h, 0, 0)),
        ],
        (4 * T * E * HEAD, 4 * T * E),
    )(sc, k, v, gathered)


def times_state(g, state):
    high = state.astype(BF)
    return dot(g, high) + dot(g, (state - high.astype(F32)).astype(BF))


def chain_call(sc, gathered, maps):
    ndp, _, hh = maps.shape[:3]

    def kernel(s, g_ref, maps_ref, m_ref):
        state = [jnp.zeros((HEAD, HEAD), F32) for _ in range(hh)]
        for a in range(ndp - 1):
            keep = g_ref[shared_at(s, a + 1, ndp), hh : hh + 1]
            before = a < s[PLACE]
            for h in range(hh):
                after = state[h] - times_state(maps_ref[a, 0, h], state[h])
                after = (after + maps_ref[a, 1, h].astype(F32)) * keep
                state[h] = jnp.where(before, after, state[h])
        for h in range(hh):
            m_ref[h] = state[h]

    return call(
        kernel,
        shape((hh, HEAD, HEAD), F32),
        (1,),
        [whole(gathered.shape), whole(maps.shape)],
        whole((hh, HEAD, HEAD)),
        (4e8, 2 * maps.size),
    )(sc, gathered, maps)


def mixout_call(sc, j, chips, q, locals_, memory, norm, mix, wo):
    T, E = q.shape
    hh = E // HEAD
    D = wo.shape[1]
    R = T // chips // 2
    n = min(512, D)
    groups = len(locals_)
    per = hh // groups

    def kernel(s, q_ref, *rest):
        l_refs = rest[:groups]
        m_ref, n_ref, mix_ref, w_ref, *outs, mixed_ref, diff_ref = rest[groups:]

        @pl.when(pl.program_id(0) == 0)
        def _():
            for i in range(2):
                off = pl.multiple_of((s[CORE] if i == 0 else 1 - s[CORE]) * R, R)
                for h in range(hh):
                    cols = slice(h * HEAD, (h + 1) * HEAD)
                    qv = q_ref[pl.ds(off, R), cols].astype(F32)
                    phi = phi_of(qv, exp_low(qv))
                    den = jnp.maximum(jnp.sum(phi * n_ref[h], axis=1, keepdims=True), 1.0)
                    read = dot(phi.astype(BF), m_ref[h].astype(BF)) * (1.0 / den)
                    local = l_refs[h // per][pl.ds(off, R), h % per * HEAD : (h % per + 1) * HEAD]
                    diff = read - local
                    mixed = local + mix_ref[h] * diff
                    diff_ref[i * R : (i + 1) * R, cols] = diff.astype(BF)
                    mixed_ref[i * R : (i + 1) * R, cols] = mixed.astype(BF)

        put_rows(outs, dot(mixed_ref[...], w_ref[...]))

    rows = pl.BlockSpec((2 * R, E), lambda c, s: (chip_block(s, j, chips), 0))
    shapes, specs = halves_out(R, D, n)
    rel = pl.BlockSpec((2 * R, E), lambda c, s: (0, 0))
    return call(
        kernel,
        shapes + (shape((2 * R, E), BF), shape((2 * R, E), BF)),
        (D // n,),
        [rows]
        + [pl.BlockSpec((2 * R, per * HEAD), lambda c, s: (chip_block(s, j, chips), 0))] * groups
        + [whole(memory.shape), whole(norm.shape), whole(mix.shape), pl.BlockSpec((E, n), lambda c, s: (0, c))],
        specs + [rel, rel],
        (4 * R * E * D + 8 * R * E * HEAD, 20 * R * E + 2 * E * D + 4 * R * D),
    )(sc, q, *locals_, memory, norm, mix, wo)


def gradmix_call(sc, j, chips, block, wo, diff, q, norm, mix, prev):
    R, D = 2 * block[0].shape[0], block[0].shape[1]
    E = wo.shape[0]
    hh = E // HEAD
    T = 2 * R * chips
    n = min(256, E)
    per = n // HEAD

    def kernel(s, *refs):
        w_ref, diff_ref, q_ref, n_ref, mix_ref = refs[4:9]
        do_ref, gm_ref, cot_ref, b_ref, x_ref = refs[-5:]
        stage(refs[:4], x_ref)
        sums = jnp.zeros((1, n), F32)
        cots = [jnp.zeros((HEAD, HEAD), F32) for _ in range(per)]
        for i in range(2):
            off = pl.multiple_of((s[CORE] if i == 0 else 1 - s[CORE]) * R, R)
            grad = dot_nt(x_ref[i * R : (i + 1) * R], w_ref[...])
            sums = sums + jnp.sum(grad * diff_ref[i * R : (i + 1) * R].astype(F32), axis=0, keepdims=True)
            for h in range(per):
                cols = slice(h * HEAD, (h + 1) * HEAD)
                part = grad[:, cols]
                grad_read = part * mix_ref[h]
                do_ref[pl.ds(off, R), cols] = (part - grad_read).astype(BF)
                gm_ref[pl.ds(off, R), cols] = grad_read.astype(BF)
                qv = q_ref[pl.ds(off, R), cols].astype(F32)
                phi = phi_of(qv, exp_low(qv))
                den = jnp.maximum(jnp.sum(phi * n_ref[h], axis=1, keepdims=True), 1.0)
                cots[h] = cots[h] + dot_tn(phi.astype(BF), (grad_read * (1.0 / den)).astype(BF))
        for h in range(per):
            cot_ref[h] = cots[h]
        b_ref[...] = sums

    rows, scratch = staged(block)
    place = pl.BlockSpec((2 * R, n), lambda c, s: (chip_block(s, j, chips), c))
    per_head = pl.BlockSpec((per, 1, HEAD), lambda c, s: (c, 0, 0))
    o = shape((T, E), BF)
    extra = [pl.BlockSpec(memory_space=pl.ANY)] * 2 if prev else []
    return call(
        kernel,
        (o, o, shape((hh, HEAD, HEAD), F32), shape((1, E), F32)),
        (E // n,),
        rows
        + [pl.BlockSpec((n, D), lambda c, s: (c, 0)), pl.BlockSpec((2 * R, n), lambda c, s: (0, c)), place, per_head, per_head]
        + extra,
        [place, place, pl.BlockSpec((per, HEAD, HEAD), lambda c, s: (c, 0, 0)), pl.BlockSpec((1, n), lambda c, s: (0, c))],
        (4 * R * E * D + 4 * R * E * HEAD, 4 * R * D + 2 * E * D + 16 * R * E),
        scratch=[scratch],
        alias={10: 0, 11: 1} if prev else None,
    )(sc, *block, wo, diff, q, norm, mix, *(prev or ()))


def memory_rows(q, k, grad_read, live, memory, norm, cot):
    low_q = exp_low(q)
    low_k = exp_low(k)
    phi_q = phi_of(q, low_q)
    phi_k = jnp.where(live, phi_of(k, low_k), 0.0)
    raw_q = jnp.sum(phi_q * norm, axis=1, keepdims=True)
    raw_k = jnp.sum(phi_k * norm, axis=1, keepdims=True)
    inv_q = 1.0 / jnp.maximum(raw_q, 1.0)
    inv_k = 1.0 / jnp.maximum(raw_k, 1.0)
    read = dot(phi_q.astype(BF), memory)
    recalled = dot(phi_k.astype(BF), memory) * inv_k
    pushed = dot(phi_k.astype(BF), cot)
    scaled = grad_read * inv_q
    w_q = jnp.where(raw_q > 1.0, -jnp.sum(scaled * read, axis=1, keepdims=True) * inv_q, 0.0)
    w_k = jnp.where(raw_k > 1.0, jnp.sum(pushed * recalled, axis=1, keepdims=True) * inv_k, 0.0)
    return low_q, low_k, phi_q, phi_k, inv_k, recalled, pushed, scaled, w_q, w_k


def memory_cot_call(sc, gathered, maps, cots, q, k, grad_read, memory, norm):
    T, E = q.shape
    hh = E // HEAD
    ndp = maps.shape[0]
    B = min(512, T)

    def kernel(s, g_ref, maps_ref, cots_ref, q_ref, k_ref, gm_ref, m_ref, n_ref, x_ref, nb_ref):
        cot = jnp.zeros((HEAD, HEAD), F32)
        for a in range(ndp - 1, 0, -1):
            before = cot - times_state(maps_ref[a, 0, 0], cot) + cots_ref[shared_at(s, a, ndp), 0].astype(F32)
            cot = jnp.where(a > s[PLACE], before * g_ref[shared_at(s, a, ndp), hh : hh + 1], cot)
        x_ref[0] = cot
        cot = cot.astype(BF)
        memory = m_ref[0].astype(BF)
        sums = jnp.zeros((1, HEAD), F32)
        for i in range(T // B):
            rows = slice(i * B, (i + 1) * B)
            live = row_ids(B, i * B) < s[VALID]
            terms = memory_rows(
                q_ref[rows].astype(F32), k_ref[rows].astype(F32), gm_ref[rows].astype(F32), live, memory, n_ref[0], cot
            )
            sums = sums + jnp.sum(terms[2] * terms[8] + terms[3] * terms[9], axis=0, keepdims=True)
        nb_ref[0] = sums

    head = pl.BlockSpec((T, HEAD), lambda h, s: (0, h))
    square = pl.BlockSpec((1, HEAD, HEAD), lambda h, s: (h, 0, 0))
    row = pl.BlockSpec((1, 1, HEAD), lambda h, s: (h, 0, 0))
    return call(
        kernel,
        (shape((hh, HEAD, HEAD), F32), shape((hh, 1, HEAD), F32)),
        (hh,),
        [
            whole(gathered.shape),
            pl.BlockSpec((ndp, 1, 1, HEAD, HEAD), lambda h, s: (0, 0, h, 0, 0)),
            pl.BlockSpec((ndp, 1, HEAD, HEAD), lambda h, s: (0, h, 0, 0)),
            head,
            head,
            head,
            square,
            row,
        ],
        [square, row],
        (8 * T * E * HEAD, 6 * T * E),
    )(sc, gathered, maps, cots, q, k, grad_read, memory, norm)


def combine_call(sc, chips, q, k, v, grad_read, local_grads, memory, norm, cot, gathered, norm_parts):
    T, E = q.shape
    hh = E // HEAD
    R = T // chips // 2
    ndp = gathered.shape[0]
    per = local_grads[0][0].shape[1] // HEAD
    groups = len(local_grads)

    def kernel(s, q_ref, k_ref, v_ref, gm_ref, *rest):
        local_refs = rest[: 3 * groups]
        m_ref, n_ref, x_ref, g_ref, nb_ref, gq_ref, gk_ref, gv_ref = rest[3 * groups :]
        begin = piece(pl.program_id(0), s) * R
        live = row_ids(R, begin) < s[VALID]
        for h in range(hh):
            cols = slice(h * HEAD, (h + 1) * HEAD)
            part = slice(h % per * HEAD, (h % per + 1) * HEAD)
            dq, dk, dv = (ref[:, part] for ref in local_refs[3 * (h // per) : 3 * (h // per) + 3])
            norm_cot = jnp.zeros((1, HEAD), F32)
            for a in range(ndp - 1, 0, -1):
                other = shared_at(s, a, ndp)
                before = (norm_cot + nb_ref[other, h : h + 1]) * g_ref[other, hh : hh + 1]
                norm_cot = jnp.where(a > s[PLACE], before, norm_cot)
            memory = m_ref[h].astype(BF)
            cot = x_ref[h].astype(BF)
            norm = n_ref[h]
            low_q, low_k, _, _, inv_k, recalled, pushed, scaled, w_q, w_k = memory_rows(
                q_ref[:, cols].astype(F32), k_ref[:, cols].astype(F32), gm_ref[:, cols].astype(F32), live, memory, norm, cot
            )
            grad_phi_q = dot_nt(scaled.astype(BF), memory) + w_q * norm
            grad_phi_k = (
                dot_nt((v_ref[:, cols].astype(F32) - recalled).astype(BF), cot)
                - dot_nt((pushed * inv_k).astype(BF), memory)
                + w_k * norm
                + norm_cot
            )
            gq_ref[:, cols] = (dq + grad_phi_q * low_q).astype(BF)
            gk_ref[:, cols] = (dk + jnp.where(live, grad_phi_k * low_k, 0.0)).astype(BF)
            gv_ref[:, cols] = (dv + pushed).astype(BF)

    def piece(p, s):
        core = lax.rem(s[CORE] + p, 2)
        return chip_block(s, p // 2, chips) * 2 + core

    rows = pl.BlockSpec((R, E), lambda p, s: (piece(p, s), 0))
    part_rows = pl.BlockSpec((R, per * HEAD), lambda p, s: (piece(p, s), 0))
    out = pl.BlockSpec((R, E), lambda p, s: (p, 0))
    o = shape((T, E), BF)
    return call(
        kernel,
        (o, o, o),
        (2 * chips,),
        [rows] * 4 + [part_rows] * (3 * groups) + [whole(x.shape) for x in (memory, norm, cot, gathered, norm_parts)],
        [out, out, out],
        (14 * T * E * HEAD, 26 * T * E),
    )(sc, q, k, v, grad_read, *[x for group in local_grads for x in group], memory, norm, cot, gathered, norm_parts)


def grad_normed_call(sc, j, gq, gk, gv, wq, wk, wv, block, chips):
    T, E = gq.shape
    R = T // chips // 2
    D = wq.shape[0]
    n = min(512, D)

    def kernel(s, gq_ref, gk_ref, gv_ref, wq_ref, wk_ref, wv_ref, *rest):
        grad = dot_nt(gq_ref[...], wq_ref[...]) + dot_nt(gk_ref[...], wk_ref[...]) + dot_nt(gv_ref[...], wv_ref[...])
        put_rows(rest[4:8], grad)
        sums, at = 0.0, 0
        for ref in rest[:4]:
            part = grad[at : at + ref.shape[0]] * ref[...].astype(F32)
            sums = sums + jnp.sum(part, axis=0, keepdims=True)
            at += ref.shape[0]
        rest[8][...] = sums

    rows = pl.BlockSpec((2 * R, E), lambda c, s: (j, 0))
    cols = pl.BlockSpec((n, E), lambda c, s: (c, 0))
    shapes, specs = halves_out(R, D, n)
    return call(
        kernel,
        shapes + (shape((1, D), F32),),
        (D // n,),
        [rows, rows, rows, cols, cols, cols] + specs,
        specs + [pl.BlockSpec((1, n), lambda c, s: (0, c))],
        (12 * R * D * E, 12 * R * E + 6 * D * E + 4 * R * D),
    )(sc, gq, gk, gv, wq, wk, wv, *block)


def swap_core(pair):
    count = lax.axis_size("tensor")
    return tuple(lax.ppermute(x, "tensor", [(i, i ^ 1) for i in range(count)]) for x in pair)


def shift_chip(pair, j):
    count = lax.axis_size("tensor")
    return tuple(lax.ppermute(x, "tensor", [(i, (i + 2 * j) % count) for i in range(count)]) for x in pair)


def with_swapped(pair):
    return tuple(pair) + swap_core(pair)


def chunk_order(me, ndp):
    parity = me % 2
    order = [2 * i + (1 - parity) for i in range(ndp // 2)] + [2 * i + parity for i in range(ndp // 2)]
    return jnp.stack(order)


def exchange_x(x):
    return lax.ppermute(x, "dp", [(i, i ^ 1) for i in range(lax.axis_size("dp"))])


def sum_z(x):
    ndp = lax.axis_size("dp")
    groups = [list(range(0, ndp, 2)), list(range(1, ndp, 2))]
    return lax.psum_scatter(x, "dp", scatter_dimension=0, axis_index_groups=groups, tiled=True)


def finish_x(both, parity):
    C = both.shape[0] // 2
    got = exchange_x(lax.dynamic_slice_in_dim(both, (1 - parity) * C, C, 0))
    return got.astype(F32) + lax.dynamic_slice_in_dim(both, parity * C, C, 0).astype(F32)


def share_steps(x):
    count = lax.axis_size("dp")
    steps = [1 << bit for bit in range(1, count.bit_length() - 1)] + [1]
    x = x[None]
    for step in steps:
        x = jnp.concatenate([x, lax.ppermute(x, "dp", [(i, i ^ step) for i in range(count)])])
        yield x


def shared_at(s, a, count):
    apart = a ^ s[PLACE]
    return (apart >> 1) + (apart & 1) * (count // 2)


def share_over_dp(x):
    return list(share_steps(x))[-1]


def sum_everywhere(x):
    for axis in ("tensor", "dp"):
        count, step = lax.axis_size(axis), 1
        while step < count:
            x = x + lax.ppermute(x, axis, [(i, i ^ step) for i in range(count)])
            step *= 2
    return x


def body(
    tokens,
    gain1,
    w_query,
    w_key,
    w_value,
    w_out,
    gate_bias,
    gain2,
    w_gate,
    w_up,
    w_down,
    seg_starts,
    seg_valid,
    cotangent,
):
    count = lax.axis_size("tensor")
    ndp = lax.axis_size("dp")
    chips = count // 2
    hh = gate_bias.shape[0]
    E = hh * HEAD
    here = lax.axis_index("tensor")
    place = lax.axis_index("dp")
    sc = jnp.concatenate(
        [
            jnp.stack([here // 2, here % 2, place]).astype(jnp.int32),
            seg_valid.astype(jnp.int32),
            chunk_order(place, ndp).astype(jnp.int32),
        ]
    )
    keep = (1 - seg_starts[0]).astype(F32)
    sig_bias = jax.nn.sigmoid(gate_bias)
    mix = jnp.broadcast_to(sig_bias[:, None, None], (hh, 1, HEAD))

    ORDERED.clear()
    per = max(1, hh // 2)

    gain1 = gain1[None]
    gain2 = gain2[None]
    chip_range = range(1, chips)
    parity = place % 2
    R = tokens.shape[0]
    four = min(4, ndp // 2)

    def norm1_kernel(x_ref, g_ref, o_ref):
        o_ref[...] = (unit_rows(x_ref[...].astype(F32))[0] * g_ref[...]).astype(BF)

    normed1 = rows_call(norm1_kernel, [[BF]], sc, [tokens], [gain1])[0]
    rows1 = [with_swapped(normed1)]
    far1 = [shift_chip(normed1, -j) for j in chip_range]
    own_cot = (cotangent[: R // 2], cotangent[R // 2 :])
    cot_rows = [with_swapped(own_cot)]
    *qkv, sums = qkv_call(sc, 0, chips, rows1[0], w_query, w_key, w_value, None)
    *far1, own_cot = hold_pairs(sc, far1 + [own_cot])
    far_cot = [shift_chip(own_cot, -j) for j in chip_range]
    for j in chip_range:
        rows1.append(with_swapped(far1[j - 1]))
        *qkv, column_sums = qkv_call(sc, j, chips, rows1[j], w_query, w_key, w_value, qkv)
        sums = sums + column_sums
    q, k, v = qkv

    own = jnp.concatenate([sums.reshape(hh, HEAD), jnp.full((8 - hh, HEAD), keep, F32)])
    gathered = share_over_dp(own)
    maps, norm = maps_call(sc, k, v, gathered)
    all_maps = lax.all_gather(maps, "dp")
    attended = [attn_fwd_call(sc, q, k, v, h, per) for h in range(0, hh, per)]
    far_cot = hold_pairs(sc, far_cot)
    cot_rows += [with_swapped(pair) for pair in far_cot]
    grad_inner = [grad_inner_call(sc, block, w_down) for block in cot_rows]
    memory = chain_call(sc, gathered, all_maps)

    mixed, diff = [None] * chips, [None] * chips

    def mixout(j):
        *block, mixed[j], diff[j] = mixout_call(sc, j, chips, q, [one[0] for one in attended], memory, norm, mix, w_out)
        return block

    def scatter(make):
        blocks = [make(j) for j in chip_range] + [make(0)]
        got = []
        for j in chip_range:
            block = blocks[j - 1]
            sums = add_rows(sc, [tuple(block[:2]), swap_core(block[2:])], True)
            got.append(shift_chip(sums, j))
        block = blocks[-1]
        return [tuple(block[:2]), swap_core(block[2:]), *got]

    hidden, normed2 = norm_call(sc, [tokens, *scatter(mixout)], gain2)
    rows2 = [with_swapped(normed2)]
    far2 = [shift_chip(normed2, -j) for j in chip_range]
    ffn = [ffn_a_call(sc, rows2[0], w_gate, w_up, grad_inner[0])]
    far2 = hold_pairs(sc, far2)
    for j in chip_range:
        rows2.append(with_swapped(far2[j - 1]))
        ffn.append(ffn_a_call(sc, rows2[j], w_gate, w_up, grad_inner[j]))
    inner, grad_gate, grad_up = zip(*ffn)

    (w_up_parts,) = wgrad_call(sc, rows2, [grad_up], ndp, 0)
    both_up = sum_z(w_up_parts.reshape((-1, w_up_parts.shape[2])))
    back = scatter(lambda j: ffn_b_call(sc, grad_gate[j], grad_up[j], w_gate, w_up))
    far_gate, near_gate = wgrad_call(sc, rows2, [grad_gate], ndp, 1)
    far_gate = exchange_x(far_gate)
    far_down, near_down = wgrad_call(sc, cot_rows, [inner], ndp, 1)
    far_down = exchange_x(far_down)
    grad_hidden, grad_low, gain2_part = norm_back_call(sc, cotangent, hidden, back, gain2, True)
    grad_rows = [with_swapped(grad_low)]
    far_grad = [shift_chip(grad_low, -j) for j in chip_range]
    down_far = [down_call(sc, inner[j], w_down) for j in chip_range]
    *grads, cot_part, bias_part = gradmix_call(sc, 0, chips, grad_rows[0], w_out, diff[0], q, norm, mix, None)
    down_near = down_call(sc, inner[0], w_down)
    far_grad = hold_pairs(sc, far_grad)
    pair_gate = pair_call(sc, [(far_gate, near_gate)])
    sum_gate = sum_z(pair_gate)
    require(both_up)
    sum_up = finish_x(both_up, parity)
    for j in chip_range:
        grad_rows.append(with_swapped(far_grad[j - 1]))
        *grads, cot_j, bias_j = gradmix_call(sc, j, chips, grad_rows[j], w_out, diff[j], q, norm, mix, grads)
        cot_part = cot_part + cot_j
        bias_part = bias_part + bias_j
    down_blocks = iter(down_far + [down_near])
    down = scatter(lambda j: next(down_blocks))
    grad_local, grad_read = grads

    local_grads = []
    steps = share_steps(cot_part.astype(BF))
    all_cots = None
    for h in range(hh):
        local_grads.append(attn_bwd_call(sc, q, k, v, grad_local, attended[h // per], h, h % per))
        if h in (0, max(2, hh - 2)):
            all_cots = next(steps)
            require(all_cots)
    for all_cots in steps:
        pass
    far_out, near_out = wgrad_call(sc, grad_rows, [mixed], ndp, 1)
    far_out = exchange_x(far_out)
    pair_down = pair_call(sc, [(far_down, near_down)])
    sum_down = sum_z(pair_down)
    memory_cot, norm_part = memory_cot_call(sc, gathered, all_maps, all_cots, q, k, grad_read, memory, norm)
    norm_parts = share_over_dp(jnp.concatenate([norm_part.reshape(hh, HEAD), jnp.zeros((8 - hh, HEAD), F32)]))
    require(sum_gate)
    gq, gk, gv = combine_call(
        sc, chips, q, k, v, grad_read, local_grads, memory, norm, memory_cot, gathered, norm_parts
    )
    gain1_sums = []

    def back_rows(j):
        *block, sums = grad_normed_call(sc, j, gq, gk, gv, w_query, w_key, w_value, rows1[j], chips)
        gain1_sums.append(sums)
        return block

    parts1 = {}

    def make1(name, grad):
        far, near = wgrad_call(sc, rows1, [[grad]], ndp, 1)
        parts1[name] = exchange_x(far), near

    make1("v", gv)
    make1("k", gk)
    back1 = scatter(back_rows)
    require(sum_up)
    sum_okv = sum_z(pair_call(sc, [(far_out, near_out), parts1["k"], parts1["v"]]))
    make1("q", gq)
    output = add_rows(sc, [hidden, *down], False)
    require(sum_down)
    (grad_tokens,) = norm_back_call(sc, grad_hidden, tokens, back1, gain1, False)
    require(sum_okv)
    sum_okv = sum_okv.astype(F32)
    sum_query = sum_z(pair_call(sc, [parts1["q"]]))
    gain1_part = sum(gain1_sums) / gain1

    bias_here = jnp.sum(bias_part.reshape(hh, HEAD), axis=1) * sig_bias * (1.0 - sig_bias)
    bias_full = lax.dynamic_update_slice(jnp.zeros((HEADS,), F32), bias_here, (here * hh,))
    small = sum_everywhere(jnp.concatenate([gain1_part[0], gain2_part[0], bias_full]))
    D = gain1.shape[1]
    return (
        output,
        grad_tokens,
        small[:D],
        sum_query.astype(F32),
        sum_okv[:, E : 2 * E],
        sum_okv[:, 2 * E :],
        sum_okv[:, :E].T,
        small[2 * D :],
        small[D : 2 * D],
        sum_gate.astype(F32),
        sum_up,
        sum_down.astype(F32).T,
    )


def solution(mesh):
    rows = P(("dp", "tensor"), None)
    return jax.shard_map(
        body,
        mesh=mesh,
        in_specs=(
            rows,
            P(),
            P(None, "tensor"),
            P(None, "tensor"),
            P(None, "tensor"),
            P("tensor", None),
            P("tensor"),
            P(),
            P(None, "tensor"),
            P(None, "tensor"),
            P("tensor", None),
            P("dp"),
            P("dp"),
            rows,
        ),
        out_specs=(
            rows,
            rows,
            P(),
            P("dp", "tensor"),
            P("dp", "tensor"),
            P("dp", "tensor"),
            P("tensor", "dp"),
            P(),
            P(),
            P("dp", "tensor"),
            P("dp", "tensor"),
            P("tensor", "dp"),
        ),
        check_vma=False,
    )
```

```python
import jax
import jax.numpy as jnp
from jax import lax
from jax.experimental import pallas as pl
from jax.experimental.pallas import tpu as pltpu
from jax.sharding import PartitionSpec as P

HEADS = 16
HEAD = 128
EPSILON = 1e-06
BF = jnp.bfloat16
F32 = jnp.float32
LOG2E = 1.4426950408889634
NEG = -1e30
VMEM_BYTES = 56 << 20


def dot(a, b):
    return jnp.dot(a, b, preferred_element_type=F32)


def dot_nt(a, b):
    return lax.dot_general(a, b, (((1,), (1,)), ((), ())), preferred_element_type=F32)


def dot_tn(a, b):
    return lax.dot_general(a, b, (((0,), (0,)), ((), ())), preferred_element_type=F32)


def shape(dims, dtype):
    return jax.ShapeDtypeStruct(dims, dtype)


COST = 20.0
ORDERED = []


def call(kernel, out_shape, grid, in_specs, out_specs, cost, scratch=(), alias=None):
    many = isinstance(out_shape, tuple)
    plain = len(in_specs) + 1
    token = [pl.BlockSpec(memory_space=pl.ANY)] * len(ORDERED)

    def ordered_kernel(*refs):
        kernel(*refs[:plain], *refs[plain + len(token) :])

    made = pl.pallas_call(
        ordered_kernel,
        out_shape=out_shape,
        grid_spec=pltpu.PrefetchScalarGridSpec(
            num_scalar_prefetch=1,
            grid=grid,
            in_specs=list(in_specs) + token,
            out_specs=out_specs,
            scratch_shapes=list(scratch),
        ),
        input_output_aliases=alias or {},
        compiler_params=pltpu.CompilerParams(
            dimension_semantics=("arbitrary",) * len(grid), vmem_limit_bytes=VMEM_BYTES
        ),
        cost_estimate=pl.CostEstimate(
            flops=int(COST * cost[0]), bytes_accessed=int(COST * cost[1]), transcendentals=0
        ),
    )

    def run(*operands):
        out = made(*operands, *ORDERED)
        ORDERED[:] = [out[-1] if many else out]
        return out

    return run


def require(*arrays):
    ORDERED.extend(arrays)


def hold(sc, *arrays):
    n = len(arrays)

    def kernel(*refs):
        del refs

    one = pl.BlockSpec(memory_space=pl.ANY)
    found = call(
        kernel,
        tuple(shape(x.shape, x.dtype) for x in arrays),
        (1,),
        [one] * n,
        [one] * n,
        (1e6, 1e4),
        alias={1 + i: i for i in range(n)},
    )(sc, *arrays)
    ORDERED.clear()
    ORDERED.append(found[0])
    return found


def hold_pairs(sc, pairs):
    found = hold(sc, *[x for pair in pairs for x in pair])
    return [tuple(found[2 * i : 2 * i + 2]) for i in range(len(pairs))]


class Halves:
    def __init__(self, low, high, first):
        self.low, self.high, self.first = low, high, first

    def __getitem__(self, at):
        return jnp.where(self.first, self.low[at], self.high[at])

    def __setitem__(self, at, value):
        @pl.when(self.first)
        def _():
            self.low[at] = value

        @pl.when(jnp.logical_not(self.first))
        def _():
            self.high[at] = value


def rows_call(kernel, outs, sc, rows, shared, sums=0):
    first = rows[0]
    R, D = (2 * first[0].shape[0], first[0].shape[1]) if isinstance(first, tuple) else first.shape
    n = min(128, R // 2)
    half = R // 2 // n
    block = pl.BlockSpec((n, D), lambda i, s: (i, 0))
    low = pl.BlockSpec((n, D), lambda i, s: (jnp.minimum(i, half - 1), 0))
    high = pl.BlockSpec((n, D), lambda i, s: (jnp.maximum(i - half, 0), 0))
    one = pl.BlockSpec((1, D), lambda i, s: (0, 0))
    in_specs, operands, kinds = [], [], []
    for x in rows:
        pair = isinstance(x, tuple)
        kinds.append(pair)
        in_specs += [low, high] if pair else [block]
        operands += list(x) if pair else [x]
    kinds += [False] * len(shared)
    out_specs, out_shapes = [], []
    for x in outs:
        pair = isinstance(x, list)
        kinds.append(pair)
        out_specs += [low, high] if pair else [block]
        out_shapes += [shape((R // 2, D), x[0])] * 2 if pair else [shape((R, D), x)]
    kinds += [False] * sums

    def body_kernel(s, *refs):
        i = pl.program_id(0)

        @pl.when(i == 0)
        def _():
            for ref in refs[len(refs) - sums :] if sums else ():
                ref[...] = jnp.zeros_like(ref)

        views, at = [], 0
        for pair in kinds:
            views.append(Halves(refs[at], refs[at + 1], i < half) if pair else refs[at])
            at += 2 if pair else 1
        kernel(*views)

    found = call(
        body_kernel,
        tuple(out_shapes + [shape((1, D), F32)] * sums),
        (R // n,),
        in_specs + [one] * len(shared),
        out_specs + [one] * sums,
        (10 * R * D, 20 * R * D),
    )(sc, *operands, *shared)
    result, at = [], 0
    for x in outs:
        pair = isinstance(x, list)
        result.append(tuple(found[at : at + 2]) if pair else found[at])
        at += 2 if pair else 1
    return result + list(found[at:])


def add_rows(sc, terms, split):
    def kernel(*refs):
        refs[-1][...] = sum(ref[...].astype(F32) for ref in refs[:-1]).astype(BF)

    return rows_call(kernel, [[BF] if split else BF], sc, terms, [])[0]


def unit_rows(values):
    inverse = lax.rsqrt(jnp.mean(values * values, axis=-1, keepdims=True) + EPSILON)
    return values * inverse, inverse


def norm_call(sc, terms, gain):
    def kernel(*refs):
        gain_ref, sum_ref, out_ref = refs[-3:]
        total = sum(ref[...].astype(F32) for ref in refs[:-3])
        sum_ref[...] = total
        out_ref[...] = (unit_rows(total)[0] * gain_ref[...]).astype(BF)

    return rows_call(kernel, [F32, [BF]], sc, terms, [gain])


def norm_back_call(sc, base, values, terms, gain, low):
    def kernel(base_ref, values_ref, *refs):
        term_refs, gain_ref, outs = refs[: len(terms)], refs[len(terms)], refs[len(terms) + 1 :]
        grad = sum(ref[...].astype(F32) for ref in term_refs)
        unit, inverse = unit_rows(values_ref[...].astype(F32))
        if low:
            outs[-1][...] += jnp.sum(grad * unit, axis=0, keepdims=True)
        scaled = grad * gain_ref[...]
        out = base_ref[...].astype(F32) + inverse * (
            scaled - unit * jnp.mean(scaled * unit, axis=-1, keepdims=True)
        )
        outs[0][...] = out
        if low:
            outs[1][...] = out.astype(BF)

    return rows_call(kernel, [F32, [BF]] if low else [F32], sc, [base, values, *terms], [gain], sums=1 if low else 0)


def pair_call(sc, parts):
    half, C, _ = parts[0][0].shape
    widths = [near.shape[2] for _, near in parts]
    N = sum(widths)

    def kernel(s, *refs):
        at = 0
        for p, width in enumerate(widths):
            total = refs[2 * p][0].astype(F32) + refs[2 * p + 1][0].astype(F32)
            refs[-1][:, at : at + width] = total.astype(BF)
            at += width

    return call(
        kernel,
        shape((half * C, N), BF),
        (half,),
        [pl.BlockSpec((1, C, width), lambda i, s: (i, 0, 0)) for width in widths for _ in range(2)],
        pl.BlockSpec((C, N), lambda i, s: (i, 0)),
        (half * C * N, 6 * half * C * N),
    )(sc, *[x for part in parts for x in part])


def stage(refs, x_ref):
    @pl.when(pl.program_id(0) == 0)
    def _():
        at = 0
        for ref in refs:
            x_ref[at : at + ref.shape[0]] = ref[...]
            at += ref.shape[0]


def staged(block):
    H, D = block[0].shape
    return [pl.BlockSpec((H, D), lambda c, s: (0, 0), pipeline_mode=pl.Buffered(1))] * 4, pltpu.VMEM((4 * H, D), BF)


def put_rows(refs, value):
    at = 0
    for ref in refs:
        ref[...] = value[at : at + ref.shape[0]].astype(BF)
        at += ref.shape[0]


def whole(dims):
    return pl.BlockSpec(dims, lambda *_: (0,) * len(dims), pipeline_mode=pl.Buffered(1))


def exp_low(values):
    return jnp.exp(jnp.minimum(values, 0.0))


def phi_of(values, low):
    return jnp.where(values > 0, values + 1.0, low)


def row_ids(count, begin):
    return begin + lax.broadcasted_iota(jnp.int32, (count, 1), 0)


CHIP, CORE, PLACE, VALID, ORDER = 0, 1, 2, 3, 4


def chip_block(s, j, chips):
    return lax.rem(s[CHIP] + j, chips)


def qkv_call(sc, j, chips, block, wq, wk, wv, prev):
    R, D = 2 * block[0].shape[0], block[0].shape[1]
    E = wq.shape[1]
    T = 2 * R * chips
    n = min(256, E)

    def kernel(s, *refs):
        wq_ref, wk_ref, wv_ref = refs[4:7]
        q_ref, k_ref, v_ref, c_ref, x_ref = refs[-5:]
        stage(refs[:4], x_ref)
        base = chip_block(s, j, chips) * 2 * R
        sums = jnp.zeros((1, n), F32)
        x = x_ref[...]
        q, k, v = (dot(x, ref[...]).astype(BF) for ref in (wq_ref, wk_ref, wv_ref))
        for i in range(2):
            off = pl.multiple_of((s[CORE] if i == 0 else 1 - s[CORE]) * R, R)
            rows, part = pl.ds(off, R), slice(i * R, (i + 1) * R)
            q_ref[rows] = q[part]
            k_ref[rows] = k[part]
            v_ref[rows] = v[part]
            keys = k[part].astype(F32)
            phi = jnp.where(row_ids(R, base + off) < s[VALID], phi_of(keys, exp_low(keys)), 0.0)
            sums = sums + jnp.sum(phi, axis=0, keepdims=True)
        c_ref[...] = sums

    rows, scratch = staged(block)
    cols = pl.BlockSpec((D, n), lambda c, s: (0, c))
    out = pl.BlockSpec((2 * R, n), lambda c, s: (chip_block(s, j, chips), c))
    o = shape((T, E), BF)
    extra = [pl.BlockSpec(memory_space=pl.ANY)] * 3 if prev else []
    return call(
        kernel,
        (o, o, o, shape((1, E), F32)),
        (E // n,),
        rows + [cols, cols, cols] + extra,
        [out, out, out, pl.BlockSpec((1, n), lambda c, s: (0, c))],
        (12 * R * D * E, 4 * R * D + 6 * D * E + 12 * R * E),
        scratch=[scratch],
        alias={8: 0, 9: 1, 10: 2} if prev else None,
    )(sc, *block, wq, wk, wv, *(prev or ()))


def grad_inner_call(sc, block, wd):
    R, D = 2 * block[0].shape[0], block[0].shape[1]
    F = wd.shape[0]
    n = min(512, F)

    def kernel(s, *refs):
        w_ref, o_ref, x_ref = refs[4:]
        stage(refs[:4], x_ref)
        o_ref[...] = dot_nt(x_ref[...], w_ref[...]).astype(BF)

    rows, scratch = staged(block)
    return call(
        kernel,
        shape((2 * R, F), BF),
        (F // n,),
        rows + [pl.BlockSpec((n, D), lambda c, s: (c, 0))],
        pl.BlockSpec((2 * R, n), lambda c, s: (0, c)),
        (4 * R * D * F, 4 * R * D + 2 * D * F + 4 * R * F),
        scratch=[scratch],
    )(sc, *block, wd)


def ffn_a_call(sc, block, wg, wu, gi):
    R, D = 2 * block[0].shape[0], block[0].shape[1]
    F = wg.shape[1]
    n = min(512, F)

    def kernel(s, *refs):
        wg_ref, wu_ref, gi_ref, inner_ref, gg_ref, gu_ref, x_ref = refs[4:]
        stage(refs[:4], x_ref)
        for i in range(2):
            rows = slice(i * R, (i + 1) * R)
            g = dot(x_ref[rows], wg_ref[...])
            u = dot(x_ref[rows], wu_ref[...])
            sig = 0.5 * jnp.tanh(0.5 * g) + 0.5
            silu = g * sig
            inner_ref[rows] = (silu * u).astype(BF)
            gi_rows = gi_ref[rows].astype(F32)
            gu_ref[rows] = (gi_rows * silu).astype(BF)
            gg_ref[rows] = (gi_rows * u * (sig + silu * (1.0 - sig))).astype(BF)

    o = shape((2 * R, F), BF)
    rows, scratch = staged(block)
    cols = pl.BlockSpec((D, n), lambda c, s: (0, c))
    out = pl.BlockSpec((2 * R, n), lambda c, s: (0, c))
    return call(
        kernel,
        (o, o, o),
        (F // n,),
        rows + [cols, cols, out],
        [out, out, out],
        (8 * R * D * F, 4 * R * D + 4 * D * F + 16 * R * F),
        scratch=[scratch],
    )(sc, *block, wg, wu, gi)


def halves_out(R, D, n):
    H = R // 2
    return (shape((H, D), BF),) * 4, [pl.BlockSpec((H, n), lambda c, s: (0, c))] * 4


def ffn_b_call(sc, gg, gu, wg, wu):
    R2, F = gg.shape
    R = R2 // 2
    D = wg.shape[0]
    n = min(512, D)

    def kernel(s, gg_ref, gu_ref, wg_ref, wu_ref, *outs):
        put_rows(outs, dot_nt(gg_ref[...], wg_ref[...]) + dot_nt(gu_ref[...], wu_ref[...]))

    rows = pl.BlockSpec((R2, F), lambda c, s: (0, 0))
    cols = pl.BlockSpec((n, F), lambda c, s: (c, 0))
    shapes, specs = halves_out(R, D, n)
    return call(
        kernel,
        shapes,
        (D // n,),
        [rows, rows, cols, cols],
        specs,
        (8 * R * D * F, 8 * R * F + 4 * D * F + 4 * R * D),
    )(sc, gg, gu, wg, wu)


def down_call(sc, inner, wd):
    R2, F = inner.shape
    R = R2 // 2
    D = wd.shape[1]
    n = min(512, D)

    def kernel(s, x_ref, w_ref, *outs):
        put_rows(outs, dot(x_ref[...], w_ref[...]))

    shapes, specs = halves_out(R, D, n)
    return call(
        kernel,
        shapes,
        (D // n,),
        [pl.BlockSpec((R2, F), lambda c, s: (0, 0)), pl.BlockSpec((F, n), lambda c, s: (0, c))],
        specs,
        (4 * R * D * F, 4 * R * F + 2 * D * F + 4 * R * D),
    )(sc, inner, wd)


def wgrad_call(sc, blocks, gs, ndp, pieces):
    xs = [x for block in blocks for x in block]
    H, D = xs[0].shape
    nx = len(xs)
    C = D // ndp
    nb = len(gs[0])
    widths = [parts[0].shape[1] for parts in gs]
    T = H * nx
    rb = T // nb
    N = sum(widths)
    flat = [g for parts in gs for g in parts]
    far = ndp // 2 if pieces else 0
    sizes = [far // max(pieces, 1)] * pieces + [ndp - far]
    begins = [p * sizes[0] for p in range(len(sizes))]

    def kernel(s, *refs):
        x_refs, g_refs, o_refs, xt = refs[:nx], refs[nx : nx + len(flat)], refs[nx + len(flat) : -1], refs[-1]
        j = pl.program_id(0)
        for p in range(nx):
            xt[:, p * H : (p + 1) * H] = x_refs[p][...].T
        at = 0
        for w, width in enumerate(widths):
            acc = None
            for b in range(nb):
                term = dot(xt[:, b * rb : (b + 1) * rb], g_refs[w * nb + b][...])
                acc = term if acc is None else acc + term
            cols = slice(at, at + width)
            at += width
            low = acc.astype(BF)
            for o_ref, begin, size in zip(o_refs, begins, sizes):

                @pl.when((j >= begin) & (j < begin + size))
                def _():
                    o_ref[0, :, cols] = low

    def spec(begin, size):
        return pl.BlockSpec((1, C, N), lambda j, s: (jnp.clip(j - begin, 0, size - 1), 0, 0))

    order = (lambda j, s: (0, s[ORDER + j])) if pieces else (lambda j, s: (0, j))
    return call(
        kernel,
        tuple(shape((size, C, N), BF) for size in sizes),
        (ndp,),
        [pl.BlockSpec((H, C), order)] * nx + [whole(g.shape) for g in flat],
        [spec(begin, size) for begin, size in zip(begins, sizes)],
        (2 * T * D * N, 2 * T * (D + N) + 2 * D * N),
        scratch=[pltpu.VMEM((C, T), BF)],
    )(sc, *xs, *flat)


def attn_fwd_call(sc, q, k, v, h0, hh):
    T = q.shape[0]
    E = hh * HEAD
    B = min(512, T)
    nb = T // B
    c = HEAD**-0.5 * LOG2E

    def kernel(s, q_ref, k_ref, v_ref, o_ref, lse_ref):
        valid = s[VALID]
        for i in range(nb):
            qb = q_ref[i * B : (i + 1) * B]
            parts = []
            for j in range(i + 1):
                x = dot_nt(k_ref[j * B : (j + 1) * B], qb)
                if j == i:
                    u = lax.broadcasted_iota(jnp.int32, (B, B), 0)
                    t = lax.broadcasted_iota(jnp.int32, (B, B), 1)
                    x = jnp.where(u <= t, x, NEG)
                if (j + 1) * B > T // 2:
                    x = jnp.where(row_ids(B, j * B) < valid, x, NEG)
                parts.append(x)
            top = jnp.max(parts[0], axis=0, keepdims=True)
            for x in parts[1:]:
                top = jnp.maximum(top, jnp.max(x, axis=0, keepdims=True))
            top = top * c
            total = jnp.zeros((1, B), F32)
            acc = jnp.zeros((HEAD, B), F32)
            for j, x in enumerate(parts):
                p = jnp.exp2(x * c - top)
                total = total + jnp.sum(p, axis=0, keepdims=True)
                acc = acc + dot_tn(v_ref[j * B : (j + 1) * B], p.astype(BF))
            o_ref[i * B : (i + 1) * B] = (acc * (1.0 / total)).T
            lse_ref[0, :, i * B : (i + 1) * B] = top + jnp.log2(total)

    head = pl.BlockSpec((T, HEAD), lambda h, s: (0, h0 + h))
    out = pl.BlockSpec((T, HEAD), lambda h, s: (0, h))
    return call(
        kernel,
        (shape((T, E), F32), shape((hh, 1, T), F32)),
        (hh,),
        [head, head, head],
        [out, pl.BlockSpec((1, 1, T), lambda h, s: (h, 0, 0))],
        (6 * T * T * E, 10 * T * E),
    )(sc, q, k, v)


def attn_bwd_call(sc, q, k, v, do, attended, h0, part):
    lo, lse = attended
    nh = 1
    T = q.shape[0]
    B = min(512, T)
    nb = T // B
    scale = HEAD**-0.5
    c = scale * LOG2E

    def kernel(s, q_ref, k_ref, v_ref, do_ref, lo_ref, lse_ref, dq_ref, dk_ref, dv_ref, delta):
        valid = s[VALID]
        ones = jnp.ones((8, HEAD), F32)
        for i in range(nb):
            rows = slice(i * B, (i + 1) * B)
            prod = do_ref[rows].astype(F32) * lo_ref[rows]
            delta[:, rows] = lax.dot_general(
                ones,
                prod,
                (((1,), (1,)), ((), ())),
                precision=lax.Precision.HIGHEST,
                preferred_element_type=F32,
            )
        dq_ref[...] = jnp.zeros_like(dq_ref)
        for j in range(nb):
            kb = k_ref[j * B : (j + 1) * B]
            vb = v_ref[j * B : (j + 1) * B]
            dk = jnp.zeros((B, HEAD), F32)
            dv = jnp.zeros((B, HEAD), F32)
            for i in range(j, nb):
                rows = slice(i * B, (i + 1) * B)
                qb = q_ref[rows]
                dob = do_ref[rows]
                p = jnp.exp2(dot_nt(kb, qb) * c - lse_ref[0, :, rows])
                if i == j:
                    u = lax.broadcasted_iota(jnp.int32, (B, B), 0)
                    t = lax.broadcasted_iota(jnp.int32, (B, B), 1)
                    p = jnp.where(u <= t, p, 0.0)
                if (j + 1) * B > T // 2:
                    p = jnp.where(row_ids(B, j * B) < valid, p, 0.0)
                ds = (p * (dot_nt(vb, dob) - delta[0:1, rows])).astype(BF)
                dv = dv + dot(p.astype(BF), dob)
                dk = dk + dot(ds, qb)
                dq_ref[rows] += dot_tn(ds, kb)
            dk_ref[j * B : (j + 1) * B] = dk * scale
            dv_ref[j * B : (j + 1) * B] = dv
        dq_ref[...] *= scale

    o = shape((T, nh * HEAD), F32)
    head = pl.BlockSpec((T, HEAD), lambda h, s: (0, h0 + h))
    out = pl.BlockSpec((T, HEAD), lambda h, s: (0, h))
    return call(
        kernel,
        (o, o, o),
        (nh,),
        [head] * 4
        + [pl.BlockSpec((T, HEAD), lambda h, s: (0, part)), pl.BlockSpec((1, 1, T), lambda h, s: (part, 0, 0))],
        [out, out, out],
        (12 * T * T * HEAD * nh, 26 * T * HEAD * nh),
        scratch=[pltpu.VMEM((8, T), F32)],
    )(sc, q, k, v, do, lo, lse)


def maps_call(sc, k, v, gathered):
    T, E = k.shape
    hh = E // HEAD
    ndp = gathered.shape[0]

    def kernel(s, k_ref, v_ref, g_ref, maps_ref, norm_ref):
        h = pl.program_id(0)
        norm = jnp.zeros((1, HEAD), F32)
        for a in range(ndp - 1):
            after = (norm + g_ref[shared_at(s, a, ndp), pl.ds(h, 1)]) * g_ref[shared_at(s, a + 1, ndp), hh : hh + 1]
            norm = jnp.where(a < s[PLACE], after, norm)
        norm_ref[0] = norm
        k = k_ref[...].astype(F32)
        phi = jnp.where(row_ids(T, 0) < s[VALID], phi_of(k, exp_low(k)), 0.0)
        den = jnp.maximum(jnp.sum(phi * norm, axis=1, keepdims=True), 1.0)
        low = phi.astype(BF)
        maps_ref[0, 0] = dot_tn((phi * (1.0 / den)).astype(BF), low).astype(BF)
        maps_ref[1, 0] = dot_tn(low, v_ref[...]).astype(BF)

    head = pl.BlockSpec((T, HEAD), lambda h, s: (0, h))
    return call(
        kernel,
        (shape((2, hh, HEAD, HEAD), BF), shape((hh, 1, HEAD), F32)),
        (hh,),
        [head, head, whole(gathered.shape)],
        [
            pl.BlockSpec((2, 1, HEAD, HEAD), lambda h, s: (0, h, 0, 0)),
            pl.BlockSpec((1, 1, HEAD), lambda h, s: (h, 0, 0)),
        ],
        (4 * T * E * HEAD, 4 * T * E),
    )(sc, k, v, gathered)


def times_state(g, state):
    high = state.astype(BF)
    return dot(g, high) + dot(g, (state - high.astype(F32)).astype(BF))


def chain_call(sc, gathered, maps):
    ndp, _, hh = maps.shape[:3]

    def kernel(s, g_ref, maps_ref, m_ref):
        state = [jnp.zeros((HEAD, HEAD), F32) for _ in range(hh)]
        for a in range(ndp - 1):
            keep = g_ref[shared_at(s, a + 1, ndp), hh : hh + 1]
            before = a < s[PLACE]
            for h in range(hh):
                after = state[h] - times_state(maps_ref[a, 0, h], state[h])
                after = (after + maps_ref[a, 1, h].astype(F32)) * keep
                state[h] = jnp.where(before, after, state[h])
        for h in range(hh):
            m_ref[h] = state[h]

    return call(
        kernel,
        shape((hh, HEAD, HEAD), F32),
        (1,),
        [whole(gathered.shape), whole(maps.shape)],
        whole((hh, HEAD, HEAD)),
        (4e8, 2 * maps.size),
    )(sc, gathered, maps)


def mixout_call(sc, j, chips, q, locals_, memory, norm, mix, wo):
    T, E = q.shape
    hh = E // HEAD
    D = wo.shape[1]
    R = T // chips // 2
    n = min(512, D)
    groups = len(locals_)
    per = hh // groups

    def kernel(s, q_ref, *rest):
        l_refs = rest[:groups]
        m_ref, n_ref, mix_ref, w_ref, *outs, mixed_ref, diff_ref = rest[groups:]

        @pl.when(pl.program_id(0) == 0)
        def _():
            for i in range(2):
                off = pl.multiple_of((s[CORE] if i == 0 else 1 - s[CORE]) * R, R)
                for h in range(hh):
                    cols = slice(h * HEAD, (h + 1) * HEAD)
                    qv = q_ref[pl.ds(off, R), cols].astype(F32)
                    phi = phi_of(qv, exp_low(qv))
                    den = jnp.maximum(jnp.sum(phi * n_ref[h], axis=1, keepdims=True), 1.0)
                    read = dot(phi.astype(BF), m_ref[h].astype(BF)) * (1.0 / den)
                    local = l_refs[h // per][pl.ds(off, R), h % per * HEAD : (h % per + 1) * HEAD]
                    diff = read - local
                    mixed = local + mix_ref[h] * diff
                    diff_ref[i * R : (i + 1) * R, cols] = diff.astype(BF)
                    mixed_ref[i * R : (i + 1) * R, cols] = mixed.astype(BF)

        put_rows(outs, dot(mixed_ref[...], w_ref[...]))

    rows = pl.BlockSpec((2 * R, E), lambda c, s: (chip_block(s, j, chips), 0))
    shapes, specs = halves_out(R, D, n)
    rel = pl.BlockSpec((2 * R, E), lambda c, s: (0, 0))
    return call(
        kernel,
        shapes + (shape((2 * R, E), BF), shape((2 * R, E), BF)),
        (D // n,),
        [rows]
        + [pl.BlockSpec((2 * R, per * HEAD), lambda c, s: (chip_block(s, j, chips), 0))] * groups
        + [whole(memory.shape), whole(norm.shape), whole(mix.shape), pl.BlockSpec((E, n), lambda c, s: (0, c))],
        specs + [rel, rel],
        (4 * R * E * D + 8 * R * E * HEAD, 20 * R * E + 2 * E * D + 4 * R * D),
    )(sc, q, *locals_, memory, norm, mix, wo)


def gradmix_call(sc, j, chips, block, wo, diff, q, norm, mix, prev):
    R, D = 2 * block[0].shape[0], block[0].shape[1]
    E = wo.shape[0]
    hh = E // HEAD
    T = 2 * R * chips
    n = min(256, E)
    per = n // HEAD

    def kernel(s, *refs):
        w_ref, diff_ref, q_ref, n_ref, mix_ref = refs[4:9]
        do_ref, gm_ref, cot_ref, b_ref, x_ref = refs[-5:]
        stage(refs[:4], x_ref)
        sums = jnp.zeros((1, n), F32)
        cots = [jnp.zeros((HEAD, HEAD), F32) for _ in range(per)]
        for i in range(2):
            off = pl.multiple_of((s[CORE] if i == 0 else 1 - s[CORE]) * R, R)
            grad = dot_nt(x_ref[i * R : (i + 1) * R], w_ref[...])
            sums = sums + jnp.sum(grad * diff_ref[i * R : (i + 1) * R].astype(F32), axis=0, keepdims=True)
            for h in range(per):
                cols = slice(h * HEAD, (h + 1) * HEAD)
                part = grad[:, cols]
                grad_read = part * mix_ref[h]
                do_ref[pl.ds(off, R), cols] = (part - grad_read).astype(BF)
                gm_ref[pl.ds(off, R), cols] = grad_read.astype(BF)
                qv = q_ref[pl.ds(off, R), cols].astype(F32)
                phi = phi_of(qv, exp_low(qv))
                den = jnp.maximum(jnp.sum(phi * n_ref[h], axis=1, keepdims=True), 1.0)
                cots[h] = cots[h] + dot_tn(phi.astype(BF), (grad_read * (1.0 / den)).astype(BF))
        for h in range(per):
            cot_ref[h] = cots[h]
        b_ref[...] = sums

    rows, scratch = staged(block)
    place = pl.BlockSpec((2 * R, n), lambda c, s: (chip_block(s, j, chips), c))
    per_head = pl.BlockSpec((per, 1, HEAD), lambda c, s: (c, 0, 0))
    o = shape((T, E), BF)
    extra = [pl.BlockSpec(memory_space=pl.ANY)] * 2 if prev else []
    return call(
        kernel,
        (o, o, shape((hh, HEAD, HEAD), F32), shape((1, E), F32)),
        (E // n,),
        rows
        + [pl.BlockSpec((n, D), lambda c, s: (c, 0)), pl.BlockSpec((2 * R, n), lambda c, s: (0, c)), place, per_head, per_head]
        + extra,
        [place, place, pl.BlockSpec((per, HEAD, HEAD), lambda c, s: (c, 0, 0)), pl.BlockSpec((1, n), lambda c, s: (0, c))],
        (4 * R * E * D + 4 * R * E * HEAD, 4 * R * D + 2 * E * D + 16 * R * E),
        scratch=[scratch],
        alias={10: 0, 11: 1} if prev else None,
    )(sc, *block, wo, diff, q, norm, mix, *(prev or ()))


def memory_rows(q, k, grad_read, live, memory, norm, cot):
    low_q = exp_low(q)
    low_k = exp_low(k)
    phi_q = phi_of(q, low_q)
    phi_k = jnp.where(live, phi_of(k, low_k), 0.0)
    raw_q = jnp.sum(phi_q * norm, axis=1, keepdims=True)
    raw_k = jnp.sum(phi_k * norm, axis=1, keepdims=True)
    inv_q = 1.0 / jnp.maximum(raw_q, 1.0)
    inv_k = 1.0 / jnp.maximum(raw_k, 1.0)
    read = dot(phi_q.astype(BF), memory)
    recalled = dot(phi_k.astype(BF), memory) * inv_k
    pushed = dot(phi_k.astype(BF), cot)
    scaled = grad_read * inv_q
    w_q = jnp.where(raw_q > 1.0, -jnp.sum(scaled * read, axis=1, keepdims=True) * inv_q, 0.0)
    w_k = jnp.where(raw_k > 1.0, jnp.sum(pushed * recalled, axis=1, keepdims=True) * inv_k, 0.0)
    return low_q, low_k, phi_q, phi_k, inv_k, recalled, pushed, scaled, w_q, w_k


def memory_cot_call(sc, gathered, maps, cots, q, k, grad_read, memory, norm):
    T, E = q.shape
    hh = E // HEAD
    ndp = maps.shape[0]
    B = min(512, T)

    def kernel(s, g_ref, maps_ref, cots_ref, q_ref, k_ref, gm_ref, m_ref, n_ref, x_ref, nb_ref):
        cot = jnp.zeros((HEAD, HEAD), F32)
        for a in range(ndp - 1, 0, -1):
            before = cot - times_state(maps_ref[a, 0, 0], cot) + cots_ref[shared_at(s, a, ndp), 0].astype(F32)
            cot = jnp.where(a > s[PLACE], before * g_ref[shared_at(s, a, ndp), hh : hh + 1], cot)
        x_ref[0] = cot
        cot = cot.astype(BF)
        memory = m_ref[0].astype(BF)
        sums = jnp.zeros((1, HEAD), F32)
        for i in range(T // B):
            rows = slice(i * B, (i + 1) * B)
            live = row_ids(B, i * B) < s[VALID]
            terms = memory_rows(
                q_ref[rows].astype(F32), k_ref[rows].astype(F32), gm_ref[rows].astype(F32), live, memory, n_ref[0], cot
            )
            sums = sums + jnp.sum(terms[2] * terms[8] + terms[3] * terms[9], axis=0, keepdims=True)
        nb_ref[0] = sums

    head = pl.BlockSpec((T, HEAD), lambda h, s: (0, h))
    square = pl.BlockSpec((1, HEAD, HEAD), lambda h, s: (h, 0, 0))
    row = pl.BlockSpec((1, 1, HEAD), lambda h, s: (h, 0, 0))
    return call(
        kernel,
        (shape((hh, HEAD, HEAD), F32), shape((hh, 1, HEAD), F32)),
        (hh,),
        [
            whole(gathered.shape),
            pl.BlockSpec((ndp, 1, 1, HEAD, HEAD), lambda h, s: (0, 0, h, 0, 0)),
            pl.BlockSpec((ndp, 1, HEAD, HEAD), lambda h, s: (0, h, 0, 0)),
            head,
            head,
            head,
            square,
            row,
        ],
        [square, row],
        (8 * T * E * HEAD, 6 * T * E),
    )(sc, gathered, maps, cots, q, k, grad_read, memory, norm)


def combine_call(sc, chips, q, k, v, grad_read, local_grads, memory, norm, cot, gathered, norm_parts):
    T, E = q.shape
    hh = E // HEAD
    R = T // chips // 2
    ndp = gathered.shape[0]
    per = local_grads[0][0].shape[1] // HEAD
    groups = len(local_grads)

    def kernel(s, q_ref, k_ref, v_ref, gm_ref, *rest):
        local_refs = rest[: 3 * groups]
        m_ref, n_ref, x_ref, g_ref, nb_ref, gq_ref, gk_ref, gv_ref = rest[3 * groups :]
        begin = piece(pl.program_id(0), s) * R
        live = row_ids(R, begin) < s[VALID]
        for h in range(hh):
            cols = slice(h * HEAD, (h + 1) * HEAD)
            part = slice(h % per * HEAD, (h % per + 1) * HEAD)
            dq, dk, dv = (ref[:, part] for ref in local_refs[3 * (h // per) : 3 * (h // per) + 3])
            norm_cot = jnp.zeros((1, HEAD), F32)
            for a in range(ndp - 1, 0, -1):
                other = shared_at(s, a, ndp)
                before = (norm_cot + nb_ref[other, h : h + 1]) * g_ref[other, hh : hh + 1]
                norm_cot = jnp.where(a > s[PLACE], before, norm_cot)
            memory = m_ref[h].astype(BF)
            cot = x_ref[h].astype(BF)
            norm = n_ref[h]
            low_q, low_k, _, _, inv_k, recalled, pushed, scaled, w_q, w_k = memory_rows(
                q_ref[:, cols].astype(F32), k_ref[:, cols].astype(F32), gm_ref[:, cols].astype(F32), live, memory, norm, cot
            )
            grad_phi_q = dot_nt(scaled.astype(BF), memory) + w_q * norm
            grad_phi_k = (
                dot_nt((v_ref[:, cols].astype(F32) - recalled).astype(BF), cot)
                - dot_nt((pushed * inv_k).astype(BF), memory)
                + w_k * norm
                + norm_cot
            )
            gq_ref[:, cols] = (dq + grad_phi_q * low_q).astype(BF)
            gk_ref[:, cols] = (dk + jnp.where(live, grad_phi_k * low_k, 0.0)).astype(BF)
            gv_ref[:, cols] = (dv + pushed).astype(BF)

    def piece(p, s):
        core = lax.rem(s[CORE] + p, 2)
        return chip_block(s, p // 2, chips) * 2 + core

    rows = pl.BlockSpec((R, E), lambda p, s: (piece(p, s), 0))
    part_rows = pl.BlockSpec((R, per * HEAD), lambda p, s: (piece(p, s), 0))
    out = pl.BlockSpec((R, E), lambda p, s: (p, 0))
    o = shape((T, E), BF)
    return call(
        kernel,
        (o, o, o),
        (2 * chips,),
        [rows] * 4 + [part_rows] * (3 * groups) + [whole(x.shape) for x in (memory, norm, cot, gathered, norm_parts)],
        [out, out, out],
        (14 * T * E * HEAD, 26 * T * E),
    )(sc, q, k, v, grad_read, *[x for group in local_grads for x in group], memory, norm, cot, gathered, norm_parts)


def grad_normed_call(sc, j, gq, gk, gv, wq, wk, wv, block, chips):
    T, E = gq.shape
    R = T // chips // 2
    D = wq.shape[0]
    n = min(512, D)

    def kernel(s, gq_ref, gk_ref, gv_ref, wq_ref, wk_ref, wv_ref, *rest):
        grad = dot_nt(gq_ref[...], wq_ref[...]) + dot_nt(gk_ref[...], wk_ref[...]) + dot_nt(gv_ref[...], wv_ref[...])
        put_rows(rest[4:8], grad)
        sums, at = 0.0, 0
        for ref in rest[:4]:
            part = grad[at : at + ref.shape[0]] * ref[...].astype(F32)
            sums = sums + jnp.sum(part, axis=0, keepdims=True)
            at += ref.shape[0]
        rest[8][...] = sums

    rows = pl.BlockSpec((2 * R, E), lambda c, s: (j, 0))
    cols = pl.BlockSpec((n, E), lambda c, s: (c, 0))
    shapes, specs = halves_out(R, D, n)
    return call(
        kernel,
        shapes + (shape((1, D), F32),),
        (D // n,),
        [rows, rows, rows, cols, cols, cols] + specs,
        specs + [pl.BlockSpec((1, n), lambda c, s: (0, c))],
        (12 * R * D * E, 12 * R * E + 6 * D * E + 4 * R * D),
    )(sc, gq, gk, gv, wq, wk, wv, *block)


def swap_core(pair):
    count = lax.axis_size("tensor")
    return tuple(lax.ppermute(x, "tensor", [(i, i ^ 1) for i in range(count)]) for x in pair)


def shift_chip(pair, j):
    count = lax.axis_size("tensor")
    return tuple(lax.ppermute(x, "tensor", [(i, (i + 2 * j) % count) for i in range(count)]) for x in pair)


def with_swapped(pair):
    return tuple(pair) + swap_core(pair)


def chunk_order(me, ndp):
    parity = me % 2
    order = [2 * i + (1 - parity) for i in range(ndp // 2)] + [2 * i + parity for i in range(ndp // 2)]
    return jnp.stack(order)


def exchange_x(x):
    return lax.ppermute(x, "dp", [(i, i ^ 1) for i in range(lax.axis_size("dp"))])


def sum_z(x):
    ndp = lax.axis_size("dp")
    groups = [list(range(0, ndp, 2)), list(range(1, ndp, 2))]
    return lax.psum_scatter(x, "dp", scatter_dimension=0, axis_index_groups=groups, tiled=True)


def finish_x(both, parity):
    C = both.shape[0] // 2
    got = exchange_x(lax.dynamic_slice_in_dim(both, (1 - parity) * C, C, 0))
    return got.astype(F32) + lax.dynamic_slice_in_dim(both, parity * C, C, 0).astype(F32)


def share_steps(x):
    count = lax.axis_size("dp")
    steps = [1 << bit for bit in range(1, count.bit_length() - 1)] + [1]
    x = x[None]
    for step in steps:
        x = jnp.concatenate([x, lax.ppermute(x, "dp", [(i, i ^ step) for i in range(count)])])
        yield x


def shared_at(s, a, count):
    apart = a ^ s[PLACE]
    return (apart >> 1) + (apart & 1) * (count // 2)


def share_over_dp(x):
    return list(share_steps(x))[-1]


def sum_everywhere(x):
    for axis in ("tensor", "dp"):
        count, step = lax.axis_size(axis), 1
        while step < count:
            x = x + lax.ppermute(x, axis, [(i, i ^ step) for i in range(count)])
            step *= 2
    return x


def body(
    tokens,
    gain1,
    w_query,
    w_key,
    w_value,
    w_out,
    gate_bias,
    gain2,
    w_gate,
    w_up,
    w_down,
    seg_starts,
    seg_valid,
    cotangent,
):
    count = lax.axis_size("tensor")
    ndp = lax.axis_size("dp")
    chips = count // 2
    hh = gate_bias.shape[0]
    E = hh * HEAD
    here = lax.axis_index("tensor")
    place = lax.axis_index("dp")
    sc = jnp.concatenate(
        [
            jnp.stack([here // 2, here % 2, place]).astype(jnp.int32),
            seg_valid.astype(jnp.int32),
            chunk_order(place, ndp).astype(jnp.int32),
        ]
    )
    keep = (1 - seg_starts[0]).astype(F32)
    sig_bias = jax.nn.sigmoid(gate_bias)
    mix = jnp.broadcast_to(sig_bias[:, None, None], (hh, 1, HEAD))

    ORDERED.clear()
    per = max(1, hh // 2)

    gain1 = gain1[None]
    gain2 = gain2[None]
    chip_range = range(1, chips)
    parity = place % 2
    R = tokens.shape[0]
    four = min(4, ndp // 2)

    def norm1_kernel(x_ref, g_ref, o_ref):
        o_ref[...] = (unit_rows(x_ref[...].astype(F32))[0] * g_ref[...]).astype(BF)

    normed1 = rows_call(norm1_kernel, [[BF]], sc, [tokens], [gain1])[0]
    rows1 = [with_swapped(normed1)]
    far1 = [shift_chip(normed1, -j) for j in chip_range]
    own_cot = (cotangent[: R // 2], cotangent[R // 2 :])
    cot_rows = [with_swapped(own_cot)]
    *qkv, sums = qkv_call(sc, 0, chips, rows1[0], w_query, w_key, w_value, None)
    *far1, own_cot = hold_pairs(sc, far1 + [own_cot])
    far_cot = [shift_chip(own_cot, -j) for j in chip_range]
    for j in chip_range:
        rows1.append(with_swapped(far1[j - 1]))
        *qkv, column_sums = qkv_call(sc, j, chips, rows1[j], w_query, w_key, w_value, qkv)
        sums = sums + column_sums
    q, k, v = qkv

    own = jnp.concatenate([sums.reshape(hh, HEAD), jnp.full((8 - hh, HEAD), keep, F32)])
    gathered = share_over_dp(own)
    maps, norm = maps_call(sc, k, v, gathered)
    all_maps = lax.all_gather(maps, "dp")
    attended = [attn_fwd_call(sc, q, k, v, h, per) for h in range(0, hh, per)]
    far_cot = hold_pairs(sc, far_cot)
    cot_rows += [with_swapped(pair) for pair in far_cot]
    grad_inner = [grad_inner_call(sc, block, w_down) for block in cot_rows]
    memory = chain_call(sc, gathered, all_maps)

    mixed, diff = [None] * chips, [None] * chips

    def mixout(j):
        *block, mixed[j], diff[j] = mixout_call(sc, j, chips, q, [one[0] for one in attended], memory, norm, mix, w_out)
        return block

    def scatter(make):
        blocks = [make(j) for j in chip_range] + [make(0)]
        got = []
        for j in chip_range:
            block = blocks[j - 1]
            sums = add_rows(sc, [tuple(block[:2]), swap_core(block[2:])], True)
            got.append(shift_chip(sums, j))
        block = blocks[-1]
        return [tuple(block[:2]), swap_core(block[2:]), *got]

    hidden, normed2 = norm_call(sc, [tokens, *scatter(mixout)], gain2)
    rows2 = [with_swapped(normed2)]
    far2 = [shift_chip(normed2, -j) for j in chip_range]
    ffn = [ffn_a_call(sc, rows2[0], w_gate, w_up, grad_inner[0])]
    far2 = hold_pairs(sc, far2)
    for j in chip_range:
        rows2.append(with_swapped(far2[j - 1]))
        ffn.append(ffn_a_call(sc, rows2[j], w_gate, w_up, grad_inner[j]))
    inner, grad_gate, grad_up = zip(*ffn)

    (w_up_parts,) = wgrad_call(sc, rows2, [grad_up], ndp, 0)
    both_up = sum_z(w_up_parts.reshape((-1, w_up_parts.shape[2])))
    back = scatter(lambda j: ffn_b_call(sc, grad_gate[j], grad_up[j], w_gate, w_up))
    far_gate, near_gate = wgrad_call(sc, rows2, [grad_gate], ndp, 1)
    far_gate = exchange_x(far_gate)
    far_down, near_down = wgrad_call(sc, cot_rows, [inner], ndp, 1)
    far_down = exchange_x(far_down)
    grad_hidden, grad_low, gain2_part = norm_back_call(sc, cotangent, hidden, back, gain2, True)
    grad_rows = [with_swapped(grad_low)]
    far_grad = [shift_chip(grad_low, -j) for j in chip_range]
    down_far = [down_call(sc, inner[j], w_down) for j in chip_range]
    *grads, cot_part, bias_part = gradmix_call(sc, 0, chips, grad_rows[0], w_out, diff[0], q, norm, mix, None)
    down_near = down_call(sc, inner[0], w_down)
    far_grad = hold_pairs(sc, far_grad)
    pair_gate = pair_call(sc, [(far_gate, near_gate)])
    sum_gate = sum_z(pair_gate)
    require(both_up)
    sum_up = finish_x(both_up, parity)
    for j in chip_range:
        grad_rows.append(with_swapped(far_grad[j - 1]))
        *grads, cot_j, bias_j = gradmix_call(sc, j, chips, grad_rows[j], w_out, diff[j], q, norm, mix, grads)
        cot_part = cot_part + cot_j
        bias_part = bias_part + bias_j
    down_blocks = iter(down_far + [down_near])
    down = scatter(lambda j: next(down_blocks))
    grad_local, grad_read = grads

    local_grads = []
    steps = share_steps(cot_part.astype(BF))
    all_cots = None
    for h in range(hh):
        local_grads.append(attn_bwd_call(sc, q, k, v, grad_local, attended[h // per], h, h % per))
        if h in (0, max(2, hh - 2)):
            all_cots = next(steps)
            require(all_cots)
    for all_cots in steps:
        pass
    pair_down = pair_call(sc, [(far_down, near_down)])
    sum_down = sum_z(pair_down)
    require(sum_up)
    memory_cot, norm_part = memory_cot_call(sc, gathered, all_maps, all_cots, q, k, grad_read, memory, norm)
    steps = share_steps(jnp.concatenate([norm_part.reshape(hh, HEAD), jnp.zeros((8 - hh, HEAD), F32)]))
    require(next(steps))
    far_out, near_out = wgrad_call(sc, grad_rows, [mixed], ndp, 1)
    far_out = exchange_x(far_out)
    for norm_parts in steps:
        pass
    require(sum_gate)
    gq, gk, gv = combine_call(
        sc, chips, q, k, v, grad_read, local_grads, memory, norm, memory_cot, gathered, norm_parts
    )
    gain1_sums = []

    def back_rows(j):
        *block, sums = grad_normed_call(sc, j, gq, gk, gv, w_query, w_key, w_value, rows1[j], chips)
        gain1_sums.append(sums)
        return block

    parts1 = {}

    def make1(name, grad):
        far, near = wgrad_call(sc, rows1, [[grad]], ndp, 1)
        parts1[name] = exchange_x(far), near

    make1("v", gv)
    make1("k", gk)
    output = add_rows(sc, [hidden, *down], False)
    back1 = scatter(back_rows)
    require(sum_down)
    sum_ovk = sum_z(pair_call(sc, [(far_out, near_out), parts1["v"], parts1["k"]]))
    make1("q", gq)
    (grad_tokens,) = norm_back_call(sc, grad_hidden, tokens, back1, gain1, False)
    require(sum_ovk)
    sum_ovk = sum_ovk.astype(F32)
    sum_query = sum_z(pair_call(sc, [parts1["q"]])).astype(F32)
    gain1_part = sum(gain1_sums) / gain1

    bias_here = jnp.sum(bias_part.reshape(hh, HEAD), axis=1) * sig_bias * (1.0 - sig_bias)
    bias_full = lax.dynamic_update_slice(jnp.zeros((HEADS,), F32), bias_here, (here * hh,))
    small = sum_everywhere(jnp.concatenate([gain1_part[0], gain2_part[0], bias_full]))
    D = gain1.shape[1]
    return (
        output,
        grad_tokens,
        small[:D],
        sum_query,
        sum_ovk[:, 2 * E :],
        sum_ovk[:, E : 2 * E],
        sum_ovk[:, :E].T,
        small[2 * D :],
        small[D : 2 * D],
        sum_gate.astype(F32),
        sum_up,
        sum_down.astype(F32).T,
    )


def solution(mesh):
    rows = P(("dp", "tensor"), None)
    return jax.shard_map(
        body,
        mesh=mesh,
        in_specs=(
            rows,
            P(),
            P(None, "tensor"),
            P(None, "tensor"),
            P(None, "tensor"),
            P("tensor", None),
            P("tensor"),
            P(),
            P(None, "tensor"),
            P(None, "tensor"),
            P("tensor", None),
            P("dp"),
            P("dp"),
            rows,
        ),
        out_specs=(
            rows,
            rows,
            P(),
            P("dp", "tensor"),
            P("dp", "tensor"),
            P("dp", "tensor"),
            P("tensor", "dp"),
            P(),
            P(),
            P("dp", "tensor"),
            P("dp", "tensor"),
            P("tensor", "dp"),
        ),
        check_vma=False,
    )
```

```python
import jax
import jax.numpy as jnp
from jax import lax
from jax.experimental import pallas as pl
from jax.experimental.pallas import tpu as pltpu
from jax.sharding import PartitionSpec as P

HEADS = 16
HEAD = 128
EPSILON = 1e-06
BF = jnp.bfloat16
F32 = jnp.float32
LOG2E = 1.4426950408889634
NEG = -1e30
VMEM_BYTES = 56 << 20


def dot(a, b):
    return jnp.dot(a, b, preferred_element_type=F32)


def dot_nt(a, b):
    return lax.dot_general(a, b, (((1,), (1,)), ((), ())), preferred_element_type=F32)


def dot_tn(a, b):
    return lax.dot_general(a, b, (((0,), (0,)), ((), ())), preferred_element_type=F32)


def shape(dims, dtype):
    return jax.ShapeDtypeStruct(dims, dtype)


COST = 20.0
ORDERED = []


def call(kernel, out_shape, grid, in_specs, out_specs, cost, scratch=(), alias=None):
    many = isinstance(out_shape, tuple)
    plain = len(in_specs) + 1
    token = [pl.BlockSpec(memory_space=pl.ANY)] * len(ORDERED)

    def ordered_kernel(*refs):
        kernel(*refs[:plain], *refs[plain + len(token) :])

    made = pl.pallas_call(
        ordered_kernel,
        out_shape=out_shape,
        grid_spec=pltpu.PrefetchScalarGridSpec(
            num_scalar_prefetch=1,
            grid=grid,
            in_specs=list(in_specs) + token,
            out_specs=out_specs,
            scratch_shapes=list(scratch),
        ),
        input_output_aliases=alias or {},
        compiler_params=pltpu.CompilerParams(
            dimension_semantics=("arbitrary",) * len(grid), vmem_limit_bytes=VMEM_BYTES
        ),
        cost_estimate=pl.CostEstimate(
            flops=int(COST * cost[0]), bytes_accessed=int(COST * cost[1]), transcendentals=0
        ),
    )

    def run(*operands):
        out = made(*operands, *ORDERED)
        ORDERED[:] = [out[-1] if many else out]
        return out

    return run


def require(*arrays):
    ORDERED.extend(arrays)


def hold(sc, *arrays):
    n = len(arrays)

    def kernel(*refs):
        del refs

    one = pl.BlockSpec(memory_space=pl.ANY)
    found = call(
        kernel,
        tuple(shape(x.shape, x.dtype) for x in arrays),
        (1,),
        [one] * n,
        [one] * n,
        (1e6, 1e4),
        alias={1 + i: i for i in range(n)},
    )(sc, *arrays)
    ORDERED.clear()
    ORDERED.append(found[0])
    return found


def hold_pairs(sc, pairs):
    found = hold(sc, *[x for pair in pairs for x in pair])
    return [tuple(found[2 * i : 2 * i + 2]) for i in range(len(pairs))]


class Halves:
    def __init__(self, low, high, first):
        self.low, self.high, self.first = low, high, first

    def __getitem__(self, at):
        return jnp.where(self.first, self.low[at], self.high[at])

    def __setitem__(self, at, value):
        @pl.when(self.first)
        def _():
            self.low[at] = value

        @pl.when(jnp.logical_not(self.first))
        def _():
            self.high[at] = value


def rows_call(kernel, outs, sc, rows, shared, sums=0):
    first = rows[0]
    R, D = (2 * first[0].shape[0], first[0].shape[1]) if isinstance(first, tuple) else first.shape
    n = min(128, R // 2)
    half = R // 2 // n
    block = pl.BlockSpec((n, D), lambda i, s: (i, 0))
    low = pl.BlockSpec((n, D), lambda i, s: (jnp.minimum(i, half - 1), 0))
    high = pl.BlockSpec((n, D), lambda i, s: (jnp.maximum(i - half, 0), 0))
    one = pl.BlockSpec((1, D), lambda i, s: (0, 0))
    in_specs, operands, kinds = [], [], []
    for x in rows:
        pair = isinstance(x, tuple)
        kinds.append(pair)
        in_specs += [low, high] if pair else [block]
        operands += list(x) if pair else [x]
    kinds += [False] * len(shared)
    out_specs, out_shapes = [], []
    for x in outs:
        pair = isinstance(x, list)
        kinds.append(pair)
        out_specs += [low, high] if pair else [block]
        out_shapes += [shape((R // 2, D), x[0])] * 2 if pair else [shape((R, D), x)]
    kinds += [False] * sums

    def body_kernel(s, *refs):
        i = pl.program_id(0)

        @pl.when(i == 0)
        def _():
            for ref in refs[len(refs) - sums :] if sums else ():
                ref[...] = jnp.zeros_like(ref)

        views, at = [], 0
        for pair in kinds:
            views.append(Halves(refs[at], refs[at + 1], i < half) if pair else refs[at])
            at += 2 if pair else 1
        kernel(*views)

    found = call(
        body_kernel,
        tuple(out_shapes + [shape((1, D), F32)] * sums),
        (R // n,),
        in_specs + [one] * len(shared),
        out_specs + [one] * sums,
        (10 * R * D, 20 * R * D),
    )(sc, *operands, *shared)
    result, at = [], 0
    for x in outs:
        pair = isinstance(x, list)
        result.append(tuple(found[at : at + 2]) if pair else found[at])
        at += 2 if pair else 1
    return result + list(found[at:])


def add_rows(sc, terms, split):
    def kernel(*refs):
        refs[-1][...] = sum(ref[...].astype(F32) for ref in refs[:-1]).astype(BF)

    return rows_call(kernel, [[BF] if split else BF], sc, terms, [])[0]


def unit_rows(values):
    inverse = lax.rsqrt(jnp.mean(values * values, axis=-1, keepdims=True) + EPSILON)
    return values * inverse, inverse


def norm_call(sc, terms, gain):
    def kernel(*refs):
        gain_ref, sum_ref, out_ref = refs[-3:]
        total = sum(ref[...].astype(F32) for ref in refs[:-3])
        sum_ref[...] = total
        out_ref[...] = (unit_rows(total)[0] * gain_ref[...]).astype(BF)

    return rows_call(kernel, [F32, [BF]], sc, terms, [gain])


def norm_back_call(sc, base, values, terms, gain, low):
    def kernel(base_ref, values_ref, *refs):
        term_refs, gain_ref, outs = refs[: len(terms)], refs[len(terms)], refs[len(terms) + 1 :]
        grad = sum(ref[...].astype(F32) for ref in term_refs)
        unit, inverse = unit_rows(values_ref[...].astype(F32))
        if low:
            outs[-1][...] += jnp.sum(grad * unit, axis=0, keepdims=True)
        scaled = grad * gain_ref[...]
        out = base_ref[...].astype(F32) + inverse * (
            scaled - unit * jnp.mean(scaled * unit, axis=-1, keepdims=True)
        )
        outs[0][...] = out
        if low:
            outs[1][...] = out.astype(BF)

    return rows_call(kernel, [F32, [BF]] if low else [F32], sc, [base, values, *terms], [gain], sums=1 if low else 0)


def pair_call(sc, parts):
    half, C, _ = parts[0][0].shape
    widths = [near.shape[2] for _, near in parts]
    N = sum(widths)

    def kernel(s, *refs):
        at = 0
        for p, width in enumerate(widths):
            total = refs[2 * p][0].astype(F32) + refs[2 * p + 1][0].astype(F32)
            refs[-1][:, at : at + width] = total.astype(BF)
            at += width

    return call(
        kernel,
        shape((half * C, N), BF),
        (half,),
        [pl.BlockSpec((1, C, width), lambda i, s: (i, 0, 0)) for width in widths for _ in range(2)],
        pl.BlockSpec((C, N), lambda i, s: (i, 0)),
        (half * C * N, 6 * half * C * N),
    )(sc, *[x for part in parts for x in part])


def stage(refs, x_ref):
    @pl.when(pl.program_id(0) == 0)
    def _():
        at = 0
        for ref in refs:
            x_ref[at : at + ref.shape[0]] = ref[...]
            at += ref.shape[0]


def staged(block):
    H, D = block[0].shape
    return [pl.BlockSpec((H, D), lambda c, s: (0, 0), pipeline_mode=pl.Buffered(1))] * 4, pltpu.VMEM((4 * H, D), BF)


def put_rows(refs, value):
    at = 0
    for ref in refs:
        ref[...] = value[at : at + ref.shape[0]].astype(BF)
        at += ref.shape[0]


def whole(dims):
    return pl.BlockSpec(dims, lambda *_: (0,) * len(dims), pipeline_mode=pl.Buffered(1))


def exp_low(values):
    return jnp.exp(jnp.minimum(values, 0.0))


def phi_of(values, low):
    return jnp.where(values > 0, values + 1.0, low)


def row_ids(count, begin):
    return begin + lax.broadcasted_iota(jnp.int32, (count, 1), 0)


CHIP, CORE, PLACE, VALID, ORDER = 0, 1, 2, 3, 4


def chip_block(s, j, chips):
    return lax.rem(s[CHIP] + j, chips)


def qkv_call(sc, j, chips, block, wq, wk, wv, prev):
    R, D = 2 * block[0].shape[0], block[0].shape[1]
    E = wq.shape[1]
    T = 2 * R * chips
    n = min(256, E)

    def kernel(s, *refs):
        wq_ref, wk_ref, wv_ref = refs[4:7]
        q_ref, k_ref, v_ref, c_ref, x_ref = refs[-5:]
        stage(refs[:4], x_ref)
        base = chip_block(s, j, chips) * 2 * R
        sums = jnp.zeros((1, n), F32)
        x = x_ref[...]
        q, k, v = (dot(x, ref[...]).astype(BF) for ref in (wq_ref, wk_ref, wv_ref))
        for i in range(2):
            off = pl.multiple_of((s[CORE] if i == 0 else 1 - s[CORE]) * R, R)
            rows, part = pl.ds(off, R), slice(i * R, (i + 1) * R)
            q_ref[rows] = q[part]
            k_ref[rows] = k[part]
            v_ref[rows] = v[part]
            keys = k[part].astype(F32)
            phi = jnp.where(row_ids(R, base + off) < s[VALID], phi_of(keys, exp_low(keys)), 0.0)
            sums = sums + jnp.sum(phi, axis=0, keepdims=True)
        c_ref[...] = sums

    rows, scratch = staged(block)
    cols = pl.BlockSpec((D, n), lambda c, s: (0, c))
    out = pl.BlockSpec((2 * R, n), lambda c, s: (chip_block(s, j, chips), c))
    o = shape((T, E), BF)
    extra = [pl.BlockSpec(memory_space=pl.ANY)] * 3 if prev else []
    return call(
        kernel,
        (o, o, o, shape((1, E), F32)),
        (E // n,),
        rows + [cols, cols, cols] + extra,
        [out, out, out, pl.BlockSpec((1, n), lambda c, s: (0, c))],
        (12 * R * D * E, 4 * R * D + 6 * D * E + 12 * R * E),
        scratch=[scratch],
        alias={8: 0, 9: 1, 10: 2} if prev else None,
    )(sc, *block, wq, wk, wv, *(prev or ()))


def grad_inner_call(sc, block, wd):
    R, D = 2 * block[0].shape[0], block[0].shape[1]
    F = wd.shape[0]
    n = min(512, F)

    def kernel(s, *refs):
        w_ref, o_ref, x_ref = refs[4:]
        stage(refs[:4], x_ref)
        o_ref[...] = dot_nt(x_ref[...], w_ref[...]).astype(BF)

    rows, scratch = staged(block)
    return call(
        kernel,
        shape((2 * R, F), BF),
        (F // n,),
        rows + [pl.BlockSpec((n, D), lambda c, s: (c, 0))],
        pl.BlockSpec((2 * R, n), lambda c, s: (0, c)),
        (4 * R * D * F, 4 * R * D + 2 * D * F + 4 * R * F),
        scratch=[scratch],
    )(sc, *block, wd)


def ffn_a_call(sc, block, wg, wu, gi):
    R, D = 2 * block[0].shape[0], block[0].shape[1]
    F = wg.shape[1]
    n = min(512, F)

    def kernel(s, *refs):
        wg_ref, wu_ref, gi_ref, inner_ref, gg_ref, gu_ref, x_ref = refs[4:]
        stage(refs[:4], x_ref)
        for i in range(2):
            rows = slice(i * R, (i + 1) * R)
            g = dot(x_ref[rows], wg_ref[...])
            u = dot(x_ref[rows], wu_ref[...])
            sig = 0.5 * jnp.tanh(0.5 * g) + 0.5
            silu = g * sig
            inner_ref[rows] = (silu * u).astype(BF)
            gi_rows = gi_ref[rows].astype(F32)
            gu_ref[rows] = (gi_rows * silu).astype(BF)
            gg_ref[rows] = (gi_rows * u * (sig + silu * (1.0 - sig))).astype(BF)

    o = shape((2 * R, F), BF)
    rows, scratch = staged(block)
    cols = pl.BlockSpec((D, n), lambda c, s: (0, c))
    out = pl.BlockSpec((2 * R, n), lambda c, s: (0, c))
    return call(
        kernel,
        (o, o, o),
        (F // n,),
        rows + [cols, cols, out],
        [out, out, out],
        (8 * R * D * F, 4 * R * D + 4 * D * F + 16 * R * F),
        scratch=[scratch],
    )(sc, *block, wg, wu, gi)


def halves_out(R, D, n):
    H = R // 2
    return (shape((H, D), BF),) * 4, [pl.BlockSpec((H, n), lambda c, s: (0, c))] * 4


def ffn_b_call(sc, gg, gu, wg, wu):
    R2, F = gg.shape
    R = R2 // 2
    D = wg.shape[0]
    n = min(512, D)

    def kernel(s, gg_ref, gu_ref, wg_ref, wu_ref, *outs):
        put_rows(outs, dot_nt(gg_ref[...], wg_ref[...]) + dot_nt(gu_ref[...], wu_ref[...]))

    rows = pl.BlockSpec((R2, F), lambda c, s: (0, 0))
    cols = pl.BlockSpec((n, F), lambda c, s: (c, 0))
    shapes, specs = halves_out(R, D, n)
    return call(
        kernel,
        shapes,
        (D // n,),
        [rows, rows, cols, cols],
        specs,
        (8 * R * D * F, 8 * R * F + 4 * D * F + 4 * R * D),
    )(sc, gg, gu, wg, wu)


def down_call(sc, inner, wd):
    R2, F = inner.shape
    R = R2 // 2
    D = wd.shape[1]
    n = min(512, D)

    def kernel(s, x_ref, w_ref, *outs):
        put_rows(outs, dot(x_ref[...], w_ref[...]))

    shapes, specs = halves_out(R, D, n)
    return call(
        kernel,
        shapes,
        (D // n,),
        [pl.BlockSpec((R2, F), lambda c, s: (0, 0)), pl.BlockSpec((F, n), lambda c, s: (0, c))],
        specs,
        (4 * R * D * F, 4 * R * F + 2 * D * F + 4 * R * D),
    )(sc, inner, wd)


def wgrad_call(sc, blocks, gs, ndp, pieces):
    xs = [x for block in blocks for x in block]
    H, D = xs[0].shape
    nx = len(xs)
    C = D // ndp
    nb = len(gs[0])
    widths = [parts[0].shape[1] for parts in gs]
    T = H * nx
    rb = T // nb
    N = sum(widths)
    flat = [g for parts in gs for g in parts]
    far = ndp // 2 if pieces else 0
    sizes = [far // max(pieces, 1)] * pieces + [ndp - far]
    begins = [p * sizes[0] for p in range(len(sizes))]

    def kernel(s, *refs):
        x_refs, g_refs, o_refs, xt = refs[:nx], refs[nx : nx + len(flat)], refs[nx + len(flat) : -1], refs[-1]
        j = pl.program_id(0)
        for p in range(nx):
            xt[:, p * H : (p + 1) * H] = x_refs[p][...].T
        at = 0
        for w, width in enumerate(widths):
            acc = None
            for b in range(nb):
                term = dot(xt[:, b * rb : (b + 1) * rb], g_refs[w * nb + b][...])
                acc = term if acc is None else acc + term
            cols = slice(at, at + width)
            at += width
            low = acc.astype(BF)
            for o_ref, begin, size in zip(o_refs, begins, sizes):

                @pl.when((j >= begin) & (j < begin + size))
                def _():
                    o_ref[0, :, cols] = low

    def spec(begin, size):
        return pl.BlockSpec((1, C, N), lambda j, s: (jnp.clip(j - begin, 0, size - 1), 0, 0))

    order = (lambda j, s: (0, s[ORDER + j])) if pieces else (lambda j, s: (0, j))
    return call(
        kernel,
        tuple(shape((size, C, N), BF) for size in sizes),
        (ndp,),
        [pl.BlockSpec((H, C), order)] * nx + [whole(g.shape) for g in flat],
        [spec(begin, size) for begin, size in zip(begins, sizes)],
        (2 * T * D * N, 2 * T * (D + N) + 2 * D * N),
        scratch=[pltpu.VMEM((C, T), BF)],
    )(sc, *xs, *flat)


def attn_fwd_call(sc, q, k, v, h0, hh):
    T = q.shape[0]
    E = hh * HEAD
    B = min(512, T)
    nb = T // B
    c = HEAD**-0.5 * LOG2E

    def kernel(s, q_ref, k_ref, v_ref, o_ref, lse_ref):
        valid = s[VALID]
        for i in range(nb):
            qb = q_ref[i * B : (i + 1) * B]
            parts = []
            for j in range(i + 1):
                x = dot_nt(k_ref[j * B : (j + 1) * B], qb)
                if j == i:
                    u = lax.broadcasted_iota(jnp.int32, (B, B), 0)
                    t = lax.broadcasted_iota(jnp.int32, (B, B), 1)
                    x = jnp.where(u <= t, x, NEG)
                if (j + 1) * B > T // 2:
                    x = jnp.where(row_ids(B, j * B) < valid, x, NEG)
                parts.append(x)
            top = jnp.max(parts[0], axis=0, keepdims=True)
            for x in parts[1:]:
                top = jnp.maximum(top, jnp.max(x, axis=0, keepdims=True))
            top = top * c
            total = jnp.zeros((1, B), F32)
            acc = jnp.zeros((HEAD, B), F32)
            for j, x in enumerate(parts):
                p = jnp.exp2(x * c - top)
                total = total + jnp.sum(p, axis=0, keepdims=True)
                acc = acc + dot_tn(v_ref[j * B : (j + 1) * B], p.astype(BF))
            o_ref[i * B : (i + 1) * B] = (acc * (1.0 / total)).T
            lse_ref[0, :, i * B : (i + 1) * B] = top + jnp.log2(total)

    head = pl.BlockSpec((T, HEAD), lambda h, s: (0, h0 + h))
    out = pl.BlockSpec((T, HEAD), lambda h, s: (0, h))
    return call(
        kernel,
        (shape((T, E), F32), shape((hh, 1, T), F32)),
        (hh,),
        [head, head, head],
        [out, pl.BlockSpec((1, 1, T), lambda h, s: (h, 0, 0))],
        (6 * T * T * E, 10 * T * E),
    )(sc, q, k, v)


def attn_bwd_call(sc, q, k, v, do, attended, h0, part):
    lo, lse = attended
    nh = 1
    T = q.shape[0]
    B = min(512, T)
    nb = T // B
    scale = HEAD**-0.5
    c = scale * LOG2E

    def kernel(s, q_ref, k_ref, v_ref, do_ref, lo_ref, lse_ref, dq_ref, dk_ref, dv_ref, delta):
        valid = s[VALID]
        ones = jnp.ones((8, HEAD), F32)
        for i in range(nb):
            rows = slice(i * B, (i + 1) * B)
            prod = do_ref[rows].astype(F32) * lo_ref[rows]
            delta[:, rows] = lax.dot_general(
                ones,
                prod,
                (((1,), (1,)), ((), ())),
                precision=lax.Precision.HIGHEST,
                preferred_element_type=F32,
            )
        dq_ref[...] = jnp.zeros_like(dq_ref)
        for j in range(nb):
            kb = k_ref[j * B : (j + 1) * B]
            vb = v_ref[j * B : (j + 1) * B]
            dk = jnp.zeros((B, HEAD), F32)
            dv = jnp.zeros((B, HEAD), F32)
            for i in range(j, nb):
                rows = slice(i * B, (i + 1) * B)
                qb = q_ref[rows]
                dob = do_ref[rows]
                p = jnp.exp2(dot_nt(kb, qb) * c - lse_ref[0, :, rows])
                if i == j:
                    u = lax.broadcasted_iota(jnp.int32, (B, B), 0)
                    t = lax.broadcasted_iota(jnp.int32, (B, B), 1)
                    p = jnp.where(u <= t, p, 0.0)
                if (j + 1) * B > T // 2:
                    p = jnp.where(row_ids(B, j * B) < valid, p, 0.0)
                ds = (p * (dot_nt(vb, dob) - delta[0:1, rows])).astype(BF)
                dv = dv + dot(p.astype(BF), dob)
                dk = dk + dot(ds, qb)
                dq_ref[rows] += dot_tn(ds, kb)
            dk_ref[j * B : (j + 1) * B] = dk * scale
            dv_ref[j * B : (j + 1) * B] = dv
        dq_ref[...] *= scale

    o = shape((T, nh * HEAD), F32)
    head = pl.BlockSpec((T, HEAD), lambda h, s: (0, h0 + h))
    out = pl.BlockSpec((T, HEAD), lambda h, s: (0, h))
    return call(
        kernel,
        (o, o, o),
        (nh,),
        [head] * 4
        + [pl.BlockSpec((T, HEAD), lambda h, s: (0, part)), pl.BlockSpec((1, 1, T), lambda h, s: (part, 0, 0))],
        [out, out, out],
        (12 * T * T * HEAD * nh, 26 * T * HEAD * nh),
        scratch=[pltpu.VMEM((8, T), F32)],
    )(sc, q, k, v, do, lo, lse)


def maps_call(sc, k, v, gathered):
    T, E = k.shape
    hh = E // HEAD
    ndp = gathered.shape[0]

    def kernel(s, k_ref, v_ref, g_ref, maps_ref, norm_ref):
        h = pl.program_id(0)
        norm = jnp.zeros((1, HEAD), F32)
        for a in range(ndp - 1):
            after = (norm + g_ref[shared_at(s, a, ndp), pl.ds(h, 1)]) * g_ref[shared_at(s, a + 1, ndp), hh : hh + 1]
            norm = jnp.where(a < s[PLACE], after, norm)
        norm_ref[0] = norm
        k = k_ref[...].astype(F32)
        phi = jnp.where(row_ids(T, 0) < s[VALID], phi_of(k, exp_low(k)), 0.0)
        den = jnp.maximum(jnp.sum(phi * norm, axis=1, keepdims=True), 1.0)
        low = phi.astype(BF)
        maps_ref[0, 0] = dot_tn((phi * (1.0 / den)).astype(BF), low).astype(BF)
        maps_ref[1, 0] = dot_tn(low, v_ref[...]).astype(BF)

    head = pl.BlockSpec((T, HEAD), lambda h, s: (0, h))
    return call(
        kernel,
        (shape((2, hh, HEAD, HEAD), BF), shape((hh, 1, HEAD), F32)),
        (hh,),
        [head, head, whole(gathered.shape)],
        [
            pl.BlockSpec((2, 1, HEAD, HEAD), lambda h, s: (0, h, 0, 0)),
            pl.BlockSpec((1, 1, HEAD), lambda h, s: (h, 0, 0)),
        ],
        (4 * T * E * HEAD, 4 * T * E),
    )(sc, k, v, gathered)


def times_state(g, state):
    high = state.astype(BF)
    return dot(g, high) + dot(g, (state - high.astype(F32)).astype(BF))


def chain_call(sc, gathered, maps):
    ndp, _, hh = maps.shape[:3]

    def kernel(s, g_ref, maps_ref, m_ref):
        state = [jnp.zeros((HEAD, HEAD), F32) for _ in range(hh)]
        for a in range(ndp - 1):
            keep = g_ref[shared_at(s, a + 1, ndp), hh : hh + 1]
            before = a < s[PLACE]
            for h in range(hh):
                after = state[h] - times_state(maps_ref[a, 0, h], state[h])
                after = (after + maps_ref[a, 1, h].astype(F32)) * keep
                state[h] = jnp.where(before, after, state[h])
        for h in range(hh):
            m_ref[h] = state[h]

    return call(
        kernel,
        shape((hh, HEAD, HEAD), F32),
        (1,),
        [whole(gathered.shape), whole(maps.shape)],
        whole((hh, HEAD, HEAD)),
        (4e8, 2 * maps.size),
    )(sc, gathered, maps)


def mixout_call(sc, j, chips, q, locals_, memory, norm, mix, wo):
    T, E = q.shape
    hh = E // HEAD
    D = wo.shape[1]
    R = T // chips // 2
    n = min(512, D)
    groups = len(locals_)
    per = hh // groups

    def kernel(s, q_ref, *rest):
        l_refs = rest[:groups]
        m_ref, n_ref, mix_ref, w_ref, *outs, mixed_ref, diff_ref = rest[groups:]

        @pl.when(pl.program_id(0) == 0)
        def _():
            for i in range(2):
                off = pl.multiple_of((s[CORE] if i == 0 else 1 - s[CORE]) * R, R)
                for h in range(hh):
                    cols = slice(h * HEAD, (h + 1) * HEAD)
                    qv = q_ref[pl.ds(off, R), cols].astype(F32)
                    phi = phi_of(qv, exp_low(qv))
                    den = jnp.maximum(jnp.sum(phi * n_ref[h], axis=1, keepdims=True), 1.0)
                    read = dot(phi.astype(BF), m_ref[h].astype(BF)) * (1.0 / den)
                    local = l_refs[h // per][pl.ds(off, R), h % per * HEAD : (h % per + 1) * HEAD]
                    diff = read - local
                    mixed = local + mix_ref[h] * diff
                    diff_ref[i * R : (i + 1) * R, cols] = diff.astype(BF)
                    mixed_ref[i * R : (i + 1) * R, cols] = mixed.astype(BF)

        put_rows(outs, dot(mixed_ref[...], w_ref[...]))

    rows = pl.BlockSpec((2 * R, E), lambda c, s: (chip_block(s, j, chips), 0))
    shapes, specs = halves_out(R, D, n)
    rel = pl.BlockSpec((2 * R, E), lambda c, s: (0, 0))
    return call(
        kernel,
        shapes + (shape((2 * R, E), BF), shape((2 * R, E), BF)),
        (D // n,),
        [rows]
        + [pl.BlockSpec((2 * R, per * HEAD), lambda c, s: (chip_block(s, j, chips), 0))] * groups
        + [whole(memory.shape), whole(norm.shape), whole(mix.shape), pl.BlockSpec((E, n), lambda c, s: (0, c))],
        specs + [rel, rel],
        (4 * R * E * D + 8 * R * E * HEAD, 20 * R * E + 2 * E * D + 4 * R * D),
    )(sc, q, *locals_, memory, norm, mix, wo)


def gradmix_call(sc, j, chips, block, wo, diff, q, norm, mix, prev):
    R, D = 2 * block[0].shape[0], block[0].shape[1]
    E = wo.shape[0]
    hh = E // HEAD
    T = 2 * R * chips
    n = min(256, E)
    per = n // HEAD

    def kernel(s, *refs):
        w_ref, diff_ref, q_ref, n_ref, mix_ref = refs[4:9]
        do_ref, gm_ref, cot_ref, b_ref, x_ref = refs[-5:]
        stage(refs[:4], x_ref)
        sums = jnp.zeros((1, n), F32)
        cots = [jnp.zeros((HEAD, HEAD), F32) for _ in range(per)]
        for i in range(2):
            off = pl.multiple_of((s[CORE] if i == 0 else 1 - s[CORE]) * R, R)
            grad = dot_nt(x_ref[i * R : (i + 1) * R], w_ref[...])
            sums = sums + jnp.sum(grad * diff_ref[i * R : (i + 1) * R].astype(F32), axis=0, keepdims=True)
            for h in range(per):
                cols = slice(h * HEAD, (h + 1) * HEAD)
                part = grad[:, cols]
                grad_read = part * mix_ref[h]
                do_ref[pl.ds(off, R), cols] = (part - grad_read).astype(BF)
                gm_ref[pl.ds(off, R), cols] = grad_read.astype(BF)
                qv = q_ref[pl.ds(off, R), cols].astype(F32)
                phi = phi_of(qv, exp_low(qv))
                den = jnp.maximum(jnp.sum(phi * n_ref[h], axis=1, keepdims=True), 1.0)
                cots[h] = cots[h] + dot_tn(phi.astype(BF), (grad_read * (1.0 / den)).astype(BF))
        for h in range(per):
            cot_ref[h] = cots[h]
        b_ref[...] = sums

    rows, scratch = staged(block)
    place = pl.BlockSpec((2 * R, n), lambda c, s: (chip_block(s, j, chips), c))
    per_head = pl.BlockSpec((per, 1, HEAD), lambda c, s: (c, 0, 0))
    o = shape((T, E), BF)
    extra = [pl.BlockSpec(memory_space=pl.ANY)] * 2 if prev else []
    return call(
        kernel,
        (o, o, shape((hh, HEAD, HEAD), F32), shape((1, E), F32)),
        (E // n,),
        rows
        + [pl.BlockSpec((n, D), lambda c, s: (c, 0)), pl.BlockSpec((2 * R, n), lambda c, s: (0, c)), place, per_head, per_head]
        + extra,
        [place, place, pl.BlockSpec((per, HEAD, HEAD), lambda c, s: (c, 0, 0)), pl.BlockSpec((1, n), lambda c, s: (0, c))],
        (4 * R * E * D + 4 * R * E * HEAD, 4 * R * D + 2 * E * D + 16 * R * E),
        scratch=[scratch],
        alias={10: 0, 11: 1} if prev else None,
    )(sc, *block, wo, diff, q, norm, mix, *(prev or ()))


def memory_rows(q, k, grad_read, live, memory, norm, cot):
    low_q = exp_low(q)
    low_k = exp_low(k)
    phi_q = phi_of(q, low_q)
    phi_k = jnp.where(live, phi_of(k, low_k), 0.0)
    raw_q = jnp.sum(phi_q * norm, axis=1, keepdims=True)
    raw_k = jnp.sum(phi_k * norm, axis=1, keepdims=True)
    inv_q = 1.0 / jnp.maximum(raw_q, 1.0)
    inv_k = 1.0 / jnp.maximum(raw_k, 1.0)
    read = dot(phi_q.astype(BF), memory)
    recalled = dot(phi_k.astype(BF), memory) * inv_k
    pushed = dot(phi_k.astype(BF), cot)
    scaled = grad_read * inv_q
    w_q = jnp.where(raw_q > 1.0, -jnp.sum(scaled * read, axis=1, keepdims=True) * inv_q, 0.0)
    w_k = jnp.where(raw_k > 1.0, jnp.sum(pushed * recalled, axis=1, keepdims=True) * inv_k, 0.0)
    return low_q, low_k, phi_q, phi_k, inv_k, recalled, pushed, scaled, w_q, w_k


def memory_cot_call(sc, gathered, maps, cots, q, k, grad_read, memory, norm):
    T, E = q.shape
    hh = E // HEAD
    ndp = maps.shape[0]
    B = min(512, T)

    def kernel(s, g_ref, maps_ref, cots_ref, q_ref, k_ref, gm_ref, m_ref, n_ref, x_ref, nb_ref):
        cot = jnp.zeros((HEAD, HEAD), F32)
        for a in range(ndp - 1, 0, -1):
            before = cot - times_state(maps_ref[a, 0, 0], cot) + cots_ref[shared_at(s, a, ndp), 0].astype(F32)
            cot = jnp.where(a > s[PLACE], before * g_ref[shared_at(s, a, ndp), hh : hh + 1], cot)
        x_ref[0] = cot
        cot = cot.astype(BF)
        memory = m_ref[0].astype(BF)
        sums = jnp.zeros((1, HEAD), F32)
        for i in range(T // B):
            rows = slice(i * B, (i + 1) * B)
            live = row_ids(B, i * B) < s[VALID]
            terms = memory_rows(
                q_ref[rows].astype(F32), k_ref[rows].astype(F32), gm_ref[rows].astype(F32), live, memory, n_ref[0], cot
            )
            sums = sums + jnp.sum(terms[2] * terms[8] + terms[3] * terms[9], axis=0, keepdims=True)
        nb_ref[0] = sums

    head = pl.BlockSpec((T, HEAD), lambda h, s: (0, h))
    square = pl.BlockSpec((1, HEAD, HEAD), lambda h, s: (h, 0, 0))
    row = pl.BlockSpec((1, 1, HEAD), lambda h, s: (h, 0, 0))
    return call(
        kernel,
        (shape((hh, HEAD, HEAD), F32), shape((hh, 1, HEAD), F32)),
        (hh,),
        [
            whole(gathered.shape),
            pl.BlockSpec((ndp, 1, 1, HEAD, HEAD), lambda h, s: (0, 0, h, 0, 0)),
            pl.BlockSpec((ndp, 1, HEAD, HEAD), lambda h, s: (0, h, 0, 0)),
            head,
            head,
            head,
            square,
            row,
        ],
        [square, row],
        (8 * T * E * HEAD, 6 * T * E),
    )(sc, gathered, maps, cots, q, k, grad_read, memory, norm)


def combine_call(sc, chips, q, k, v, grad_read, local_grads, memory, norm, cot, gathered, norm_parts):
    T, E = q.shape
    hh = E // HEAD
    R = T // chips // 2
    ndp = gathered.shape[0]
    per = local_grads[0][0].shape[1] // HEAD
    groups = len(local_grads)

    def kernel(s, q_ref, k_ref, v_ref, gm_ref, *rest):
        local_refs = rest[: 3 * groups]
        m_ref, n_ref, x_ref, g_ref, nb_ref, gq_ref, gk_ref, gv_ref = rest[3 * groups :]
        begin = piece(pl.program_id(0), s) * R
        live = row_ids(R, begin) < s[VALID]
        for h in range(hh):
            cols = slice(h * HEAD, (h + 1) * HEAD)
            part = slice(h % per * HEAD, (h % per + 1) * HEAD)
            dq, dk, dv = (ref[:, part] for ref in local_refs[3 * (h // per) : 3 * (h // per) + 3])
            norm_cot = jnp.zeros((1, HEAD), F32)
            for a in range(ndp - 1, 0, -1):
                other = shared_at(s, a, ndp)
                before = (norm_cot + nb_ref[other, h : h + 1]) * g_ref[other, hh : hh + 1]
                norm_cot = jnp.where(a > s[PLACE], before, norm_cot)
            memory = m_ref[h].astype(BF)
            cot = x_ref[h].astype(BF)
            norm = n_ref[h]
            low_q, low_k, _, _, inv_k, recalled, pushed, scaled, w_q, w_k = memory_rows(
                q_ref[:, cols].astype(F32), k_ref[:, cols].astype(F32), gm_ref[:, cols].astype(F32), live, memory, norm, cot
            )
            grad_phi_q = dot_nt(scaled.astype(BF), memory) + w_q * norm
            grad_phi_k = (
                dot_nt((v_ref[:, cols].astype(F32) - recalled).astype(BF), cot)
                - dot_nt((pushed * inv_k).astype(BF), memory)
                + w_k * norm
                + norm_cot
            )
            gq_ref[:, cols] = (dq + grad_phi_q * low_q).astype(BF)
            gk_ref[:, cols] = (dk + jnp.where(live, grad_phi_k * low_k, 0.0)).astype(BF)
            gv_ref[:, cols] = (dv + pushed).astype(BF)

    def piece(p, s):
        core = lax.rem(s[CORE] + p, 2)
        return chip_block(s, p // 2, chips) * 2 + core

    rows = pl.BlockSpec((R, E), lambda p, s: (piece(p, s), 0))
    part_rows = pl.BlockSpec((R, per * HEAD), lambda p, s: (piece(p, s), 0))
    out = pl.BlockSpec((R, E), lambda p, s: (p, 0))
    o = shape((T, E), BF)
    return call(
        kernel,
        (o, o, o),
        (2 * chips,),
        [rows] * 4 + [part_rows] * (3 * groups) + [whole(x.shape) for x in (memory, norm, cot, gathered, norm_parts)],
        [out, out, out],
        (14 * T * E * HEAD, 26 * T * E),
    )(sc, q, k, v, grad_read, *[x for group in local_grads for x in group], memory, norm, cot, gathered, norm_parts)


def grad_normed_call(sc, j, gq, gk, gv, wq, wk, wv, block, chips):
    T, E = gq.shape
    R = T // chips // 2
    D = wq.shape[0]
    n = min(512, D)

    def kernel(s, gq_ref, gk_ref, gv_ref, wq_ref, wk_ref, wv_ref, *rest):
        grad = dot_nt(gq_ref[...], wq_ref[...]) + dot_nt(gk_ref[...], wk_ref[...]) + dot_nt(gv_ref[...], wv_ref[...])
        put_rows(rest[4:8], grad)
        sums, at = 0.0, 0
        for ref in rest[:4]:
            part = grad[at : at + ref.shape[0]] * ref[...].astype(F32)
            sums = sums + jnp.sum(part, axis=0, keepdims=True)
            at += ref.shape[0]
        rest[8][...] = sums

    rows = pl.BlockSpec((2 * R, E), lambda c, s: (j, 0))
    cols = pl.BlockSpec((n, E), lambda c, s: (c, 0))
    shapes, specs = halves_out(R, D, n)
    return call(
        kernel,
        shapes + (shape((1, D), F32),),
        (D // n,),
        [rows, rows, rows, cols, cols, cols] + specs,
        specs + [pl.BlockSpec((1, n), lambda c, s: (0, c))],
        (12 * R * D * E, 12 * R * E + 6 * D * E + 4 * R * D),
    )(sc, gq, gk, gv, wq, wk, wv, *block)


def swap_core(pair):
    count = lax.axis_size("tensor")
    return tuple(lax.ppermute(x, "tensor", [(i, i ^ 1) for i in range(count)]) for x in pair)


def shift_chip(pair, j):
    count = lax.axis_size("tensor")
    return tuple(lax.ppermute(x, "tensor", [(i, (i + 2 * j) % count) for i in range(count)]) for x in pair)


def with_swapped(pair):
    return tuple(pair) + swap_core(pair)


def chunk_order(me, ndp):
    parity = me % 2
    order = [2 * i + (1 - parity) for i in range(ndp // 2)] + [2 * i + parity for i in range(ndp // 2)]
    return jnp.stack(order)


def exchange_x(x):
    return lax.ppermute(x, "dp", [(i, i ^ 1) for i in range(lax.axis_size("dp"))])


def sum_z(x):
    ndp = lax.axis_size("dp")
    groups = [list(range(0, ndp, 2)), list(range(1, ndp, 2))]
    return lax.psum_scatter(x, "dp", scatter_dimension=0, axis_index_groups=groups, tiled=True)


def finish_x(both, parity):
    C = both.shape[0] // 2
    got = exchange_x(lax.dynamic_slice_in_dim(both, (1 - parity) * C, C, 0))
    return got.astype(F32) + lax.dynamic_slice_in_dim(both, parity * C, C, 0).astype(F32)


def share_steps(x):
    count = lax.axis_size("dp")
    steps = [1 << bit for bit in range(1, count.bit_length() - 1)] + [1]
    x = x[None]
    for step in steps:
        x = jnp.concatenate([x, lax.ppermute(x, "dp", [(i, i ^ step) for i in range(count)])])
        yield x


def shared_at(s, a, count):
    apart = a ^ s[PLACE]
    return (apart >> 1) + (apart & 1) * (count // 2)


def share_over_dp(x):
    return list(share_steps(x))[-1]


def sum_everywhere(x):
    for axis in ("tensor", "dp"):
        count, step = lax.axis_size(axis), 1
        while step < count:
            x = x + lax.ppermute(x, axis, [(i, i ^ step) for i in range(count)])
            step *= 2
    return x


def body(
    tokens,
    gain1,
    w_query,
    w_key,
    w_value,
    w_out,
    gate_bias,
    gain2,
    w_gate,
    w_up,
    w_down,
    seg_starts,
    seg_valid,
    cotangent,
):
    count = lax.axis_size("tensor")
    ndp = lax.axis_size("dp")
    chips = count // 2
    hh = gate_bias.shape[0]
    E = hh * HEAD
    here = lax.axis_index("tensor")
    place = lax.axis_index("dp")
    sc = jnp.concatenate(
        [
            jnp.stack([here // 2, here % 2, place]).astype(jnp.int32),
            seg_valid.astype(jnp.int32),
            chunk_order(place, ndp).astype(jnp.int32),
        ]
    )
    keep = (1 - seg_starts[0]).astype(F32)
    sig_bias = jax.nn.sigmoid(gate_bias)
    mix = jnp.broadcast_to(sig_bias[:, None, None], (hh, 1, HEAD))

    ORDERED.clear()
    per = max(1, hh // 2)

    gain1 = gain1[None]
    gain2 = gain2[None]
    chip_range = range(1, chips)
    parity = place % 2
    R = tokens.shape[0]
    four = min(4, ndp // 2)

    def norm1_kernel(x_ref, g_ref, o_ref):
        o_ref[...] = (unit_rows(x_ref[...].astype(F32))[0] * g_ref[...]).astype(BF)

    normed1 = rows_call(norm1_kernel, [[BF]], sc, [tokens], [gain1])[0]
    rows1 = [with_swapped(normed1)]
    far1 = [shift_chip(normed1, -j) for j in chip_range]
    own_cot = (cotangent[: R // 2], cotangent[R // 2 :])
    cot_rows = [with_swapped(own_cot)]
    *qkv, sums = qkv_call(sc, 0, chips, rows1[0], w_query, w_key, w_value, None)
    *far1, own_cot = hold_pairs(sc, far1 + [own_cot])
    far_cot = [shift_chip(own_cot, -j) for j in chip_range]
    for j in chip_range:
        rows1.append(with_swapped(far1[j - 1]))
        *qkv, column_sums = qkv_call(sc, j, chips, rows1[j], w_query, w_key, w_value, qkv)
        sums = sums + column_sums
    q, k, v = qkv

    own = jnp.concatenate([sums.reshape(hh, HEAD), jnp.full((8 - hh, HEAD), keep, F32)])
    gathered = share_over_dp(own)
    maps, norm = maps_call(sc, k, v, gathered)
    all_maps = lax.all_gather(maps, "dp")
    attended = [attn_fwd_call(sc, q, k, v, h, per) for h in range(0, hh, per)]
    far_cot = hold_pairs(sc, far_cot)
    cot_rows += [with_swapped(pair) for pair in far_cot]
    grad_inner = [grad_inner_call(sc, block, w_down) for block in cot_rows]
    memory = chain_call(sc, gathered, all_maps)

    mixed, diff = [None] * chips, [None] * chips

    def mixout(j):
        *block, mixed[j], diff[j] = mixout_call(sc, j, chips, q, [one[0] for one in attended], memory, norm, mix, w_out)
        return block

    def scatter(make):
        blocks = [make(j) for j in chip_range] + [make(0)]
        got = []
        for j in chip_range:
            block = blocks[j - 1]
            sums = add_rows(sc, [tuple(block[:2]), swap_core(block[2:])], True)
            got.append(shift_chip(sums, j))
        block = blocks[-1]
        return [tuple(block[:2]), swap_core(block[2:]), *got]

    hidden, normed2 = norm_call(sc, [tokens, *scatter(mixout)], gain2)
    rows2 = [with_swapped(normed2)]
    far2 = [shift_chip(normed2, -j) for j in chip_range]
    ffn = [ffn_a_call(sc, rows2[0], w_gate, w_up, grad_inner[0])]
    far2 = hold_pairs(sc, far2)
    for j in chip_range:
        rows2.append(with_swapped(far2[j - 1]))
        ffn.append(ffn_a_call(sc, rows2[j], w_gate, w_up, grad_inner[j]))
    inner, grad_gate, grad_up = zip(*ffn)

    (w_up_parts,) = wgrad_call(sc, rows2, [grad_up], ndp, 0)
    both_up = sum_z(w_up_parts.reshape((-1, w_up_parts.shape[2])))
    back = scatter(lambda j: ffn_b_call(sc, grad_gate[j], grad_up[j], w_gate, w_up))
    far_gate, near_gate = wgrad_call(sc, rows2, [grad_gate], ndp, 1)
    far_gate = exchange_x(far_gate)
    far_down, near_down = wgrad_call(sc, cot_rows, [inner], ndp, 1)
    far_down = exchange_x(far_down)
    grad_hidden, grad_low, gain2_part = norm_back_call(sc, cotangent, hidden, back, gain2, True)
    grad_rows = [with_swapped(grad_low)]
    far_grad = [shift_chip(grad_low, -j) for j in chip_range]
    down_far = [down_call(sc, inner[j], w_down) for j in chip_range]
    *grads, cot_part, bias_part = gradmix_call(sc, 0, chips, grad_rows[0], w_out, diff[0], q, norm, mix, None)
    down_near = down_call(sc, inner[0], w_down)
    far_grad = hold_pairs(sc, far_grad)
    pair_gate = pair_call(sc, [(far_gate, near_gate)])
    sum_gate = sum_z(pair_gate)
    require(both_up)
    sum_up = finish_x(both_up, parity)
    for j in chip_range:
        grad_rows.append(with_swapped(far_grad[j - 1]))
        *grads, cot_j, bias_j = gradmix_call(sc, j, chips, grad_rows[j], w_out, diff[j], q, norm, mix, grads)
        cot_part = cot_part + cot_j
        bias_part = bias_part + bias_j
    down_blocks = iter(down_far + [down_near])
    down = scatter(lambda j: next(down_blocks))
    grad_local, grad_read = grads

    local_grads = []
    steps = share_steps(cot_part.astype(BF))
    all_cots = None
    for h in range(hh):
        local_grads.append(attn_bwd_call(sc, q, k, v, grad_local, attended[h // per], h, h % per))
        if h in (0, max(2, hh - 2)):
            all_cots = next(steps)
            require(all_cots)
    for all_cots in steps:
        pass
    pair_down = pair_call(sc, [(far_down, near_down)])
    sum_down = sum_z(pair_down)
    memory_cot, norm_part = memory_cot_call(sc, gathered, all_maps, all_cots, q, k, grad_read, memory, norm)
    steps = share_steps(jnp.concatenate([norm_part.reshape(hh, HEAD), jnp.zeros((8 - hh, HEAD), F32)]))
    require(next(steps))
    far_out, near_out = wgrad_call(sc, grad_rows, [mixed], ndp, 1)
    far_out = exchange_x(far_out)
    for norm_parts in steps:
        pass
    require(sum_gate)
    gq, gk, gv = combine_call(
        sc, chips, q, k, v, grad_read, local_grads, memory, norm, memory_cot, gathered, norm_parts
    )
    gain1_sums = []

    def back_rows(j):
        *block, sums = grad_normed_call(sc, j, gq, gk, gv, w_query, w_key, w_value, rows1[j], chips)
        gain1_sums.append(sums)
        return block

    parts1 = {}

    def make1(name, grad):
        far, near = wgrad_call(sc, rows1, [[grad]], ndp, 1)
        parts1[name] = exchange_x(far), near

    make1("v", gv)
    make1("k", gk)
    output = add_rows(sc, [hidden, *down], False)
    back1 = scatter(back_rows)
    require(sum_down)
    sum_ovk = sum_z(pair_call(sc, [(far_out, near_out), parts1["v"], parts1["k"]]))
    make1("q", gq)
    (grad_tokens,) = norm_back_call(sc, grad_hidden, tokens, back1, gain1, False)
    require(sum_ovk)
    sum_ovk = sum_ovk.astype(F32)
    sum_query = sum_z(pair_call(sc, [parts1["q"]])).astype(F32)
    gain1_part = sum(gain1_sums) / gain1

    bias_here = jnp.sum(bias_part.reshape(hh, HEAD), axis=1) * sig_bias * (1.0 - sig_bias)
    bias_full = lax.dynamic_update_slice(jnp.zeros((HEADS,), F32), bias_here, (here * hh,))
    small = sum_everywhere(jnp.concatenate([gain1_part[0], gain2_part[0], bias_full]))
    D = gain1.shape[1]
    return (
        output,
        grad_tokens,
        small[:D],
        sum_query,
        sum_ovk[:, 2 * E :],
        sum_ovk[:, E : 2 * E],
        sum_ovk[:, :E].T,
        small[2 * D :],
        small[D : 2 * D],
        sum_gate.astype(F32),
        sum_up,
        sum_down.astype(F32).T,
    )


def solution(mesh):
    rows = P(("dp", "tensor"), None)
    return jax.shard_map(
        body,
        mesh=mesh,
        in_specs=(
            rows,
            P(),
            P(None, "tensor"),
            P(None, "tensor"),
            P(None, "tensor"),
            P("tensor", None),
            P("tensor"),
            P(),
            P(None, "tensor"),
            P(None, "tensor"),
            P("tensor", None),
            P("dp"),
            P("dp"),
            rows,
        ),
        out_specs=(
            rows,
            rows,
            P(),
            P("dp", "tensor"),
            P("dp", "tensor"),
            P("dp", "tensor"),
            P("tensor", "dp"),
            P(),
            P(),
            P("dp", "tensor"),
            P("dp", "tensor"),
            P("tensor", "dp"),
        ),
        check_vma=False,
    )
```

```python
import jax
import jax.numpy as jnp
from jax import lax
from jax.experimental import pallas as pl
from jax.experimental.pallas import tpu as pltpu
from jax.sharding import PartitionSpec as P

HEADS = 16
HEAD = 128
EPSILON = 1e-06
BF = jnp.bfloat16
F32 = jnp.float32
LOG2E = 1.4426950408889634
NEG = -1e30
VMEM_BYTES = 56 << 20


def dot(a, b):
    return jnp.dot(a, b, preferred_element_type=F32)


def dot_nt(a, b):
    return lax.dot_general(a, b, (((1,), (1,)), ((), ())), preferred_element_type=F32)


def dot_tn(a, b):
    return lax.dot_general(a, b, (((0,), (0,)), ((), ())), preferred_element_type=F32)


def shape(dims, dtype):
    return jax.ShapeDtypeStruct(dims, dtype)


COST = 20.0
ORDERED = []


def call(kernel, out_shape, grid, in_specs, out_specs, cost, scratch=(), alias=None):
    many = isinstance(out_shape, tuple)
    plain = len(in_specs) + 1
    token = [pl.BlockSpec(memory_space=pl.ANY)] * len(ORDERED)

    def ordered_kernel(*refs):
        kernel(*refs[:plain], *refs[plain + len(token) :])

    made = pl.pallas_call(
        ordered_kernel,
        out_shape=out_shape,
        grid_spec=pltpu.PrefetchScalarGridSpec(
            num_scalar_prefetch=1,
            grid=grid,
            in_specs=list(in_specs) + token,
            out_specs=out_specs,
            scratch_shapes=list(scratch),
        ),
        input_output_aliases=alias or {},
        compiler_params=pltpu.CompilerParams(
            dimension_semantics=("arbitrary",) * len(grid), vmem_limit_bytes=VMEM_BYTES
        ),
        cost_estimate=pl.CostEstimate(
            flops=int(COST * cost[0]), bytes_accessed=int(COST * cost[1]), transcendentals=0
        ),
    )

    def run(*operands):
        out = made(*operands, *ORDERED)
        ORDERED[:] = [out[-1] if many else out]
        return out

    return run


def require(*arrays):
    ORDERED.extend(arrays)


def hold(sc, *arrays):
    n = len(arrays)

    def kernel(*refs):
        del refs

    one = pl.BlockSpec(memory_space=pl.ANY)
    found = call(
        kernel,
        tuple(shape(x.shape, x.dtype) for x in arrays),
        (1,),
        [one] * n,
        [one] * n,
        (1e6, 1e4),
        alias={1 + i: i for i in range(n)},
    )(sc, *arrays)
    ORDERED.clear()
    ORDERED.append(found[0])
    return found


def hold_pairs(sc, pairs):
    found = hold(sc, *[x for pair in pairs for x in pair])
    return [tuple(found[2 * i : 2 * i + 2]) for i in range(len(pairs))]


class Halves:
    def __init__(self, low, high, first):
        self.low, self.high, self.first = low, high, first

    def __getitem__(self, at):
        return jnp.where(self.first, self.low[at], self.high[at])

    def __setitem__(self, at, value):
        @pl.when(self.first)
        def _():
            self.low[at] = value

        @pl.when(jnp.logical_not(self.first))
        def _():
            self.high[at] = value


def rows_call(kernel, outs, sc, rows, shared, sums=0):
    first = rows[0]
    R, D = (2 * first[0].shape[0], first[0].shape[1]) if isinstance(first, tuple) else first.shape
    n = min(64, R // 2)
    half = R // 2 // n
    block = pl.BlockSpec((n, D), lambda i, s: (i, 0))
    low = pl.BlockSpec((n, D), lambda i, s: (jnp.minimum(i, half - 1), 0))
    high = pl.BlockSpec((n, D), lambda i, s: (jnp.maximum(i - half, 0), 0))
    one = pl.BlockSpec((1, D), lambda i, s: (0, 0))
    in_specs, operands, kinds = [], [], []
    for x in rows:
        pair = isinstance(x, tuple)
        kinds.append(pair)
        in_specs += [low, high] if pair else [block]
        operands += list(x) if pair else [x]
    kinds += [False] * len(shared)
    out_specs, out_shapes = [], []
    for x in outs:
        pair = isinstance(x, list)
        kinds.append(pair)
        out_specs += [low, high] if pair else [block]
        out_shapes += [shape((R // 2, D), x[0])] * 2 if pair else [shape((R, D), x)]
    kinds += [False] * sums

    def body_kernel(s, *refs):
        i = pl.program_id(0)

        @pl.when(i == 0)
        def _():
            for ref in refs[len(refs) - sums :] if sums else ():
                ref[...] = jnp.zeros_like(ref)

        views, at = [], 0
        for pair in kinds:
            views.append(Halves(refs[at], refs[at + 1], i < half) if pair else refs[at])
            at += 2 if pair else 1
        kernel(*views)

    found = call(
        body_kernel,
        tuple(out_shapes + [shape((1, D), F32)] * sums),
        (R // n,),
        in_specs + [one] * len(shared),
        out_specs + [one] * sums,
        (10 * R * D, 20 * R * D),
    )(sc, *operands, *shared)
    result, at = [], 0
    for x in outs:
        pair = isinstance(x, list)
        result.append(tuple(found[at : at + 2]) if pair else found[at])
        at += 2 if pair else 1
    return result + list(found[at:])


def add_rows(sc, terms, split):
    def kernel(*refs):
        refs[-1][...] = sum(ref[...].astype(F32) for ref in refs[:-1]).astype(BF)

    return rows_call(kernel, [[BF] if split else BF], sc, terms, [])[0]


def unit_rows(values):
    inverse = lax.rsqrt(jnp.mean(values * values, axis=-1, keepdims=True) + EPSILON)
    return values * inverse, inverse


def norm_call(sc, terms, gain):
    def kernel(*refs):
        gain_ref, sum_ref, out_ref = refs[-3:]
        total = sum(ref[...].astype(F32) for ref in refs[:-3])
        sum_ref[...] = total
        out_ref[...] = (unit_rows(total)[0] * gain_ref[...]).astype(BF)

    return rows_call(kernel, [F32, [BF]], sc, terms, [gain])


def norm_back_call(sc, base, values, terms, gain, low):
    def kernel(base_ref, values_ref, *refs):
        term_refs, gain_ref, outs = refs[: len(terms)], refs[len(terms)], refs[len(terms) + 1 :]
        grad = sum(ref[...].astype(F32) for ref in term_refs)
        unit, inverse = unit_rows(values_ref[...].astype(F32))
        if low:
            outs[-1][...] += jnp.sum(grad * unit, axis=0, keepdims=True)
        scaled = grad * gain_ref[...]
        out = base_ref[...].astype(F32) + inverse * (
            scaled - unit * jnp.mean(scaled * unit, axis=-1, keepdims=True)
        )
        outs[0][...] = out
        if low:
            outs[1][...] = out.astype(BF)

    return rows_call(kernel, [F32, [BF]] if low else [F32], sc, [base, values, *terms], [gain], sums=1 if low else 0)


def pair_call(sc, parts):
    half, C, _ = parts[0][0].shape
    widths = [near.shape[2] for _, near in parts]
    N = sum(widths)

    def kernel(s, *refs):
        at = 0
        for p, width in enumerate(widths):
            total = refs[2 * p][0].astype(F32) + refs[2 * p + 1][0].astype(F32)
            refs[-1][:, at : at + width] = total.astype(BF)
            at += width

    return call(
        kernel,
        shape((half * C, N), BF),
        (half,),
        [pl.BlockSpec((1, C, width), lambda i, s: (i, 0, 0)) for width in widths for _ in range(2)],
        pl.BlockSpec((C, N), lambda i, s: (i, 0)),
        (half * C * N, 6 * half * C * N),
    )(sc, *[x for part in parts for x in part])


def stage(refs, x_ref):
    @pl.when(pl.program_id(0) == 0)
    def _():
        at = 0
        for ref in refs:
            x_ref[at : at + ref.shape[0]] = ref[...]
            at += ref.shape[0]


def staged(block):
    H, D = block[0].shape
    return [pl.BlockSpec((H, D), lambda c, s: (0, 0), pipeline_mode=pl.Buffered(1))] * 4, pltpu.VMEM((4 * H, D), BF)


def put_rows(refs, value):
    at = 0
    for ref in refs:
        ref[...] = value[at : at + ref.shape[0]].astype(BF)
        at += ref.shape[0]


def whole(dims):
    return pl.BlockSpec(dims, lambda *_: (0,) * len(dims), pipeline_mode=pl.Buffered(1))


def exp_low(values):
    return jnp.exp(jnp.minimum(values, 0.0))


def phi_of(values, low):
    return jnp.where(values > 0, values + 1.0, low)


def row_ids(count, begin):
    return begin + lax.broadcasted_iota(jnp.int32, (count, 1), 0)


CHIP, CORE, PLACE, VALID, ORDER = 0, 1, 2, 3, 4


def chip_block(s, j, chips):
    return lax.rem(s[CHIP] + j, chips)


def qkv_call(sc, j, chips, block, wq, wk, wv, prev):
    R, D = 2 * block[0].shape[0], block[0].shape[1]
    E = wq.shape[1]
    T = 2 * R * chips
    n = min(256, E)

    def kernel(s, *refs):
        wq_ref, wk_ref, wv_ref = refs[4:7]
        q_ref, k_ref, v_ref, c_ref, x_ref = refs[-5:]
        stage(refs[:4], x_ref)
        base = chip_block(s, j, chips) * 2 * R
        sums = jnp.zeros((1, n), F32)
        x = x_ref[...]
        q, k, v = (dot(x, ref[...]).astype(BF) for ref in (wq_ref, wk_ref, wv_ref))
        for i in range(2):
            off = pl.multiple_of((s[CORE] if i == 0 else 1 - s[CORE]) * R, R)
            rows, part = pl.ds(off, R), slice(i * R, (i + 1) * R)
            q_ref[rows] = q[part]
            k_ref[rows] = k[part]
            v_ref[rows] = v[part]
            keys = k[part].astype(F32)
            phi = jnp.where(row_ids(R, base + off) < s[VALID], phi_of(keys, exp_low(keys)), 0.0)
            sums = sums + jnp.sum(phi, axis=0, keepdims=True)
        c_ref[...] = sums

    rows, scratch = staged(block)
    cols = pl.BlockSpec((D, n), lambda c, s: (0, c))
    out = pl.BlockSpec((2 * R, n), lambda c, s: (chip_block(s, j, chips), c))
    o = shape((T, E), BF)
    extra = [pl.BlockSpec(memory_space=pl.ANY)] * 3 if prev else []
    return call(
        kernel,
        (o, o, o, shape((1, E), F32)),
        (E // n,),
        rows + [cols, cols, cols] + extra,
        [out, out, out, pl.BlockSpec((1, n), lambda c, s: (0, c))],
        (12 * R * D * E, 4 * R * D + 6 * D * E + 12 * R * E),
        scratch=[scratch],
        alias={8: 0, 9: 1, 10: 2} if prev else None,
    )(sc, *block, wq, wk, wv, *(prev or ()))


def grad_inner_call(sc, block, wd):
    R, D = 2 * block[0].shape[0], block[0].shape[1]
    F = wd.shape[0]
    n = min(512, F)

    def kernel(s, *refs):
        w_ref, o_ref, x_ref = refs[4:]
        stage(refs[:4], x_ref)
        o_ref[...] = dot_nt(x_ref[...], w_ref[...]).astype(BF)

    rows, scratch = staged(block)
    return call(
        kernel,
        shape((2 * R, F), BF),
        (F // n,),
        rows + [pl.BlockSpec((n, D), lambda c, s: (c, 0))],
        pl.BlockSpec((2 * R, n), lambda c, s: (0, c)),
        (4 * R * D * F, 4 * R * D + 2 * D * F + 4 * R * F),
        scratch=[scratch],
    )(sc, *block, wd)


def ffn_a_call(sc, block, wg, wu, gi):
    R, D = 2 * block[0].shape[0], block[0].shape[1]
    F = wg.shape[1]
    n = min(512, F)

    def kernel(s, *refs):
        wg_ref, wu_ref, gi_ref, inner_ref, gg_ref, gu_ref, x_ref = refs[4:]
        stage(refs[:4], x_ref)
        for i in range(2):
            rows = slice(i * R, (i + 1) * R)
            g = dot(x_ref[rows], wg_ref[...])
            u = dot(x_ref[rows], wu_ref[...])
            sig = 0.5 * jnp.tanh(0.5 * g) + 0.5
            silu = g * sig
            inner_ref[rows] = (silu * u).astype(BF)
            gi_rows = gi_ref[rows].astype(F32)
            gu_ref[rows] = (gi_rows * silu).astype(BF)
            gg_ref[rows] = (gi_rows * u * (sig + silu * (1.0 - sig))).astype(BF)

    o = shape((2 * R, F), BF)
    rows, scratch = staged(block)
    cols = pl.BlockSpec((D, n), lambda c, s: (0, c))
    out = pl.BlockSpec((2 * R, n), lambda c, s: (0, c))
    return call(
        kernel,
        (o, o, o),
        (F // n,),
        rows + [cols, cols, out],
        [out, out, out],
        (8 * R * D * F, 4 * R * D + 4 * D * F + 16 * R * F),
        scratch=[scratch],
    )(sc, *block, wg, wu, gi)


def halves_out(R, D, n):
    H = R // 2
    return (shape((H, D), BF),) * 4, [pl.BlockSpec((H, n), lambda c, s: (0, c))] * 4


def ffn_b_call(sc, gg, gu, wg, wu):
    R2, F = gg.shape
    R = R2 // 2
    D = wg.shape[0]
    n = min(512, D)

    def kernel(s, gg_ref, gu_ref, wg_ref, wu_ref, *outs):
        put_rows(outs, dot_nt(gg_ref[...], wg_ref[...]) + dot_nt(gu_ref[...], wu_ref[...]))

    rows = pl.BlockSpec((R2, F), lambda c, s: (0, 0))
    cols = pl.BlockSpec((n, F), lambda c, s: (c, 0))
    shapes, specs = halves_out(R, D, n)
    return call(
        kernel,
        shapes,
        (D // n,),
        [rows, rows, cols, cols],
        specs,
        (8 * R * D * F, 8 * R * F + 4 * D * F + 4 * R * D),
    )(sc, gg, gu, wg, wu)


def down_call(sc, inner, wd):
    R2, F = inner.shape
    R = R2 // 2
    D = wd.shape[1]
    n = min(512, D)

    def kernel(s, x_ref, w_ref, *outs):
        put_rows(outs, dot(x_ref[...], w_ref[...]))

    shapes, specs = halves_out(R, D, n)
    return call(
        kernel,
        shapes,
        (D // n,),
        [pl.BlockSpec((R2, F), lambda c, s: (0, 0)), pl.BlockSpec((F, n), lambda c, s: (0, c))],
        specs,
        (4 * R * D * F, 4 * R * F + 2 * D * F + 4 * R * D),
    )(sc, inner, wd)


def wgrad_call(sc, blocks, gs, ndp, pieces):
    xs = [x for block in blocks for x in block]
    H, D = xs[0].shape
    nx = len(xs)
    C = D // ndp
    nb = len(gs[0])
    widths = [parts[0].shape[1] for parts in gs]
    T = H * nx
    rb = T // nb
    N = sum(widths)
    flat = [g for parts in gs for g in parts]
    far = ndp // 2 if pieces else 0
    sizes = [far // max(pieces, 1)] * pieces + [ndp - far]
    begins = [p * sizes[0] for p in range(len(sizes))]

    def kernel(s, *refs):
        x_refs, g_refs, o_refs, xt = refs[:nx], refs[nx : nx + len(flat)], refs[nx + len(flat) : -1], refs[-1]
        j = pl.program_id(0)
        for p in range(nx):
            xt[:, p * H : (p + 1) * H] = x_refs[p][...].T
        at = 0
        for w, width in enumerate(widths):
            acc = None
            for b in range(nb):
                term = dot(xt[:, b * rb : (b + 1) * rb], g_refs[w * nb + b][...])
                acc = term if acc is None else acc + term
            cols = slice(at, at + width)
            at += width
            low = acc.astype(BF)
            for o_ref, begin, size in zip(o_refs, begins, sizes):

                @pl.when((j >= begin) & (j < begin + size))
                def _():
                    o_ref[0, :, cols] = low

    def spec(begin, size):
        return pl.BlockSpec((1, C, N), lambda j, s: (jnp.clip(j - begin, 0, size - 1), 0, 0))

    order = (lambda j, s: (0, s[ORDER + j])) if pieces else (lambda j, s: (0, j))
    return call(
        kernel,
        tuple(shape((size, C, N), BF) for size in sizes),
        (ndp,),
        [pl.BlockSpec((H, C), order)] * nx + [whole(g.shape) for g in flat],
        [spec(begin, size) for begin, size in zip(begins, sizes)],
        (2 * T * D * N, 2 * T * (D + N) + 2 * D * N),
        scratch=[pltpu.VMEM((C, T), BF)],
    )(sc, *xs, *flat)


def attn_fwd_call(sc, q, k, v, h0, hh):
    T = q.shape[0]
    E = hh * HEAD
    B = min(512, T)
    nb = T // B
    c = HEAD**-0.5 * LOG2E

    def kernel(s, q_ref, k_ref, v_ref, o_ref, lse_ref):
        valid = s[VALID]
        for i in range(nb):
            qb = q_ref[i * B : (i + 1) * B]
            parts = []
            for j in range(i + 1):
                x = dot_nt(k_ref[j * B : (j + 1) * B], qb)
                if j == i:
                    u = lax.broadcasted_iota(jnp.int32, (B, B), 0)
                    t = lax.broadcasted_iota(jnp.int32, (B, B), 1)
                    x = jnp.where(u <= t, x, NEG)
                if (j + 1) * B > T // 2:
                    x = jnp.where(row_ids(B, j * B) < valid, x, NEG)
                parts.append(x)
            top = jnp.max(parts[0], axis=0, keepdims=True)
            for x in parts[1:]:
                top = jnp.maximum(top, jnp.max(x, axis=0, keepdims=True))
            top = top * c
            total = jnp.zeros((1, B), F32)
            acc = jnp.zeros((HEAD, B), F32)
            for j, x in enumerate(parts):
                p = jnp.exp2(x * c - top)
                total = total + jnp.sum(p, axis=0, keepdims=True)
                acc = acc + dot_tn(v_ref[j * B : (j + 1) * B], p.astype(BF))
            o_ref[i * B : (i + 1) * B] = (acc * (1.0 / total)).T
            lse_ref[0, :, i * B : (i + 1) * B] = top + jnp.log2(total)

    head = pl.BlockSpec((T, HEAD), lambda h, s: (0, h0 + h))
    out = pl.BlockSpec((T, HEAD), lambda h, s: (0, h))
    return call(
        kernel,
        (shape((T, E), F32), shape((hh, 1, T), F32)),
        (hh,),
        [head, head, head],
        [out, pl.BlockSpec((1, 1, T), lambda h, s: (h, 0, 0))],
        (6 * T * T * E, 10 * T * E),
    )(sc, q, k, v)


def attn_bwd_call(sc, q, k, v, do, attended, h0, part):
    lo, lse = attended
    nh = 1
    T = q.shape[0]
    B = min(512, T)
    nb = T // B
    scale = HEAD**-0.5
    c = scale * LOG2E

    def kernel(s, q_ref, k_ref, v_ref, do_ref, lo_ref, lse_ref, dq_ref, dk_ref, dv_ref, delta):
        valid = s[VALID]
        ones = jnp.ones((8, HEAD), F32)
        for i in range(nb):
            rows = slice(i * B, (i + 1) * B)
            prod = do_ref[rows].astype(F32) * lo_ref[rows]
            delta[:, rows] = lax.dot_general(
                ones,
                prod,
                (((1,), (1,)), ((), ())),
                precision=lax.Precision.HIGHEST,
                preferred_element_type=F32,
            )
        dq_ref[...] = jnp.zeros_like(dq_ref)
        for j in range(nb):
            kb = k_ref[j * B : (j + 1) * B]
            vb = v_ref[j * B : (j + 1) * B]
            dk = jnp.zeros((B, HEAD), F32)
            dv = jnp.zeros((B, HEAD), F32)
            for i in range(j, nb):
                rows = slice(i * B, (i + 1) * B)
                qb = q_ref[rows]
                dob = do_ref[rows]
                p = jnp.exp2(dot_nt(kb, qb) * c - lse_ref[0, :, rows])
                if i == j:
                    u = lax.broadcasted_iota(jnp.int32, (B, B), 0)
                    t = lax.broadcasted_iota(jnp.int32, (B, B), 1)
                    p = jnp.where(u <= t, p, 0.0)
                if (j + 1) * B > T // 2:
                    p = jnp.where(row_ids(B, j * B) < valid, p, 0.0)
                ds = (p * (dot_nt(vb, dob) - delta[0:1, rows])).astype(BF)
                dv = dv + dot(p.astype(BF), dob)
                dk = dk + dot(ds, qb)
                dq_ref[rows] += dot_tn(ds, kb)
            dk_ref[j * B : (j + 1) * B] = dk * scale
            dv_ref[j * B : (j + 1) * B] = dv
        dq_ref[...] *= scale

    o = shape((T, nh * HEAD), F32)
    head = pl.BlockSpec((T, HEAD), lambda h, s: (0, h0 + h))
    out = pl.BlockSpec((T, HEAD), lambda h, s: (0, h))
    return call(
        kernel,
        (o, o, o),
        (nh,),
        [head] * 4
        + [pl.BlockSpec((T, HEAD), lambda h, s: (0, part)), pl.BlockSpec((1, 1, T), lambda h, s: (part, 0, 0))],
        [out, out, out],
        (12 * T * T * HEAD * nh, 26 * T * HEAD * nh),
        scratch=[pltpu.VMEM((8, T), F32)],
    )(sc, q, k, v, do, lo, lse)


def maps_call(sc, k, v, gathered):
    T, E = k.shape
    hh = E // HEAD
    ndp = gathered.shape[0]

    def kernel(s, k_ref, v_ref, g_ref, maps_ref, norm_ref):
        h = pl.program_id(0)
        norm = jnp.zeros((1, HEAD), F32)
        for a in range(ndp - 1):
            after = (norm + g_ref[shared_at(s, a, ndp), pl.ds(h, 1)]) * g_ref[shared_at(s, a + 1, ndp), hh : hh + 1]
            norm = jnp.where(a < s[PLACE], after, norm)
        norm_ref[0] = norm
        k = k_ref[...].astype(F32)
        phi = jnp.where(row_ids(T, 0) < s[VALID], phi_of(k, exp_low(k)), 0.0)
        den = jnp.maximum(jnp.sum(phi * norm, axis=1, keepdims=True), 1.0)
        low = phi.astype(BF)
        maps_ref[0, 0] = dot_tn((phi * (1.0 / den)).astype(BF), low).astype(BF)
        maps_ref[1, 0] = dot_tn(low, v_ref[...]).astype(BF)

    head = pl.BlockSpec((T, HEAD), lambda h, s: (0, h))
    return call(
        kernel,
        (shape((2, hh, HEAD, HEAD), BF), shape((hh, 1, HEAD), F32)),
        (hh,),
        [head, head, whole(gathered.shape)],
        [
            pl.BlockSpec((2, 1, HEAD, HEAD), lambda h, s: (0, h, 0, 0)),
            pl.BlockSpec((1, 1, HEAD), lambda h, s: (h, 0, 0)),
        ],
        (4 * T * E * HEAD, 4 * T * E),
    )(sc, k, v, gathered)


def times_state(g, state):
    high = state.astype(BF)
    return dot(g, high) + dot(g, (state - high.astype(F32)).astype(BF))


def chain_call(sc, gathered, maps):
    ndp, _, hh = maps.shape[:3]

    def kernel(s, g_ref, maps_ref, m_ref):
        state = [jnp.zeros((HEAD, HEAD), F32) for _ in range(hh)]
        for a in range(ndp - 1):
            keep = g_ref[shared_at(s, a + 1, ndp), hh : hh + 1]
            before = a < s[PLACE]
            for h in range(hh):
                after = state[h] - times_state(maps_ref[a, 0, h], state[h])
                after = (after + maps_ref[a, 1, h].astype(F32)) * keep
                state[h] = jnp.where(before, after, state[h])
        for h in range(hh):
            m_ref[h] = state[h]

    return call(
        kernel,
        shape((hh, HEAD, HEAD), F32),
        (1,),
        [whole(gathered.shape), whole(maps.shape)],
        whole((hh, HEAD, HEAD)),
        (4e8, 2 * maps.size),
    )(sc, gathered, maps)


def mixout_call(sc, j, chips, q, locals_, memory, norm, mix, wo):
    T, E = q.shape
    hh = E // HEAD
    D = wo.shape[1]
    R = T // chips // 2
    n = min(512, D)
    groups = len(locals_)
    per = hh // groups

    def kernel(s, q_ref, *rest):
        l_refs = rest[:groups]
        m_ref, n_ref, mix_ref, w_ref, *outs, mixed_ref, diff_ref = rest[groups:]

        @pl.when(pl.program_id(0) == 0)
        def _():
            for i in range(2):
                off = pl.multiple_of((s[CORE] if i == 0 else 1 - s[CORE]) * R, R)
                for h in range(hh):
                    cols = slice(h * HEAD, (h + 1) * HEAD)
                    qv = q_ref[pl.ds(off, R), cols].astype(F32)
                    phi = phi_of(qv, exp_low(qv))
                    den = jnp.maximum(jnp.sum(phi * n_ref[h], axis=1, keepdims=True), 1.0)
                    read = dot(phi.astype(BF), m_ref[h].astype(BF)) * (1.0 / den)
                    local = l_refs[h // per][pl.ds(off, R), h % per * HEAD : (h % per + 1) * HEAD]
                    diff = read - local
                    mixed = local + mix_ref[h] * diff
                    diff_ref[i * R : (i + 1) * R, cols] = diff.astype(BF)
                    mixed_ref[i * R : (i + 1) * R, cols] = mixed.astype(BF)

        put_rows(outs, dot(mixed_ref[...], w_ref[...]))

    rows = pl.BlockSpec((2 * R, E), lambda c, s: (chip_block(s, j, chips), 0))
    shapes, specs = halves_out(R, D, n)
    rel = pl.BlockSpec((2 * R, E), lambda c, s: (0, 0))
    return call(
        kernel,
        shapes + (shape((2 * R, E), BF), shape((2 * R, E), BF)),
        (D // n,),
        [rows]
        + [pl.BlockSpec((2 * R, per * HEAD), lambda c, s: (chip_block(s, j, chips), 0))] * groups
        + [whole(memory.shape), whole(norm.shape), whole(mix.shape), pl.BlockSpec((E, n), lambda c, s: (0, c))],
        specs + [rel, rel],
        (4 * R * E * D + 8 * R * E * HEAD, 20 * R * E + 2 * E * D + 4 * R * D),
    )(sc, q, *locals_, memory, norm, mix, wo)


def gradmix_call(sc, j, chips, block, wo, diff, q, norm, mix, prev):
    R, D = 2 * block[0].shape[0], block[0].shape[1]
    E = wo.shape[0]
    hh = E // HEAD
    T = 2 * R * chips
    n = min(256, E)
    per = n // HEAD

    def kernel(s, *refs):
        w_ref, diff_ref, q_ref, n_ref, mix_ref = refs[4:9]
        do_ref, gm_ref, cot_ref, b_ref, x_ref = refs[-5:]
        stage(refs[:4], x_ref)
        sums = jnp.zeros((1, n), F32)
        cots = [jnp.zeros((HEAD, HEAD), F32) for _ in range(per)]
        for i in range(2):
            off = pl.multiple_of((s[CORE] if i == 0 else 1 - s[CORE]) * R, R)
            grad = dot_nt(x_ref[i * R : (i + 1) * R], w_ref[...])
            sums = sums + jnp.sum(grad * diff_ref[i * R : (i + 1) * R].astype(F32), axis=0, keepdims=True)
            for h in range(per):
                cols = slice(h * HEAD, (h + 1) * HEAD)
                part = grad[:, cols]
                grad_read = part * mix_ref[h]
                do_ref[pl.ds(off, R), cols] = (part - grad_read).astype(BF)
                gm_ref[pl.ds(off, R), cols] = grad_read.astype(BF)
                qv = q_ref[pl.ds(off, R), cols].astype(F32)
                phi = phi_of(qv, exp_low(qv))
                den = jnp.maximum(jnp.sum(phi * n_ref[h], axis=1, keepdims=True), 1.0)
                cots[h] = cots[h] + dot_tn(phi.astype(BF), (grad_read * (1.0 / den)).astype(BF))
        for h in range(per):
            cot_ref[h] = cots[h]
        b_ref[...] = sums

    rows, scratch = staged(block)
    place = pl.BlockSpec((2 * R, n), lambda c, s: (chip_block(s, j, chips), c))
    per_head = pl.BlockSpec((per, 1, HEAD), lambda c, s: (c, 0, 0))
    o = shape((T, E), BF)
    extra = [pl.BlockSpec(memory_space=pl.ANY)] * 2 if prev else []
    return call(
        kernel,
        (o, o, shape((hh, HEAD, HEAD), F32), shape((1, E), F32)),
        (E // n,),
        rows
        + [pl.BlockSpec((n, D), lambda c, s: (c, 0)), pl.BlockSpec((2 * R, n), lambda c, s: (0, c)), place, per_head, per_head]
        + extra,
        [place, place, pl.BlockSpec((per, HEAD, HEAD), lambda c, s: (c, 0, 0)), pl.BlockSpec((1, n), lambda c, s: (0, c))],
        (4 * R * E * D + 4 * R * E * HEAD, 4 * R * D + 2 * E * D + 16 * R * E),
        scratch=[scratch],
        alias={10: 0, 11: 1} if prev else None,
    )(sc, *block, wo, diff, q, norm, mix, *(prev or ()))


def memory_rows(q, k, grad_read, live, memory, norm, cot):
    low_q = exp_low(q)
    low_k = exp_low(k)
    phi_q = phi_of(q, low_q)
    phi_k = jnp.where(live, phi_of(k, low_k), 0.0)
    raw_q = jnp.sum(phi_q * norm, axis=1, keepdims=True)
    raw_k = jnp.sum(phi_k * norm, axis=1, keepdims=True)
    inv_q = 1.0 / jnp.maximum(raw_q, 1.0)
    inv_k = 1.0 / jnp.maximum(raw_k, 1.0)
    read = dot(phi_q.astype(BF), memory)
    recalled = dot(phi_k.astype(BF), memory) * inv_k
    pushed = dot(phi_k.astype(BF), cot)
    scaled = grad_read * inv_q
    w_q = jnp.where(raw_q > 1.0, -jnp.sum(scaled * read, axis=1, keepdims=True) * inv_q, 0.0)
    w_k = jnp.where(raw_k > 1.0, jnp.sum(pushed * recalled, axis=1, keepdims=True) * inv_k, 0.0)
    return low_q, low_k, phi_q, phi_k, inv_k, recalled, pushed, scaled, w_q, w_k


def memory_cot_call(sc, gathered, maps, cots, q, k, grad_read, memory, norm):
    T, E = q.shape
    hh = E // HEAD
    ndp = maps.shape[0]
    B = min(512, T)

    def kernel(s, g_ref, maps_ref, cots_ref, q_ref, k_ref, gm_ref, m_ref, n_ref, x_ref, nb_ref):
        cot = jnp.zeros((HEAD, HEAD), F32)
        for a in range(ndp - 1, 0, -1):
            before = cot - times_state(maps_ref[a, 0, 0], cot) + cots_ref[shared_at(s, a, ndp), 0].astype(F32)
            cot = jnp.where(a > s[PLACE], before * g_ref[shared_at(s, a, ndp), hh : hh + 1], cot)
        x_ref[0] = cot
        cot = cot.astype(BF)
        memory = m_ref[0].astype(BF)
        sums = jnp.zeros((1, HEAD), F32)
        for i in range(T // B):
            rows = slice(i * B, (i + 1) * B)
            live = row_ids(B, i * B) < s[VALID]
            terms = memory_rows(
                q_ref[rows].astype(F32), k_ref[rows].astype(F32), gm_ref[rows].astype(F32), live, memory, n_ref[0], cot
            )
            sums = sums + jnp.sum(terms[2] * terms[8] + terms[3] * terms[9], axis=0, keepdims=True)
        nb_ref[0] = sums

    head = pl.BlockSpec((T, HEAD), lambda h, s: (0, h))
    square = pl.BlockSpec((1, HEAD, HEAD), lambda h, s: (h, 0, 0))
    row = pl.BlockSpec((1, 1, HEAD), lambda h, s: (h, 0, 0))
    return call(
        kernel,
        (shape((hh, HEAD, HEAD), F32), shape((hh, 1, HEAD), F32)),
        (hh,),
        [
            whole(gathered.shape),
            pl.BlockSpec((ndp, 1, 1, HEAD, HEAD), lambda h, s: (0, 0, h, 0, 0)),
            pl.BlockSpec((ndp, 1, HEAD, HEAD), lambda h, s: (0, h, 0, 0)),
            head,
            head,
            head,
            square,
            row,
        ],
        [square, row],
        (8 * T * E * HEAD, 6 * T * E),
    )(sc, gathered, maps, cots, q, k, grad_read, memory, norm)


def combine_call(sc, chips, q, k, v, grad_read, local_grads, memory, norm, cot, gathered, norm_parts):
    T, E = q.shape
    hh = E // HEAD
    R = T // chips // 2
    ndp = gathered.shape[0]
    per = local_grads[0][0].shape[1] // HEAD
    groups = len(local_grads)

    def kernel(s, q_ref, k_ref, v_ref, gm_ref, *rest):
        local_refs = rest[: 3 * groups]
        m_ref, n_ref, x_ref, g_ref, nb_ref, gq_ref, gk_ref, gv_ref = rest[3 * groups :]
        begin = piece(pl.program_id(0), s) * R
        live = row_ids(R, begin) < s[VALID]
        for h in range(hh):
            cols = slice(h * HEAD, (h + 1) * HEAD)
            part = slice(h % per * HEAD, (h % per + 1) * HEAD)
            dq, dk, dv = (ref[:, part] for ref in local_refs[3 * (h // per) : 3 * (h // per) + 3])
            norm_cot = jnp.zeros((1, HEAD), F32)
            for a in range(ndp - 1, 0, -1):
                other = shared_at(s, a, ndp)
                before = (norm_cot + nb_ref[other, h : h + 1]) * g_ref[other, hh : hh + 1]
                norm_cot = jnp.where(a > s[PLACE], before, norm_cot)
            memory = m_ref[h].astype(BF)
            cot = x_ref[h].astype(BF)
            norm = n_ref[h]
            low_q, low_k, _, _, inv_k, recalled, pushed, scaled, w_q, w_k = memory_rows(
                q_ref[:, cols].astype(F32), k_ref[:, cols].astype(F32), gm_ref[:, cols].astype(F32), live, memory, norm, cot
            )
            grad_phi_q = dot_nt(scaled.astype(BF), memory) + w_q * norm
            grad_phi_k = (
                dot_nt((v_ref[:, cols].astype(F32) - recalled).astype(BF), cot)
                - dot_nt((pushed * inv_k).astype(BF), memory)
                + w_k * norm
                + norm_cot
            )
            gq_ref[:, cols] = (dq + grad_phi_q * low_q).astype(BF)
            gk_ref[:, cols] = (dk + jnp.where(live, grad_phi_k * low_k, 0.0)).astype(BF)
            gv_ref[:, cols] = (dv + pushed).astype(BF)

    def piece(p, s):
        core = lax.rem(s[CORE] + p, 2)
        return chip_block(s, p // 2, chips) * 2 + core

    rows = pl.BlockSpec((R, E), lambda p, s: (piece(p, s), 0))
    part_rows = pl.BlockSpec((R, per * HEAD), lambda p, s: (piece(p, s), 0))
    out = pl.BlockSpec((R, E), lambda p, s: (p, 0))
    o = shape((T, E), BF)
    return call(
        kernel,
        (o, o, o),
        (2 * chips,),
        [rows] * 4 + [part_rows] * (3 * groups) + [whole(x.shape) for x in (memory, norm, cot, gathered, norm_parts)],
        [out, out, out],
        (14 * T * E * HEAD, 26 * T * E),
    )(sc, q, k, v, grad_read, *[x for group in local_grads for x in group], memory, norm, cot, gathered, norm_parts)


def grad_normed_call(sc, j, gq, gk, gv, wq, wk, wv, block, chips):
    T, E = gq.shape
    R = T // chips // 2
    D = wq.shape[0]
    n = min(512, D)

    def kernel(s, gq_ref, gk_ref, gv_ref, wq_ref, wk_ref, wv_ref, *rest):
        grad = dot_nt(gq_ref[...], wq_ref[...]) + dot_nt(gk_ref[...], wk_ref[...]) + dot_nt(gv_ref[...], wv_ref[...])
        put_rows(rest[4:8], grad)
        sums, at = 0.0, 0
        for ref in rest[:4]:
            part = grad[at : at + ref.shape[0]] * ref[...].astype(F32)
            sums = sums + jnp.sum(part, axis=0, keepdims=True)
            at += ref.shape[0]
        rest[8][...] = sums

    rows = pl.BlockSpec((2 * R, E), lambda c, s: (j, 0))
    cols = pl.BlockSpec((n, E), lambda c, s: (c, 0))
    shapes, specs = halves_out(R, D, n)
    return call(
        kernel,
        shapes + (shape((1, D), F32),),
        (D // n,),
        [rows, rows, rows, cols, cols, cols] + specs,
        specs + [pl.BlockSpec((1, n), lambda c, s: (0, c))],
        (12 * R * D * E, 12 * R * E + 6 * D * E + 4 * R * D),
    )(sc, gq, gk, gv, wq, wk, wv, *block)


def swap_core(pair):
    count = lax.axis_size("tensor")
    return tuple(lax.ppermute(x, "tensor", [(i, i ^ 1) for i in range(count)]) for x in pair)


def shift_chip(pair, j):
    count = lax.axis_size("tensor")
    return tuple(lax.ppermute(x, "tensor", [(i, (i + 2 * j) % count) for i in range(count)]) for x in pair)


def with_swapped(pair):
    return tuple(pair) + swap_core(pair)


def chunk_order(me, ndp):
    parity = me % 2
    order = [2 * i + (1 - parity) for i in range(ndp // 2)] + [2 * i + parity for i in range(ndp // 2)]
    return jnp.stack(order)


def exchange_x(x):
    return lax.ppermute(x, "dp", [(i, i ^ 1) for i in range(lax.axis_size("dp"))])


def sum_z(x):
    ndp = lax.axis_size("dp")
    groups = [list(range(0, ndp, 2)), list(range(1, ndp, 2))]
    return lax.psum_scatter(x, "dp", scatter_dimension=0, axis_index_groups=groups, tiled=True)


def finish_x(both, parity):
    C = both.shape[0] // 2
    got = exchange_x(lax.dynamic_slice_in_dim(both, (1 - parity) * C, C, 0))
    return got.astype(F32) + lax.dynamic_slice_in_dim(both, parity * C, C, 0).astype(F32)


def share_steps(x):
    count = lax.axis_size("dp")
    steps = [1 << bit for bit in range(1, count.bit_length() - 1)] + [1]
    x = x[None]
    for step in steps:
        x = jnp.concatenate([x, lax.ppermute(x, "dp", [(i, i ^ step) for i in range(count)])])
        yield x


def shared_at(s, a, count):
    apart = a ^ s[PLACE]
    return (apart >> 1) + (apart & 1) * (count // 2)


def share_over_dp(x):
    return list(share_steps(x))[-1]


def sum_everywhere(x):
    for axis in ("tensor", "dp"):
        count, step = lax.axis_size(axis), 1
        while step < count:
            x = x + lax.ppermute(x, axis, [(i, i ^ step) for i in range(count)])
            step *= 2
    return x


def body(
    tokens,
    gain1,
    w_query,
    w_key,
    w_value,
    w_out,
    gate_bias,
    gain2,
    w_gate,
    w_up,
    w_down,
    seg_starts,
    seg_valid,
    cotangent,
):
    count = lax.axis_size("tensor")
    ndp = lax.axis_size("dp")
    chips = count // 2
    hh = gate_bias.shape[0]
    E = hh * HEAD
    here = lax.axis_index("tensor")
    place = lax.axis_index("dp")
    sc = jnp.concatenate(
        [
            jnp.stack([here // 2, here % 2, place]).astype(jnp.int32),
            seg_valid.astype(jnp.int32),
            chunk_order(place, ndp).astype(jnp.int32),
        ]
    )
    keep = (1 - seg_starts[0]).astype(F32)
    sig_bias = jax.nn.sigmoid(gate_bias)
    mix = jnp.broadcast_to(sig_bias[:, None, None], (hh, 1, HEAD))

    ORDERED.clear()
    per = max(1, hh // 2)

    gain1 = gain1[None]
    gain2 = gain2[None]
    chip_range = range(1, chips)
    parity = place % 2
    R = tokens.shape[0]
    four = min(4, ndp // 2)

    def norm1_kernel(x_ref, g_ref, o_ref):
        o_ref[...] = (unit_rows(x_ref[...].astype(F32))[0] * g_ref[...]).astype(BF)

    normed1 = rows_call(norm1_kernel, [[BF]], sc, [tokens], [gain1])[0]
    rows1 = [with_swapped(normed1)]
    far1 = [shift_chip(normed1, -j) for j in chip_range]
    own_cot = (cotangent[: R // 2], cotangent[R // 2 :])
    cot_rows = [with_swapped(own_cot)]
    *qkv, sums = qkv_call(sc, 0, chips, rows1[0], w_query, w_key, w_value, None)
    *far1, own_cot = hold_pairs(sc, far1 + [own_cot])
    far_cot = [shift_chip(own_cot, -j) for j in chip_range]
    for j in chip_range:
        rows1.append(with_swapped(far1[j - 1]))
        *qkv, column_sums = qkv_call(sc, j, chips, rows1[j], w_query, w_key, w_value, qkv)
        sums = sums + column_sums
    q, k, v = qkv

    own = jnp.concatenate([sums.reshape(hh, HEAD), jnp.full((8 - hh, HEAD), keep, F32)])
    gathered = share_over_dp(own)
    maps, norm = maps_call(sc, k, v, gathered)
    all_maps = lax.all_gather(maps, "dp")
    attended = [attn_fwd_call(sc, q, k, v, h, per) for h in range(0, hh, per)]
    far_cot = hold_pairs(sc, far_cot)
    cot_rows += [with_swapped(pair) for pair in far_cot]
    grad_inner = [grad_inner_call(sc, block, w_down) for block in cot_rows]
    memory = chain_call(sc, gathered, all_maps)

    mixed, diff = [None] * chips, [None] * chips

    def mixout(j):
        *block, mixed[j], diff[j] = mixout_call(sc, j, chips, q, [one[0] for one in attended], memory, norm, mix, w_out)
        return block

    def scatter(make):
        blocks = [make(j) for j in chip_range] + [make(0)]
        got = []
        for j in chip_range:
            block = blocks[j - 1]
            sums = add_rows(sc, [tuple(block[:2]), swap_core(block[2:])], True)
            got.append(shift_chip(sums, j))
        block = blocks[-1]
        return [tuple(block[:2]), swap_core(block[2:]), *got]

    hidden, normed2 = norm_call(sc, [tokens, *scatter(mixout)], gain2)
    rows2 = [with_swapped(normed2)]
    far2 = [shift_chip(normed2, -j) for j in chip_range]
    ffn = [ffn_a_call(sc, rows2[0], w_gate, w_up, grad_inner[0])]
    far2 = hold_pairs(sc, far2)
    for j in chip_range:
        rows2.append(with_swapped(far2[j - 1]))
        ffn.append(ffn_a_call(sc, rows2[j], w_gate, w_up, grad_inner[j]))
    inner, grad_gate, grad_up = zip(*ffn)

    (w_up_parts,) = wgrad_call(sc, rows2, [grad_up], ndp, 0)
    both_up = sum_z(w_up_parts.reshape((-1, w_up_parts.shape[2])))
    back = scatter(lambda j: ffn_b_call(sc, grad_gate[j], grad_up[j], w_gate, w_up))
    far_gate, near_gate = wgrad_call(sc, rows2, [grad_gate], ndp, 1)
    far_gate = exchange_x(far_gate)
    far_down, near_down = wgrad_call(sc, cot_rows, [inner], ndp, 1)
    far_down = exchange_x(far_down)
    grad_hidden, grad_low, gain2_part = norm_back_call(sc, cotangent, hidden, back, gain2, True)
    grad_rows = [with_swapped(grad_low)]
    far_grad = [shift_chip(grad_low, -j) for j in chip_range]
    down_far = [down_call(sc, inner[j], w_down) for j in chip_range]
    *grads, cot_part, bias_part = gradmix_call(sc, 0, chips, grad_rows[0], w_out, diff[0], q, norm, mix, None)
    down_near = down_call(sc, inner[0], w_down)
    far_grad = hold_pairs(sc, far_grad)
    pair_gate = pair_call(sc, [(far_gate, near_gate)])
    sum_gate = sum_z(pair_gate)
    require(both_up)
    sum_up = finish_x(both_up, parity)
    for j in chip_range:
        grad_rows.append(with_swapped(far_grad[j - 1]))
        *grads, cot_j, bias_j = gradmix_call(sc, j, chips, grad_rows[j], w_out, diff[j], q, norm, mix, grads)
        cot_part = cot_part + cot_j
        bias_part = bias_part + bias_j
    down_blocks = iter(down_far + [down_near])
    down = scatter(lambda j: next(down_blocks))
    grad_local, grad_read = grads

    local_grads = []
    steps = share_steps(cot_part.astype(BF))
    all_cots = None
    for h in range(hh):
        local_grads.append(attn_bwd_call(sc, q, k, v, grad_local, attended[h // per], h, h % per))
        if h in (0, max(2, hh - 2)):
            all_cots = next(steps)
            require(all_cots)
    for all_cots in steps:
        pass
    pair_down = pair_call(sc, [(far_down, near_down)])
    sum_down = sum_z(pair_down)
    memory_cot, norm_part = memory_cot_call(sc, gathered, all_maps, all_cots, q, k, grad_read, memory, norm)
    steps = share_steps(jnp.concatenate([norm_part.reshape(hh, HEAD), jnp.zeros((8 - hh, HEAD), F32)]))
    require(next(steps))
    far_out, near_out = wgrad_call(sc, grad_rows, [mixed], ndp, 1)
    far_out = exchange_x(far_out)
    for norm_parts in steps:
        pass
    require(sum_gate)
    gq, gk, gv = combine_call(
        sc, chips, q, k, v, grad_read, local_grads, memory, norm, memory_cot, gathered, norm_parts
    )
    gain1_sums = []

    def back_rows(j):
        *block, sums = grad_normed_call(sc, j, gq, gk, gv, w_query, w_key, w_value, rows1[j], chips)
        gain1_sums.append(sums)
        return block

    parts1 = {}

    def make1(name, grad):
        far, near = wgrad_call(sc, rows1, [[grad]], ndp, 1)
        parts1[name] = exchange_x(far), near

    make1("v", gv)
    make1("k", gk)
    output = add_rows(sc, [hidden, *down], False)
    back1 = scatter(back_rows)
    require(sum_down)
    sum_ovk = sum_z(pair_call(sc, [(far_out, near_out), parts1["v"], parts1["k"]]))
    make1("q", gq)
    (grad_tokens,) = norm_back_call(sc, grad_hidden, tokens, back1, gain1, False)
    require(sum_ovk)
    sum_ovk = sum_ovk.astype(F32)
    sum_query = sum_z(pair_call(sc, [parts1["q"]])).astype(F32)
    gain1_part = sum(gain1_sums) / gain1

    bias_here = jnp.sum(bias_part.reshape(hh, HEAD), axis=1) * sig_bias * (1.0 - sig_bias)
    bias_full = lax.dynamic_update_slice(jnp.zeros((HEADS,), F32), bias_here, (here * hh,))
    small = sum_everywhere(jnp.concatenate([gain1_part[0], gain2_part[0], bias_full]))
    D = gain1.shape[1]
    return (
        output,
        grad_tokens,
        small[:D],
        sum_query,
        sum_ovk[:, 2 * E :],
        sum_ovk[:, E : 2 * E],
        sum_ovk[:, :E].T,
        small[2 * D :],
        small[D : 2 * D],
        sum_gate.astype(F32),
        sum_up,
        sum_down.astype(F32).T,
    )


def solution(mesh):
    rows = P(("dp", "tensor"), None)
    return jax.shard_map(
        body,
        mesh=mesh,
        in_specs=(
            rows,
            P(),
            P(None, "tensor"),
            P(None, "tensor"),
            P(None, "tensor"),
            P("tensor", None),
            P("tensor"),
            P(),
            P(None, "tensor"),
            P(None, "tensor"),
            P("tensor", None),
            P("dp"),
            P("dp"),
            rows,
        ),
        out_specs=(
            rows,
            rows,
            P(),
            P("dp", "tensor"),
            P("dp", "tensor"),
            P("dp", "tensor"),
            P("tensor", "dp"),
            P(),
            P(),
            P("dp", "tensor"),
            P("dp", "tensor"),
            P("tensor", "dp"),
        ),
        check_vma=False,
    )
```
